32 devices in a mesh: seq: 8 (over z, y), batch: 4 (over x, core).
Axes of the slice: x: 2, y: 2, z: 4, core: 2. Of those that a mesh axis runs over, the one named last changes fastest.
Arguments:
- tokens: bfloat16 [28, 1152, 768], P('batch', 'seq'), may hold values from -6 to 6
- cotangent: bfloat16 [28, 1152, 768], P('batch', 'seq'), may hold values from -6 to 6
- gain_in: float32 [768], replicated, may hold values from 0.5 to 1.5
- w_mix: bfloat16 [768, 1920], replicated, may hold values from -0.21875 to 0.21875
- lower: float32 [384], replicated, may hold values from 0.5 to 0.96
- fbias: float32 [384], replicated, may hold values from -1 to 11
- phase: float32 [384], replicated, may hold values from -0.5 to 0.5
- gain_out: float32 [768], replicated, may hold values from 0.5 to 1.5
- w_out: bfloat16 [768, 768], replicated, may hold values from -0.4375 to 0.4375
- gain_ffn: float32 [768], replicated, may hold values from 0.5 to 1.5
- w_gu: bfloat16 [768, 3072], replicated, may hold values from -0.21875 to 0.21875
- w_down: bfloat16 [1536, 768], replicated, may hold values from -0.3125 to 0.3125
Outputs:
- output: bfloat16 [28, 1152, 768], P('batch', 'seq')
- grad_tokens: float32 [28, 1152, 768], P('batch', 'seq')
- grad_w_mix: float32 [768, 1920], P('seq')
- grad_w_out: float32 [768, 768], P('seq')
- grad_w_gu: float32 [768, 3072], P('seq')
- grad_w_down: float32 [1536, 768], P('seq')
- grad_gain_in: float32 [768], replicated
- grad_gain_out: float32 [768], replicated
- grad_gain_ffn: float32 [768], replicated
- grad_lower: float32 [384], replicated
- grad_fbias: float32 [384], replicated
- grad_phase: float32 [384], replicated
The draws below stay inside these ranges and needn't reach their ends.
All inputs are finite; a program needn't handle non-finite values.
Results may differ from the reference program's by a relative error of at most 0.0099.
Values sent between devices are 32-bit elements; how exact they have to be, the bound alone decides.
No kernel may reach another device: no remote copies, remote signals or barrier semaphores. Data moves between devices by JAX's collectives and lax.ppermute only.
A program may use at most 192 MiB of HBM per device.

```python
import jax
import jax.numpy as jnp
from jax import lax

D = 768
C = 384
F = 1536
LENGTH = 1152
SEQUENCES = 28


def channel_split(key, slow_count):
    order = jax.random.permutation(jax.random.fold_in(key, 11), C)
    slow = order < slow_count
    drop_slow = jnp.exp(jax.random.uniform(jax.random.fold_in(key, 12), (C,), jnp.float32, jnp.log(0.2), jnp.log(0.5)))
    drop_fast = jnp.exp(jax.random.uniform(jax.random.fold_in(key, 13), (C,), jnp.float32, jnp.log(0.04), jnp.log(0.1)))
    return (slow, jnp.where(slow, drop_slow, drop_fast))


def draw_lower(key, part):
    count = C // 2
    slow, drop = channel_split(key, count)
    return (1.0 - drop).astype(jnp.float32)


def draw_fbias(key, part):
    count = C // 2
    slow, drop = channel_split(key, count)
    own = jax.random.fold_in(key, 5)
    ratio = jnp.exp(jax.random.uniform(jax.random.fold_in(own, 1), (C,), jnp.float32, jnp.log(0.3), jnp.log(1.5)))
    slow_bias = jnp.log(drop * LENGTH / ratio) + 0.5
    fast_bias = jax.random.uniform(jax.random.fold_in(own, 2), (C,), jnp.float32, -1.0, 1.0)
    return jnp.where(slow, slow_bias, fast_bias).astype(jnp.float32)


def block_scale(own_key, dims, shards, least, largest):
    factor_of = 1.0
    for dim, parts in shards:
        heights = jax.random.uniform(jax.random.fold_in(jax.random.fold_in(own_key, 6), dim), (parts,), jnp.float32, least / len(shards), largest / len(shards))
        factor_of = factor_of * jnp.repeat(jnp.exp(heights), dims[dim] // parts).reshape((-1,) + (1,) * (len(dims) - 1 - dim))
    return factor_of


def normal_values(own_key, dims, deviation, limit, split=(), held_as=jnp.bfloat16):
    drawn = jax.random.normal(own_key, dims, jnp.float32) * deviation
    if len(split) > 0:
        drawn = block_scale(own_key, dims, split, -0.22, 0.18) * drawn
    return jnp.clip(drawn, min=-limit, max=limit).astype(held_as)


def setup_inputs(seed: int = 0) -> dict:
    seeds = jax.random.split(jax.random.key(seed), 13)
    tokens = normal_values(seeds[0], (SEQUENCES, LENGTH, D), 1.0, 6.0, ((0, 4), (1, 8)))
    cotangent = normal_values(seeds[1], (SEQUENCES, LENGTH, D), 1.0, 6.0, ((0, 4), (1, 8)))
    gain_in = jnp.clip(1.0 + 0.1 * jax.random.normal(seeds[2], (D,), jnp.float32), 0.5, 1.5)
    w_mix = normal_values(seeds[3], (D, 3 * C + D), D ** -0.5, 0.21875)
    lower = draw_lower(jax.random.fold_in(seeds[12], 71), 0)
    fbias = draw_fbias(jax.random.fold_in(seeds[12], 71), 0)
    phase = jnp.clip(jax.random.uniform(seeds[6], (C,), jnp.float32, -0.5, 0.5), -0.5, 0.5)
    gain_out = jnp.clip(1.0 + 0.1 * jax.random.normal(seeds[7], (D,), jnp.float32), 0.5, 1.5)
    w_out = normal_values(seeds[8], (D, D), (D // 4) ** -0.5, 0.4375)
    gain_ffn = jnp.clip(1.0 + 0.1 * jax.random.normal(seeds[9], (D,), jnp.float32), 0.5, 1.5)
    w_gu = normal_values(seeds[10], (D, 2 * F), D ** -0.5, 0.21875)
    w_down = normal_values(seeds[11], (F, D), (F // 4) ** -0.5, 0.3125)
    return {"tokens": tokens, "cotangent": cotangent, "gain_in": gain_in, "w_mix": w_mix, "lower": lower, "fbias": fbias, "phase": phase, "gain_out": gain_out, "w_out": w_out, "gain_ffn": gain_ffn, "w_gu": w_gu, "w_down": w_down}


@jax.custom_vjp
def low(v):
    return lax.optimization_barrier(v.astype(jnp.bfloat16)).astype(jnp.float32)

@jax.custom_vjp
def low_back(v):
    return v

def low_keep(v):
    return (low(v), None)

def low_pass(kept, grad):
    return (grad,)

def back_keep(v):
    return (v, None)

def back_low(kept, grad):
    return (low(grad),)
low.defvjp(low_keep, low_pass)
low_back.defvjp(back_keep, back_low)
epsilon = 1e-06

def combine(earlier, later_part):
    mul_r, mul_i, add_r, add_i = earlier
    new_r, new_i, plus_r, plus_i = later_part
    out_mr = mul_r * new_r - mul_i * new_i
    out_mi = mul_r * new_i + mul_i * new_r
    out_ar = new_r * add_r - new_i * add_i + plus_r
    out_ai = new_r * add_i + new_i * add_r + plus_i
    return (out_mr, out_mi, out_ar, out_ai)

def normalize(values):
    return values * lax.rsqrt(lax.optimization_barrier(jnp.mean(values * values, axis=-1, keepdims=True)) + epsilon)

def matmul(left, right):
    return jnp.dot(left, right, precision=lax.Precision.HIGHEST, preferred_element_type=jnp.float32)

def sequence_block(inputs, params):
    gain_in, w_mix, lower, fbias, phase, gain_out, w_out, gain_ffn, w_gu, w_down = params
    normed_in = low(normalize(inputs) * gain_in)
    projected = low_back(matmul(normed_in, w_mix))
    in_r = jax.nn.silu(projected[:, :C])
    in_i = jax.nn.silu(projected[:, C:2 * C])
    forget = projected[:, 2 * C:3 * C] + fbias
    gate_pre = projected[:, 3 * C:]
    retain = lower + (1.0 - lower) * jax.nn.sigmoid(forget)
    intake = 1.0 - retain
    elements = (retain * jnp.cos(phase), retain * jnp.sin(phase), intake * in_r, intake * in_i)
    scanned = lax.associative_scan(combine, elements, axis=0)
    states = jnp.concatenate([scanned[2], scanned[3]], axis=-1)
    mixed = low(normalize(states) * gain_out * jax.nn.silu(gate_pre))
    after_mix = inputs + low_back(matmul(mixed, w_out))
    ffn_in = low(normalize(after_mix) * gain_ffn)
    gate_up = low_back(matmul(ffn_in, w_gu))
    hidden = low(jax.nn.silu(gate_up[:, :F]) * gate_up[:, F:])
    return after_mix + low_back(matmul(hidden, w_down))

def reference(tokens, cotangent, gain_in, w_mix, lower, fbias, phase, gain_out, w_out, gain_ffn, w_gu, w_down):
    params = (gain_in.astype(jnp.float32), w_mix.astype(jnp.float32), lower.astype(jnp.float32), fbias.astype(jnp.float32), phase.astype(jnp.float32), gain_out.astype(jnp.float32), w_out.astype(jnp.float32), gain_ffn.astype(jnp.float32), w_gu.astype(jnp.float32), w_down.astype(jnp.float32))
    inputs = tokens.astype(jnp.float32)

    def whole(values, weights):
        per_sequence = jax.checkpoint(lambda single: sequence_block(single, weights))
        return lax.map(per_sequence, values)
    result, pullback = jax.vjp(whole, inputs, params)
    grad_inputs, grads = pullback(cotangent.astype(jnp.float32))
    return (result.astype(jnp.bfloat16), grad_inputs, grads[1], grads[6], grads[8], grads[9], grads[0], grads[5], grads[7], grads[2], grads[3], grads[4])
```

```python
import functools

import jax
import jax.numpy as jnp
import numpy as np
from jax import lax
from jax.experimental import pallas as pl
from jax.experimental.pallas import tpu as pltpu
from jax.sharding import PartitionSpec as P

epsilon = 1e-06
LANES = 128
SUB = 8
F32 = jnp.float32
BF16 = jnp.bfloat16
MIB = 2**20
VM = 8


def sigmoid(values):
    return 0.5 * jnp.tanh(0.5 * values) + 0.5


def forget_gate(forget, lower):
    decay = jnp.exp(jnp.minimum(-forget, 80.0))
    total = 1.0 + decay
    guess = pl.reciprocal(total, approx=True)
    open_part = guess * (2.0 - total * guess)
    shut_part = decay * open_part
    intake = (1.0 - lower) * shut_part
    return open_part, shut_part, intake, 1.0 - intake


def dot(left, right, left_dim, right_dim):
    return lax.dot_general(
        left, right, (((left_dim,), (right_dim,)), ((), ())), preferred_element_type=F32
    )


def row_block(rows, most):
    best = 16
    for size in range(16, most + 1, 16):
        if rows % size == 0:
            best = size
    return best


def rows_at(step, size):
    return pl.ds(pl.multiple_of(step * size, 16), size)


def tile_of(ref, tile):
    return ref[:, tile * LANES : (tile + 1) * LANES]


def fold_rows(values):
    rows, lanes = values.shape
    return jnp.sum(values.reshape(rows // SUB, SUB, lanes), axis=0)


def loop(count, body):
    lax.fori_loop(0, count, lambda step, _: (body(step), 0)[1], 0)


def project_kernel(shape, tokens, gain, weight, lower, fbias, phase, low, pre, chunks, ends):
    seqs, positions, chans = shape
    tiles = chans // LANES
    steps = positions // SUB
    rows = seqs * positions
    size = row_block(rows, 336)

    def project(step):
        at = rows_at(step, size)
        inputs = tokens[at, :].astype(F32)
        scale = lax.rsqrt(jnp.mean(inputs * inputs, axis=-1, keepdims=True) + epsilon)
        block = (inputs * scale * gain[...]).astype(BF16)
        low[at, :] = block
        for part in range(3):
            made = dot(block, weight[:, part * chans : (part + 1) * chans], 1, 0)
            if part == 2:
                made = made + fbias[...]
            for tile in range(tiles):
                pre[part * tiles + tile, at, :] = made[:, tile * LANES : (tile + 1) * LANES]

    loop(rows // size, project)

    cosine, sine = jnp.cos(phase[...]), jnp.sin(phase[...])

    def scan(seq):
        for tile in range(tiles):
            lanes = slice(tile * LANES, (tile + 1) * LANES)
            low_bound, cos_t, sin_t = lower[:, lanes], cosine[:, lanes], sine[:, lanes]
            product = jnp.ones((SUB, LANES), F32)
            state_r = jnp.zeros((SUB, LANES), F32)
            state_i = jnp.zeros((SUB, LANES), F32)
            for step in range(steps):
                at = pl.ds(seq * positions + step, SUB, stride=steps)
                in_r, in_i = pre[tile, at, :], pre[tiles + tile, at, :]
                _, _, intake, retain = forget_gate(pre[2 * tiles + tile, at, :], low_bound)
                mul_r, mul_i = retain * cos_t, retain * sin_t
                add_r, add_i = intake * (in_r * sigmoid(in_r)), intake * (in_i * sigmoid(in_i))
                state_r, state_i = (
                    mul_r * state_r - mul_i * state_i + add_r,
                    mul_r * state_i + mul_i * state_r + add_i,
                )
                product = product * retain
            at = pl.ds(pl.multiple_of(seq * SUB, SUB), SUB)
            chunks[tile, at, :] = product
            chunks[tiles + tile, at, :] = state_r
            chunks[2 * tiles + tile, at, :] = state_i

    chunks[...] = jnp.zeros(chunks.shape, F32)
    loop(seqs, scan)

    span_c, span_s = jnp.cos(phase[...] * steps), jnp.sin(phase[...] * steps)
    pad = ends.shape[1]
    for tile in range(tiles):
        lanes = slice(tile * LANES, (tile + 1) * LANES)
        mul_r, mul_i = jnp.ones((pad, LANES), F32), jnp.zeros((pad, LANES), F32)
        add_r, add_i = jnp.zeros((pad, LANES), F32), jnp.zeros((pad, LANES), F32)
        for chunk in range(SUB):
            at = pl.ds(chunk, pad, stride=SUB)
            product = chunks[tile, at, :]
            new_r, new_i = product * span_c[:, lanes], product * span_s[:, lanes]
            plus_r, plus_i = chunks[tiles + tile, at, :], chunks[2 * tiles + tile, at, :]
            mul_r, mul_i = mul_r * new_r - mul_i * new_i, mul_r * new_i + mul_i * new_r
            add_r, add_i = (
                new_r * add_r - new_i * add_i + plus_r,
                new_r * add_i + new_i * add_r + plus_i,
            )
        ends[tile] = mul_r
        ends[tiles + tile] = mul_i
        ends[2 * tiles + tile] = add_r
        ends[3 * tiles + tile] = add_i


def gate_kernel(low, weight, gate):
    rows, width = gate.shape
    chans3 = weight.shape[1] - width
    size = row_block(rows, 336)

    def step_of(step):
        at = rows_at(step, size)
        gate[at, :] = dot(low[at, :], weight[:, chans3:], 1, 0)

    loop(rows // size, step_of)


def hidden_back_kernel(upstream, weight, made):
    rows, units = made.shape
    size = row_block(rows, 336)

    def step_of(step):
        at = rows_at(step, size)
        for part in range(units // 256):
            cols = slice(part * 256, (part + 1) * 256)
            made[at, cols] = dot(upstream[at, :], weight[cols, :], 1, 1).astype(BF16)

    loop(rows // size, step_of)


def mix_kernel(
    shape, pre, chunks, start, gate, tokens, phase, lower, gain_out, gain_ffn, w_out,
    states, entries, mixed, after, ffn_low,
):
    seqs, positions, chans = shape
    tiles = chans // LANES
    steps = positions // SUB
    rows = seqs * positions
    size = row_block(rows, 144)
    pad = start.shape[1]
    span_c, span_s = jnp.cos(phase[...] * steps), jnp.sin(phase[...] * steps)
    for tile in range(tiles):
        lanes = slice(tile * LANES, (tile + 1) * LANES)
        now_r, now_i = start[tile], start[tiles + tile]
        for chunk in range(SUB):
            at = pl.ds(chunk, pad, stride=SUB)
            entries[tile, at, :] = now_r
            entries[tiles + tile, at, :] = now_i
            product = chunks[tile, at, :]
            new_r, new_i = product * span_c[:, lanes], product * span_s[:, lanes]
            now_r, now_i = (
                new_r * now_r - new_i * now_i + chunks[tiles + tile, at, :],
                new_r * now_i + new_i * now_r + chunks[2 * tiles + tile, at, :],
            )
    cosine, sine = jnp.cos(phase[...]), jnp.sin(phase[...])

    def scan(seq):
        for tile in range(tiles):
            lanes = slice(tile * LANES, (tile + 1) * LANES)
            low_bound, cos_t, sin_t = lower[:, lanes], cosine[:, lanes], sine[:, lanes]
            at = pl.ds(pl.multiple_of(seq * SUB, SUB), SUB)
            state_r, state_i = entries[tile, at, :], entries[tiles + tile, at, :]
            for step in range(steps):
                at = pl.ds(seq * positions + step, SUB, stride=steps)
                in_r, in_i = pre[tile, at, :], pre[tiles + tile, at, :]
                _, _, intake, retain = forget_gate(pre[2 * tiles + tile, at, :], low_bound)
                mul_r, mul_i = retain * cos_t, retain * sin_t
                add_r, add_i = intake * (in_r * sigmoid(in_r)), intake * (in_i * sigmoid(in_i))
                state_r, state_i = (
                    mul_r * state_r - mul_i * state_i + add_r,
                    mul_r * state_i + mul_i * state_r + add_i,
                )
                states[tile, at, :] = state_r
                states[tiles + tile, at, :] = state_i

    loop(seqs, scan)

    def mix(step):
        at = rows_at(step, size)
        squares = jnp.zeros((size, LANES), F32)
        for tile in range(2 * tiles):
            part = states[tile, at, :]
            squares = squares + part * part
        scale = lax.rsqrt(jnp.sum(squares, axis=-1, keepdims=True) / (2 * chans) + epsilon)
        for tile in range(2 * tiles):
            lanes = slice(tile * LANES, (tile + 1) * LANES)
            gated = gate[at, lanes]
            part = states[tile, at, :] * scale * gain_out[:, lanes] * (gated * sigmoid(gated))
            mixed[at, lanes] = part.astype(BF16)
        total = tokens[at, :].astype(F32) + dot(mixed[at, :], w_out[...], 1, 0)
        after[at, :] = total
        scale = lax.rsqrt(jnp.mean(total * total, axis=-1, keepdims=True) + epsilon)
        ffn_low[at, :] = (total * scale * gain_ffn[...]).astype(BF16)

    loop(rows // size, mix)


def ffn_kernel(ffn_low, w_gu, hidden_back, hidden, grad_gu):
    rows, units = hidden.shape
    size = row_block(rows, 336)
    wide = 256

    def step_of(step):
        at = rows_at(step, size)
        block = ffn_low[at, :]
        for part in range(units // wide):
            cols = slice(part * wide, (part + 1) * wide)
            later = slice(units + part * wide, units + (part + 1) * wide)
            gate = dot(block, w_gu[:, cols], 1, 0)
            up = dot(block, w_gu[:, later], 1, 0)
            back = hidden_back[at, cols].astype(F32)
            sigma = sigmoid(gate)
            act = gate * sigma
            hidden[at, cols] = (act * up).astype(BF16)
            grad_gu[at, cols] = (back * up * (sigma + act * (1.0 - sigma))).astype(BF16)
            grad_gu[at, later] = (back * act).astype(BF16)

    loop(rows // size, step_of)


def store_blocks(ref, slots, first, blocks, size, cols, values):
    for block in range(blocks):
        at = pl.ds(pl.multiple_of(slots[first + block] * size, SUB), size)
        ref[at, cols] = values[block * size : (block + 1) * size, :]


def grad_narrow_kernel(blocks, slots, *refs):
    pairs, (keep, send, turned) = refs[:-3], refs[-3:]
    mine = slots[2 * blocks]
    for index in range(len(pairs) // 2):
        left, right = pairs[2 * index], pairs[2 * index + 1]
        half = right.shape[1] // 2
        keep_at = pl.ds(pl.multiple_of(mine * half, LANES), half)
        send_at = pl.ds(pl.multiple_of((1 - mine) * half, LANES), half)
        turned[:, :half] = right[:, keep_at]
        turned[:, half:] = right[:, send_at]
        size = left.shape[1] // blocks
        tall = min(left.shape[1], 384)
        cols = slice(index * half, (index + 1) * half)
        for part in range(left.shape[1] // tall):
            made = dot(left[:, part * tall : (part + 1) * tall], turned[...], 0, 0)
            count = tall // size
            first = part * count
            store_blocks(keep, slots, first, count, size, cols, made[:, :half])
            store_blocks(send, slots, blocks + first, count, size, cols, made[:, half:])


def grad_wide_kernel(blocks, wide, slots, left, right, keep, send):
    mine = slots[2 * blocks]
    half = right.shape[1] // 2
    size = left.shape[1] // blocks

    def step_of(part):
        cols = pl.ds(pl.multiple_of(part * wide, LANES), wide)
        for ref, owner, base in ((keep, mine, 0), (send, 1 - mine, blocks)):
            source = pl.ds(pl.multiple_of(owner * half + part * wide, LANES), wide)
            made = dot(left[...], right[:, source], 0, 0)
            store_blocks(ref, slots, base, blocks, size, cols, made)

    loop(half // wide, step_of)


def middle_back_kernel(
    shape, grad_gu, w_gu, after, cotangent, gain_ffn, w_out, states, gate, gain_out, pre, chunks, lower, phase,
    grad_mid, grad_mid_low, grad_gate, seeds, chunks_back, ends_back, sums,
):
    seqs, positions, chans = shape
    tiles = chans // LANES
    steps = positions // SUB
    rows = seqs * positions
    width = 2 * chans
    size = row_block(rows, 336)
    sums[...] = jnp.zeros(sums.shape, F32)

    def ffn_back(step):
        at = rows_at(step, size)
        back = dot(grad_gu[at, :], w_gu[...], 1, 1)
        total = after[at, :]
        scale = lax.rsqrt(jnp.mean(total * total, axis=-1, keepdims=True) + epsilon)
        normed = total * scale
        sums[0:SUB, :] += fold_rows(back * normed)
        scaled = back * gain_ffn[...]
        shared = jnp.mean(scaled * normed, axis=-1, keepdims=True)
        made = cotangent[at, :].astype(F32) + scale * (scaled - normed * shared)
        grad_mid[at, :] = made
        grad_mid_low[at, :] = made.astype(BF16)

    loop(rows // size, ffn_back)
    small = row_block(rows, 144)

    def mix_back(step):
        at = rows_at(step, small)
        back = dot(grad_mid_low[at, :], w_out[...], 1, 1)
        squares = jnp.zeros((small, LANES), F32)
        for tile in range(2 * tiles):
            part = states[tile, at, :]
            squares = squares + part * part
        scale = lax.rsqrt(jnp.sum(squares, axis=-1, keepdims=True) / width + epsilon)
        shared = jnp.zeros((small, LANES), F32)
        for tile in range(2 * tiles):
            lanes = slice(tile * LANES, (tile + 1) * LANES)
            gated = gate[at, lanes]
            sigma = sigmoid(gated)
            act = gated * sigma
            normed = states[tile, at, :] * scale
            part = back[:, lanes]
            gain = gain_out[:, lanes]
            grad_gate[at, lanes] = (part * normed * gain * (sigma + act * (1.0 - sigma))).astype(BF16)
            inner = part * act
            product = inner * normed
            sums[SUB : 2 * SUB, lanes] += fold_rows(product)
            shared = shared + product * gain
            seeds[tile, at, :] = inner * gain
        mean = jnp.sum(shared, axis=-1, keepdims=True) / width
        for tile in range(2 * tiles):
            normed = states[tile, at, :] * scale
            seeds[tile, at, :] = scale * (seeds[tile, at, :] - normed * mean)

    loop(rows // small, mix_back)
    cosine, sine = jnp.cos(phase[...]), jnp.sin(phase[...])

    def scan(seq):
        for tile in range(tiles):
            lanes = slice(tile * LANES, (tile + 1) * LANES)
            low_bound, cos_t, sin_t = lower[:, lanes], cosine[:, lanes], sine[:, lanes]
            flow_r = jnp.zeros((SUB, LANES), F32)
            flow_i = jnp.zeros((SUB, LANES), F32)
            for step in reversed(range(steps)):
                at = pl.ds(seq * positions + step, SUB, stride=steps)
                _, _, _, retain = forget_gate(pre[2 * tiles + tile, at, :], low_bound)
                mul_r, mul_i = retain * cos_t, retain * sin_t
                adj_r = seeds[tile, at, :] + flow_r
                adj_i = seeds[tiles + tile, at, :] + flow_i
                flow_r = mul_r * adj_r + mul_i * adj_i
                flow_i = mul_r * adj_i - mul_i * adj_r
            at = pl.ds(pl.multiple_of(seq * SUB, SUB), SUB)
            chunks_back[tile, at, :] = flow_r
            chunks_back[tiles + tile, at, :] = flow_i

    chunks_back[...] = jnp.zeros(chunks_back.shape, F32)
    loop(seqs, scan)
    span_c, span_s = jnp.cos(phase[...] * steps), jnp.sin(phase[...] * steps)
    pad = ends_back.shape[1]
    for tile in range(tiles):
        lanes = slice(tile * LANES, (tile + 1) * LANES)
        mul_r, mul_i = jnp.ones((pad, LANES), F32), jnp.zeros((pad, LANES), F32)
        add_r, add_i = jnp.zeros((pad, LANES), F32), jnp.zeros((pad, LANES), F32)
        for chunk in reversed(range(SUB)):
            at = pl.ds(chunk, pad, stride=SUB)
            product = chunks[tile, at, :]
            new_r, new_i = product * span_c[:, lanes], -product * span_s[:, lanes]
            plus_r, plus_i = chunks_back[tile, at, :], chunks_back[tiles + tile, at, :]
            mul_r, mul_i = mul_r * new_r - mul_i * new_i, mul_r * new_i + mul_i * new_r
            add_r, add_i = (
                new_r * add_r - new_i * add_i + plus_r,
                new_r * add_i + new_i * add_r + plus_i,
            )
        ends_back[tile] = mul_r
        ends_back[tiles + tile] = mul_i
        ends_back[2 * tiles + tile] = add_r
        ends_back[3 * tiles + tile] = add_i


def scan_back_kernel(
    shape, blocks, slots, seeds, chunks, chunks_back, enter, pre, states, entries, lower, phase, low,
    grad_pre, sums, keep, send, entries_back, made_pre, turned,
):
    seqs, positions, chans = shape
    tiles = chans // LANES
    steps = positions // SUB
    rows = seqs * positions
    pad = enter.shape[1]
    span_c, span_s = jnp.cos(phase[...] * steps), jnp.sin(phase[...] * steps)
    for tile in range(tiles):
        lanes = slice(tile * LANES, (tile + 1) * LANES)
        now_r, now_i = enter[tile], enter[tiles + tile]
        for chunk in reversed(range(SUB)):
            at = pl.ds(chunk, pad, stride=SUB)
            entries_back[tile, at, :] = now_r
            entries_back[tiles + tile, at, :] = now_i
            product = chunks[tile, at, :]
            new_r, new_i = product * span_c[:, lanes], -product * span_s[:, lanes]
            now_r, now_i = (
                new_r * now_r - new_i * now_i + chunks_back[tile, at, :],
                new_r * now_i + new_i * now_r + chunks_back[tiles + tile, at, :],
            )
    cosine, sine = jnp.cos(phase[...]), jnp.sin(phase[...])
    sums[...] = jnp.zeros(sums.shape, F32)
    mine = slots[2 * blocks]
    half = keep.shape[1]
    shift = 3 * chans - half
    keep_at = pl.ds(pl.multiple_of(mine * shift, LANES), half)
    send_at = pl.ds(pl.multiple_of((1 - mine) * shift, LANES), half)

    def scan(seq):
        for tile in range(tiles):
            lanes = slice(tile * LANES, (tile + 1) * LANES)
            low_bound, cos_t, sin_t = lower[:, lanes], cosine[:, lanes], sine[:, lanes]
            chunk_at = pl.ds(pl.multiple_of(seq * SUB, SUB), SUB)
            flow_r, flow_i = entries_back[tile, chunk_at, :], entries_back[tiles + tile, chunk_at, :]
            sum_lower = jnp.zeros((SUB, LANES), F32)
            sum_fbias = jnp.zeros((SUB, LANES), F32)
            sum_phase = jnp.zeros((SUB, LANES), F32)
            for step in reversed(range(steps)):
                at = pl.ds(seq * positions + step, SUB, stride=steps)
                in_r, in_i = pre[tile, at, :], pre[tiles + tile, at, :]
                opened, shut, intake, retain = forget_gate(pre[2 * tiles + tile, at, :], low_bound)
                sig_r, sig_i = sigmoid(in_r), sigmoid(in_i)
                act_r, act_i = in_r * sig_r, in_i * sig_i
                adj_r = seeds[tile, at, :] + flow_r
                adj_i = seeds[tiles + tile, at, :] + flow_i
                mul_r, mul_i = retain * cos_t, retain * sin_t
                flow_r = mul_r * adj_r + mul_i * adj_i
                flow_i = mul_r * adj_i - mul_i * adj_r
                if step > 0:
                    before = pl.ds(seq * positions + step - 1, SUB, stride=steps)
                    past_r, past_i = states[tile, before, :], states[tiles + tile, before, :]
                else:
                    past_r, past_i = entries[tile, chunk_at, :], entries[tiles + tile, chunk_at, :]
                grad_r = adj_r * past_r + adj_i * past_i
                grad_i = adj_i * past_r - adj_r * past_i
                grad_retain = grad_r * cos_t + grad_i * sin_t - (adj_r * act_r + adj_i * act_i)
                sum_phase = sum_phase + retain * (grad_i * cos_t - grad_r * sin_t)
                sum_lower = sum_lower + grad_retain * shut
                grad_forget = grad_retain * intake * opened
                sum_fbias = sum_fbias + grad_forget
                at = pl.ds(step, SUB, stride=steps)
                made_pre[tile, at, :] = adj_r * intake * (sig_r + act_r * (1.0 - sig_r))
                made_pre[tiles + tile, at, :] = adj_i * intake * (sig_i + act_i * (1.0 - sig_i))
                made_pre[2 * tiles + tile, at, :] = grad_forget
            sums[0:SUB, lanes] += sum_lower
            sums[SUB : 2 * SUB, lanes] += sum_fbias
            sums[2 * SUB : 3 * SUB, lanes] += sum_phase

        seq_rows = rows_at(seq, positions)
        for tile in range(3 * tiles):
            grad_pre[seq_rows, tile * LANES : (tile + 1) * LANES] = made_pre[tile].astype(BF16)
        turned[seq_rows, :half] = grad_pre[seq_rows, keep_at]
        turned[seq_rows, half:] = grad_pre[seq_rows, send_at]

    loop(seqs, scan)
    block_rows = low.shape[1] // blocks
    tall = min(low.shape[1], 384)
    count = tall // block_rows
    for part in range(low.shape[1] // tall):
        made = dot(low[:, part * tall : (part + 1) * tall], turned[...], 0, 0)
        store_blocks(keep, slots, part * count, count, block_rows, slice(0, half), made[:, :half])
        store_blocks(
            send, slots, blocks + part * count, count, block_rows, slice(0, half), made[:, half:]
        )


def input_back_kernel(grad_pre, grad_gate, w_mix, tokens, gain, grad_mid, grad_tokens, sums):
    rows, chans3 = grad_pre.shape
    size = row_block(rows, 336)
    sums[...] = jnp.zeros(sums.shape, F32)

    def step_of(step):
        at = rows_at(step, size)
        back = dot(grad_pre[at, :], w_mix[:, :chans3], 1, 1)
        back = back + dot(grad_gate[at, :], w_mix[:, chans3:], 1, 1)
        inputs = tokens[at, :].astype(F32)
        scale = lax.rsqrt(jnp.mean(inputs * inputs, axis=-1, keepdims=True) + epsilon)
        normed = inputs * scale
        sums[...] += fold_rows(back * normed)
        scaled = back * gain[...]
        shared = jnp.mean(scaled * normed, axis=-1, keepdims=True)
        grad_tokens[at, :] = grad_mid[at, :] + scale * (scaled - normed * shared)

    loop(rows // size, step_of)


def output_kernel(after, hidden, w_down, output):
    rows, _ = output.shape
    size = row_block(rows, 336)

    def step_of(step):
        at = rows_at(step, size)
        output[at, :] = (after[at, :] + dot(hidden[at, :], w_down[...], 1, 0)).astype(BF16)

    loop(rows // size, step_of)


def call(kernel, name, args, outs, scratch=(), smem=0, vmem=VM, flops=0):
    in_specs = [pl.BlockSpec(memory_space=pltpu.SMEM)] * smem
    in_specs = in_specs + [pl.BlockSpec(memory_space=pltpu.VMEM)] * (len(args) - smem)
    made = pl.pallas_call(
        kernel,
        out_shape=[jax.ShapeDtypeStruct(shape, kind) for shape, kind in outs],
        in_specs=in_specs,
        out_specs=[pl.BlockSpec(memory_space=pltpu.VMEM)] * len(outs),
        scratch_shapes=list(scratch),
        compiler_params=pltpu.CompilerParams(vmem_limit_bytes=vmem * MIB),
        cost_estimate=pl.CostEstimate(flops=flops, bytes_accessed=1024, transcendentals=0),
        name=name,
    )(*args)
    return made


def flipped(seq_size, batch_size, dims):
    pairs = []
    for seq in range(seq_size):
        for batch in range(batch_size):
            axis, bit = dims[batch & 1]
            to = (seq ^ bit, batch) if axis == "seq" else (seq, batch ^ bit)
            pairs.append((seq * batch_size + batch, to[0] * batch_size + to[1]))
    return pairs


def step_orders(seq_size, batch_size):
    along_seq = [("seq", 1 << bit) for bit in range(seq_size.bit_length() - 1)]
    along_batch = [("batch", 1 << bit) for bit in range(1, batch_size.bit_length() - 1)]
    return (along_seq + along_batch, along_batch + along_seq)


def slot_table(seq_size, batch_size):
    orders = step_orders(seq_size, batch_size)
    seq, batch = lax.axis_index("seq"), lax.axis_index("batch")
    rest = batch_size // 2
    block = np.arange(seq_size * rest)
    seq_diff = jnp.asarray(block // rest, jnp.int32) ^ seq
    batch_diff = jnp.asarray((block % rest) * 2, jnp.int32) ^ (batch & ~1)

    def slots(order):
        count = len(order)
        total = jnp.zeros(block.shape, jnp.int32)
        for place, (axis, bit) in enumerate(order):
            diff = seq_diff if axis == "seq" else batch_diff
            total = total + jnp.where((diff & bit) != 0, 1 << (count - 1 - place), 0)
        return total

    first, second = slots(orders[0]), slots(orders[1])
    odd = (batch & 1) == 1
    keep, send = jnp.where(odd, second, first), jnp.where(odd, first, second)
    return jnp.concatenate([keep, send, (batch & 1).astype(jnp.int32)[None]])


def combine(earlier, later_part):
    mul_r, mul_i, add_r, add_i = earlier
    new_r, new_i, plus_r, plus_i = later_part
    out_mr = mul_r * new_r - mul_i * new_i
    out_mi = mul_r * new_i + mul_i * new_r
    out_ar = new_r * add_r - new_i * add_i + plus_r
    out_ai = new_r * add_i + new_i * add_r + plus_i
    return (out_mr, out_mi, out_ar, out_ai)


def carried(ends, backward):
    size = lax.axis_size("seq")
    mine = lax.axis_index("seq")
    tiles = ends.shape[0] // 4

    def parts(values):
        return tuple(values[part * tiles : (part + 1) * tiles] for part in range(4))

    total = ends
    one, zero = jnp.ones(ends[:tiles].shape, F32), jnp.zeros(ends[:tiles].shape, F32)
    before = (one, zero, zero, zero)
    bit = 1
    while bit < size:
        got = lax.ppermute(total, "seq", [(at, at ^ bit) for at in range(size)])
        later = (mine & bit) != 0
        if backward:
            later = jnp.logical_not(later)
        mine_parts, got_parts = parts(total), parts(got)
        longer = combine(got_parts, before)
        before = tuple(jnp.where(later, new, old) for new, old in zip(longer, before))
        if 2 * bit < size:
            first = tuple(jnp.where(later, b, a) for a, b in zip(mine_parts, got_parts))
            second = tuple(jnp.where(later, a, b) for a, b in zip(mine_parts, got_parts))
            total = jnp.concatenate(combine(first, second), axis=0)
        bit *= 2
    return jnp.concatenate([before[2], before[3]], axis=0)


def scatter_sum(keep, send, seq_size, batch_size):
    orders = step_orders(seq_size, batch_size)
    got = lax.ppermute(send, "batch", [(at, at ^ 1) for at in range(batch_size)])
    for first, second in zip(*orders):
        half = keep.shape[0] // 2
        out = keep[half:] + got[half:]
        keep = keep[:half] + got[:half]
        got = lax.ppermute(
            out, ("seq", "batch"), flipped(seq_size, batch_size, (first, second))
        )
    return keep + got


def gather_batch(values, bit, batch_size):
    other = lax.ppermute(values, "batch", [(at, at ^ bit) for at in range(batch_size)])
    upper = (lax.axis_index("batch") & bit) != 0
    return jnp.where(upper, other, values), jnp.where(upper, values, other)


def per_device(
    tokens, cotangent, gain_in, w_mix, lower, fbias, phase, gain_out, w_out, gain_ffn, w_gu, w_down
):
    seqs, positions, width = tokens.shape
    chans = lower.shape[0]
    units = w_down.shape[0]
    rows = seqs * positions
    tiles = chans // LANES
    shape = (seqs, positions, chans)
    pad = -(-seqs // SUB) * SUB
    seq_size, batch_size = lax.axis_size("seq"), lax.axis_size("batch")
    blocks = seq_size * batch_size // 2
    tokens = tokens.reshape(rows, width)
    cotangent = cotangent.reshape(rows, width)
    gain_in, gain_out, gain_ffn = gain_in[None], gain_out[None], gain_ffn[None]
    lower, fbias, phase = lower[None], fbias[None], phase[None]
    slots = slot_table(seq_size, batch_size)
    in_place = width % (blocks * SUB) == 0
    if in_place:
        made_blocks, used = blocks, slots
    else:
        made_blocks = 2 * SUB
        natural = jnp.arange(made_blocks, dtype=jnp.int32)
        used = jnp.concatenate([natural, natural, slots[2 * blocks :]])

    def arranged(keep, send):
        if in_place:
            return keep, send
        made = []
        for index, values in enumerate((keep, send)):
            order = jnp.argsort(slots[index * blocks : (index + 1) * blocks])
            cut = values.reshape((blocks, -1) + values.shape[1:])
            made.append(jnp.take(cut, order, axis=0).reshape(values.shape))
        return made

    def reduced(keep, send):
        keep, send = arranged(keep, send)
        return scatter_sum(keep, send, seq_size, batch_size)

    low, pre, chunks, ends = call(
        functools.partial(project_kernel, shape), "project",
        (tokens, gain_in, w_mix, lower, fbias, phase),
        [((rows, width), BF16), ((3 * tiles, rows, LANES), F32), ((3 * tiles, pad * SUB, LANES), F32), ((4 * tiles, pad, LANES), F32)],
        flops=2 * rows * width * 3 * chans,
    )
    (gate,) = call(gate_kernel, "gate", (low, w_mix), [((rows, width), F32)], flops=2 * rows * width * width)
    (hidden_back,) = call(
        hidden_back_kernel, "hidden_back", (cotangent, w_down), [((rows, units), BF16)], flops=2 * rows * width * units
    )
    start = carried(ends, False)
    states, entries, mixed, after, ffn_low = call(
        functools.partial(mix_kernel, shape), "mix",
        (pre, chunks, start, gate, tokens, phase, lower, gain_out, gain_ffn, w_out),
        [((2 * tiles, rows, LANES), F32), ((2 * tiles, pad * SUB, LANES), F32), ((rows, width), BF16), ((rows, width), F32), ((rows, width), BF16)],
        flops=2 * rows * width * width,
    )
    hidden, grad_gu = call(
        ffn_kernel, "ffn", (ffn_low, w_gu, hidden_back),
        [((rows, units), BF16), ((rows, 2 * units), BF16)], flops=4 * rows * width * units,
    )
    down = call(
        functools.partial(grad_narrow_kernel, made_blocks), "grad_down", (used, hidden, cotangent),
        [((units, width // 2), F32)] * 2, [pltpu.VMEM((rows, width), BF16)], smem=1, flops=2 * rows * width * units,
    )
    wide = call(
        functools.partial(grad_wide_kernel, made_blocks, 512), "grad_gu", (used, ffn_low, grad_gu),
        [((width, units), F32)] * 2, smem=1, flops=4 * rows * width * units,
    )
    grad_mid, grad_mid_low, grad_gate, seeds, chunks_back, ends_back, sums_mid = call(
        functools.partial(middle_back_kernel, shape), "middle_back",
        (grad_gu, w_gu, after, cotangent, gain_ffn, w_out, states, gate, gain_out, pre, chunks, lower, phase),
        [((rows, width), F32), ((rows, width), BF16), ((rows, width), BF16), ((2 * tiles, rows, LANES), F32),
         ((2 * tiles, pad * SUB, LANES), F32), ((4 * tiles, pad, LANES), F32), ((2 * SUB, width), F32)],
        flops=2 * rows * width * (2 * units + width),
    )
    third = call(
        functools.partial(grad_narrow_kernel, made_blocks), "grad_out_gate",
        (used, mixed, grad_mid_low, low, grad_gate),
        [((width, width), F32)] * 2, [pltpu.VMEM((rows, width), BF16)], smem=1, flops=4 * rows * width * width,
    )
    enter = carried(ends_back, True)
    span = -(-3 * tiles // 2) * LANES
    grad_pre, sums_scan, *fourth = call(
        functools.partial(scan_back_kernel, shape, made_blocks), "scan_back",
        (used, seeds, chunks, chunks_back, enter, pre, states, entries, lower, phase, low),
        [((rows, 3 * chans), BF16), ((3 * SUB, chans), F32), ((width, span), F32), ((width, span), F32)],
        [pltpu.VMEM((2 * tiles, pad * SUB, LANES), F32), pltpu.VMEM((3 * tiles, positions, LANES), F32), pltpu.VMEM((rows, 2 * span), BF16)],
        smem=1, flops=2 * rows * width * 3 * chans,
    )
    grad_tokens, sums_in = call(
        input_back_kernel, "input_back", (grad_pre, grad_gate, w_mix, tokens, gain_in, grad_mid),
        [((rows, width), F32), ((SUB, width), F32)], flops=2 * rows * width * (3 * chans + width),
    )
    (output,) = call(
        output_kernel, "output", (after, hidden, w_down), [((rows, width), BF16)], flops=2 * rows * width * units
    )

    parts = [reduced(*pair) for pair in (down, wide, third, fourth)]
    gathered = []
    for part in parts:
        bit = 2
        while bit < batch_size:
            part = jnp.concatenate(gather_batch(part, bit, batch_size), axis=0)
            bit *= 2
        gathered.append(part)
    sides = [gather_batch(part, 1, batch_size) for part in gathered]
    half = width // 2
    grad_down = jnp.concatenate(sides[0], axis=1)
    grad_wide = jnp.concatenate(sides[1], axis=1)
    grad_out = jnp.concatenate([side[:, :half] for side in sides[2]], axis=1)
    shared = 2 * span - 3 * chans
    grad_mix = jnp.concatenate(
        [sides[3][0], sides[3][1][:, shared:]] + [side[:, half:] for side in sides[2]], axis=1
    )

    vectors = jnp.concatenate(
        [
            jnp.sum(sums_in, axis=0),
            jnp.sum(sums_mid.reshape(2, SUB, width), axis=1)[::-1].reshape(-1),
            jnp.sum(sums_scan.reshape(3, SUB, chans), axis=1).reshape(-1),
        ]
    ).reshape(-1, LANES)
    for axis, size in (("batch", batch_size), ("seq", seq_size)):
        bit = 1
        while bit < size:
            vectors = vectors + lax.ppermute(vectors, axis, [(at, at ^ bit) for at in range(size)])
            bit *= 2
    vectors = vectors.reshape(-1)
    cuts = np.cumsum([width, width, width, chans, chans]).tolist()
    gains = jnp.split(vectors, cuts)
    return (
        output.reshape(seqs, positions, width),
        grad_tokens.reshape(seqs, positions, width),
        grad_mix,
        grad_out,
        grad_wide,
        grad_down,
        *gains,
    )


def solution(mesh):
    in_specs = (P("batch", "seq", None), P("batch", "seq", None)) + (P(),) * 10
    rows = P("seq", None)
    out_specs = (P("batch", "seq", None), P("batch", "seq", None), rows, rows, rows, rows) + (P(),) * 6
    return jax.shard_map(
        per_device, mesh=mesh, in_specs=in_specs, out_specs=out_specs, check_vma=False
    )
```

```python
import functools
import types

import jax
import jax.numpy as jnp
import numpy as np
from jax import lax
from jax.experimental import pallas as pl
from jax.experimental.pallas import tpu as pltpu
from jax.sharding import PartitionSpec as P

epsilon = 1e-06
LANES = 128
SUB = 8
F32 = jnp.float32
BF16 = jnp.bfloat16
MIB = 2**20


class Names:
    def __getattr__(self, name):
        return name


N = Names()
SCALE = 0.2
FOLD = 0.3
HOPS = (2, 1, 0)
ORDERS = {N.wide: (N.yzxw, N.xwyz), N.down: (N.yxwz, N.xyzw), N.scan: (N.yxzw, N.zxyw)}
ROUNDS = N.wpsposwpswpssp
DEPS = {N.s0: "p0 w2", N.p1: N.s0, "o": N.p1, N.s1: "o", N.w3: N.s1, N.p2: N.s1, N.p3: N.s2, N.w4: N.s2, N.s3: N.w4, N.p4: N.s4}
PIECES = 2
TIME = {
    N.project: 8.0, N.gate: 1.8, N.hidden_back: 1.9, N.mix: 5.9, N.ffn: 7.3, N.grad_gu: 3.2, N.grad_down: 3.6, N.ffn_back: 6.5,
    N.mix_back: 7.0, N.grad_out: 1.6, N.grad_gate: 1.6, N.scan_back: 4.0, N.input_back: 5.6, N.grad_scan: 2.4, N.output: 7.0,
}


def sigmoid(values):
    return 0.5 * jnp.tanh(0.5 * values) + 0.5


def forget_gate(forget, lower):
    decay = jnp.exp(jnp.minimum(-forget, 80.0))
    total = 1.0 + decay
    guess = pl.reciprocal(total, approx=True)
    open_part = guess * (2.0 - total * guess)
    shut_part = decay * open_part
    intake = (1.0 - lower) * shut_part
    return open_part, shut_part, intake, 1.0 - intake


def dot(left, right, left_dim, right_dim):
    return lax.dot_general(
        left, right, (((left_dim,), (right_dim,)), ((), ())), preferred_element_type=F32
    )


def row_block(rows, most):
    best = 16
    for size in range(16, most + 1, 16):
        if rows % size == 0:
            best = size
    return best


def rows_at(step, size):
    return pl.ds(pl.multiple_of(step * size, 16), size)


def tile_of(ref, tile):
    return ref[:, tile * LANES : (tile + 1) * LANES]


def fold_rows(values):
    rows, lanes = values.shape
    return jnp.sum(values.reshape(rows // SUB, SUB, lanes), axis=0)


def loop(count, body):
    lax.fori_loop(0, count, lambda step, _: (body(step), 0)[1], 0)


def project_kernel(shape, r):
    seqs, positions, chans = shape
    tiles = chans // LANES
    steps = positions // SUB
    rows = seqs * positions
    size = row_block(rows, 336)
    width = r.tok.shape[1]
    r.vec[...] = jnp.zeros(r.vec.shape, F32)
    for name in (N.raw_in, N.raw_lower, N.raw_fbias, N.raw_phase, N.raw_out, N.raw_ffn):
        r.wait(name)
    for row, name in enumerate((N.raw_in, N.raw_out, N.raw_ffn)):
        r.vec[row : row + 1, :] = getattr(r, name)[...].reshape(1, width)
    phase = r.raw_phase[...].reshape(1, chans)
    r.vec[3:4, :chans] = r.raw_lower[...].reshape(1, chans)
    r.vec[3:4, chans:] = r.raw_fbias[...].reshape(1, chans)
    r.vec[4:5, :chans] = jnp.cos(phase)
    r.vec[4:5, chans:] = jnp.sin(phase)
    r.vec[5:6, :chans] = jnp.cos(phase * steps)
    r.vec[5:6, chans:] = jnp.sin(phase * steps)
    r.vec[6:7, :chans] = jnp.cos(phase * positions)
    r.vec[6:7, chans:] = jnp.sin(phase * positions)
    gain = r.vec[0:1, :]
    fbias = r.vec[3:4, chans:]
    r.wait(N.tok)

    def norm(step):
        at = rows_at(step, size)
        inputs = r.tok[at, :].astype(F32)
        scale = lax.rsqrt(jnp.mean(inputs * inputs, axis=-1, keepdims=True) + epsilon)
        r.low[at, :] = (inputs * scale * gain).astype(BF16)

    loop(rows // size, norm)
    r.wait(N.wmix)
    r.start_late()

    def project(step):
        at = rows_at(step, size)
        for part in range(3):
            made = dot(r.low[at, :], r.wmix[:, part * chans : (part + 1) * chans], 1, 0)
            if part == 2:
                made = made + fbias
            for tile in range(tiles):
                r.pre[part * tiles + tile, at, :] = made[:, tile * LANES : (tile + 1) * LANES]

    loop(rows // size, project)

    def scan(seq):
        for tile in range(tiles):
            lanes = slice(tile * LANES, (tile + 1) * LANES)
            low_bound, cos_t, sin_t = r.vec[3:4, lanes], r.vec[4:5, lanes], sine_of(r, lanes)
            product = jnp.ones((SUB, LANES), F32)
            state_r = jnp.zeros((SUB, LANES), F32)
            state_i = jnp.zeros((SUB, LANES), F32)
            for step in range(steps):
                at = pl.ds(seq * positions + step, SUB, stride=steps)
                in_r, in_i = r.pre[tile, at, :], r.pre[tiles + tile, at, :]
                _, _, intake, retain = forget_gate(r.pre[2 * tiles + tile, at, :], low_bound)
                mul_r, mul_i = retain * cos_t, retain * sin_t
                add_r, add_i = intake * (in_r * sigmoid(in_r)), intake * (in_i * sigmoid(in_i))
                state_r, state_i = (
                    mul_r * state_r - mul_i * state_i + add_r,
                    mul_r * state_i + mul_i * state_r + add_i,
                )
                product = product * retain
                r.steps[tile, at, :] = retain
                r.steps[tiles + tile, at, :] = add_r
                r.steps[2 * tiles + tile, at, :] = add_i
            at = pl.ds(pl.multiple_of(seq * SUB, SUB), SUB)
            r.chunks[tile, at, :] = product
            r.chunks[tiles + tile, at, :] = state_r
            r.chunks[2 * tiles + tile, at, :] = state_i

    r.chunks[...] = jnp.zeros(r.chunks.shape, F32)
    loop(seqs, scan)
    joined(r, tiles, r.chunks, tiles, r.ends, False)


def sine_of(r, lanes):
    chans = r.vec.shape[1] // 2
    return r.vec[4:5, chans + lanes.start : chans + lanes.stop]


def chunk_step(r, tiles, tile, at, added, base, now_r, now_i, backward):
    lanes = slice(tile * LANES, (tile + 1) * LANES)
    chans = r.vec.shape[1] // 2
    product = r.chunks[tile, at, :]
    new_r = product * r.vec[5:6, lanes]
    new_i = product * r.vec[5:6, chans + lanes.start : chans + lanes.stop]
    if backward:
        new_i = -new_i
    return (
        new_r,
        new_i,
        new_r * now_r - new_i * now_i + added[base + tile, at, :],
        new_r * now_i + new_i * now_r + added[base + tiles + tile, at, :],
    )


def joined(r, tiles, added, base, ends, backward):
    pad = ends.shape[1]
    for tile in range(tiles):
        mul_r, mul_i = jnp.ones((pad, LANES), F32), jnp.zeros((pad, LANES), F32)
        add_r, add_i = jnp.zeros((pad, LANES), F32), jnp.zeros((pad, LANES), F32)
        for chunk in reversed(range(SUB)) if backward else range(SUB):
            at = pl.ds(chunk, pad, stride=SUB)
            new_r, new_i, add_r, add_i = chunk_step(r, tiles, tile, at, added, base, add_r, add_i, backward)
            mul_r, mul_i = mul_r * new_r - mul_i * new_i, mul_r * new_i + mul_i * new_r
        ends[tile] = mul_r
        ends[tiles + tile] = mul_i
        ends[2 * tiles + tile] = add_r
        ends[3 * tiles + tile] = add_i


def entered(r, tiles, added, base, start, entries, backward):
    pad = start.shape[1]
    for tile in range(tiles):
        now_r, now_i = start[tile], start[tiles + tile]
        for chunk in reversed(range(SUB)) if backward else range(SUB):
            at = pl.ds(chunk, pad, stride=SUB)
            entries[tile, at, :] = now_r
            entries[tiles + tile, at, :] = now_i
            _, _, now_r, now_i = chunk_step(r, tiles, tile, at, added, base, now_r, now_i, backward)


def carry_kernel(bit, first, last, backward, r):
    tiles = r.total.shape[0] // 4
    later = (lax.axis_index(N.seq) & bit) != 0
    if backward:
        later = jnp.logical_not(later)
    for tile in range(tiles):
        parts = [part * tiles + tile for part in range(4)]
        mine = tuple(r.total[part] for part in parts)
        got = tuple(r.got[part] for part in parts)
        one, zero = jnp.ones(mine[0].shape, F32), jnp.zeros(mine[0].shape, F32)
        before = (one, zero, zero, zero) if first else tuple(r.before[part] for part in parts)
        longer = combine(got, before)
        before = [jnp.where(later, new, old) for new, old in zip(longer, before)]
        if last:
            r.start[tile] = before[2]
            r.start[tiles + tile] = before[3]
        else:
            ahead = [jnp.where(later, b, a) for a, b in zip(mine, got)]
            behind = [jnp.where(later, a, b) for a, b in zip(mine, got)]
            for part, new, total in zip(parts, before, combine(ahead, behind)):
                r.before_next[part] = new
                r.total_next[part] = total


def gate_kernel(chans, r):
    tiles, rows, _ = r.gate.shape
    size = row_block(rows, 336)

    def step_of(step):
        at = rows_at(step, size)
        made = dot(r.low[at, :], r.wmix[:, 3 * chans :], 1, 0)
        for tile in range(tiles):
            r.gate[tile, at, :] = made[:, tile * LANES : (tile + 1) * LANES]

    loop(rows // size, step_of)


def hidden_back_kernel(first, name, r):
    made = getattr(r, name)
    rows, units = made.shape
    size = row_block(rows, 336)

    def step_of(step):
        at = rows_at(step, size)
        for part in range(units // 256):
            cols = slice(part * 256, (part + 1) * 256)
            weight = r.wdown[first + part * 256 : first + (part + 1) * 256, :]
            made[at, cols] = dot(r.cot[at, :], weight, 1, 1).astype(BF16)

    loop(rows // size, step_of)


def mix_kernel(shape, r):
    seqs, positions, chans = shape
    tiles = chans // LANES
    steps = positions // SUB
    rows = seqs * positions
    width = 2 * chans
    size = row_block(rows, 144)
    entered(r, tiles, r.chunks, tiles, r.start, r.entries, False)

    def scan(seq):
        for tile in range(tiles):
            lanes = slice(tile * LANES, (tile + 1) * LANES)
            cos_t, sin_t = r.vec[4:5, lanes], sine_of(r, lanes)
            at = pl.ds(pl.multiple_of(seq * SUB, SUB), SUB)
            state_r, state_i = r.entries[tile, at, :], r.entries[tiles + tile, at, :]
            for step in range(steps):
                at = pl.ds(seq * positions + step, SUB, stride=steps)
                retain = r.steps[tile, at, :]
                add_r, add_i = r.steps[tiles + tile, at, :], r.steps[2 * tiles + tile, at, :]
                mul_r, mul_i = retain * cos_t, retain * sin_t
                state_r, state_i = (
                    mul_r * state_r - mul_i * state_i + add_r,
                    mul_r * state_i + mul_i * state_r + add_i,
                )
                r.states[tile, at, :] = state_r
                r.states[tiles + tile, at, :] = state_i

    loop(seqs, scan)

    def mix(step):
        at = rows_at(step, size)
        squares = jnp.zeros((size, LANES), F32)
        for tile in range(2 * tiles):
            part = r.states[tile, at, :]
            squares = squares + part * part
        scale = lax.rsqrt(jnp.sum(squares, axis=-1, keepdims=True) / width + epsilon)
        for tile in range(2 * tiles):
            lanes = slice(tile * LANES, (tile + 1) * LANES)
            gated = r.gate[tile, at, :]
            part = r.states[tile, at, :] * scale * r.vec[1:2, lanes] * (gated * sigmoid(gated))
            r.mixed[at, lanes] = part.astype(BF16)
        total = r.tok[at, :].astype(F32) + dot(r.mixed[at, :], r.wout[...], 1, 0)
        r.after[at, :] = total
        scale = lax.rsqrt(jnp.mean(total * total, axis=-1, keepdims=True) + epsilon)
        r.ffn_low[at, :] = (total * scale * r.vec[2:3, :]).astype(BF16)

    loop(rows // size, mix)


def ffn_kernel(r):
    rows, units = r.hidden.shape
    for name in (N.after, N.mixed, N.low, N.pre, N.states, N.gate):
        r.save(getattr(r, name), getattr(r, name + N._out))
    size = row_block(rows, 336)
    wide = 256

    def step_of(step):
        at = rows_at(step, size)
        block = r.ffn_low[at, :]
        for part in range(units // wide):
            cols = slice(part * wide, (part + 1) * wide)
            later = slice(units + part * wide, units + (part + 1) * wide)
            gate = dot(block, r.wgu[:, cols], 1, 0)
            up = dot(block, r.wgu[:, later], 1, 0)
            side, at_side = (r.back0, part) if 2 * part * wide < units else (r.back1, part - units // wide // 2)
            back = side[at, at_side * wide : (at_side + 1) * wide].astype(F32)
            sigma = sigmoid(gate)
            act = gate * sigma
            r.hidden[at, cols] = (act * up).astype(BF16)
            r.grad_gu[at, cols] = (back * up * (sigma + act * (1.0 - sigma))).astype(BF16)
            r.grad_gu[at, later] = (back * act).astype(BF16)

    loop(rows // size, step_of)


def block_slots(plan):
    if not plan.in_place:
        return list(range(plan.made)), list(range(plan.made))
    seq, batch = lax.axis_index(N.seq), lax.axis_index(N.batch)
    odd = (batch & 1) == 1
    rest = plan.rest

    def place(order, seq_bits, batch_bits):
        total = 0
        for index, (axis, bit) in enumerate(order):
            value = seq_bits if axis == N.seq else batch_bits
            total = total + (((value & bit) // bit) << (len(order) - 1 - index))
        return total

    mine = [place(order, seq, batch) for order in plan.orders]
    keep, send = [], []
    for block in range(plan.blocks):
        fixed = [place(order, block // rest, (block % rest) * 2) for order in plan.orders]
        first, second = fixed[0] ^ mine[0], fixed[1] ^ mine[1]
        keep.append(jnp.where(odd, second, first))
        send.append(jnp.where(odd, first, second))
    return keep, send


def store_blocks(ref, slots, size, cols, values, base=0):
    for block, slot in enumerate(slots):
        at = base + slot * size if isinstance(slot, int) else pl.multiple_of(base + slot * size, SUB)
        ref[pl.ds(at, size), cols] = values[block * size : (block + 1) * size, :]


def grad_narrow_kernel(plan, left, right, keep, send, r):
    left, right, keep, send = (getattr(r, name) for name in (left, right, keep, send))
    mine = lax.axis_index(N.batch) & 1
    kept, sent = block_slots(plan)
    half = right.shape[1] // 2
    r.turned[:, :half] = right[:, pl.ds(pl.multiple_of(mine * half, LANES), half)]
    r.turned[:, half:] = right[:, pl.ds(pl.multiple_of((1 - mine) * half, LANES), half)]
    size = left.shape[1] // plan.made
    tall = min(left.shape[1], 384)
    cols = slice(0, half)
    count = tall // size
    for part in range(left.shape[1] // tall):
        made = dot(left[:, part * tall : (part + 1) * tall], r.turned[...], 0, 0)
        there = slice(part * count, (part + 1) * count)
        store_blocks(keep, kept[there], size, cols, made[:, :half])
        store_blocks(send, sent[there], size, cols, made[:, half:])


def grad_wide_kernel(plan, left, right, made_name, sending, wide, r):
    left, right, out = getattr(r, left), getattr(r, right), getattr(r, made_name)
    mine = lax.axis_index(N.batch) & 1
    owner = 1 - mine if sending else mine
    slots = block_slots(plan)[1 if sending else 0]
    half = right.shape[1] // 2
    size = left.shape[1] // plan.made

    def step_of(part):
        cols = pl.ds(pl.multiple_of(part * wide, LANES), wide)
        source = pl.ds(pl.multiple_of(owner * half + part * wide, LANES), wide)
        store_blocks(out, slots, size, cols, dot(left[...], right[:, source], 0, 0))

    loop(half // wide, step_of)


def fold_kernel(names, head, r):
    keep, got = getattr(r, names[0]), r.got
    send_next, keep_next = getattr(r, names[1]), getattr(r, names[2])
    half = (keep.shape[0] - head) // 2
    send_next[head:, :] = keep[head + half :, :] + got[head + half :, :]
    keep_next[head:, :] = keep[head : head + half, :] + got[head : head + half, :]
    if head:
        both = keep[:head, :] + got[:head, :]
        send_next[:head, :] = both
        keep_next[:head, :] = both


def fold_first_kernel(parts, head, pieces, names, r):
    send_next, keep_next = getattr(r, names[0]), getattr(r, names[1])
    start = 0
    for part in parts:
        keep = getattr(r, N.keep_ + part)
        rows = keep.shape[0] - head
        half = rows // 2
        cols = slice(start, start + keep.shape[1])
        start = cols.stop
        count = max(pieces, 2)
        size = rows // count
        for piece in range(count):
            at = piece * size
            if pieces == 1:
                got = getattr(r, "got_%s0" % part)[head + at : head + at + size, :]
            else:
                first = head if piece == 0 else 0
                got = getattr(r, "got_%s%d" % (part, piece))[first : first + size, :]
            value = keep[head + at : head + at + size, :] + got
            if at < half:
                keep_next[head + at : head + at + size, cols] = value
            else:
                send_next[head + at - half : head + at - half + size, cols] = value
        if head:
            both = keep[:head, :] + getattr(r, "got_%s0" % part)[:head, :]
            send_next[:head, cols] = both
            keep_next[:head, cols] = both


def sum_kernel(name, r):
    r.total[...] = getattr(r, name)[...] + r.got[...]


def fold_pair_kernel(slots, r):
    per, wide = r.keep_down.shape[0] // slots, r.keep_down.shape[1]
    rows = r.keep_third.shape[0] // slots
    for slot in range(slots):
        out = r.later_pair if 2 * slot < slots else r.send_pair
        to = slot % (slots // 2) * per
        at = slice(slot * per, (slot + 1) * per)
        out[to : to + per, :wide] = r.keep_down[at, :] + r.got_down[at, :]
        at = slice(slot * rows, (slot + 1) * rows)
        value = r.keep_third[at, :] + r.got_third[at, :]
        out[to : to + rows, wide:] = value[:, :wide]
        out[to + rows : to + per, wide:] = value[:, wide:]


def pack_kernel(r):
    rows, wide = r.packed.shape[0], r.keep_pair.shape[1] // 2
    total = r.keep_pair[...] + r.got[...]
    r.packed[:, :wide] = total[:rows, wide:]
    r.packed[:, wide : 2 * wide] = total[rows:, wide:]
    r.packed[:, 2 * wide : 3 * wide] = total[:rows, :wide]
    r.packed[:, 3 * wide :] = total[rows:, :wide]


def stack_kernel(axis, bit, r):
    upper = (lax.axis_index(axis) & bit) != 0
    start = 0
    for mine, got in ((r.first, r.first_got), (r.second, r.second_got)):
        rows, wide = mine.shape
        cols = slice(start, start + wide)
        start = cols.stop
        r.both[:rows, cols] = jnp.where(upper, got[...], mine[...])
        r.both[rows:, cols] = jnp.where(upper, mine[...], got[...])


def stack_head_kernel(axis, bit, head, r):
    upper = (lax.axis_index(axis) & bit) != 0
    rows = r.mine.shape[0]
    r.both[:head, :] = r.mine[:head, :]
    r.both[head:rows, :] = jnp.where(upper, r.got[head:, :], r.mine[head:, :])
    r.both[rows:, :] = jnp.where(upper, r.mine[head:, :], r.got[head:, :])


def unpack_kernel(parts, r):
    upper = (lax.axis_index(N.batch) & 1) != 0
    units, width = r.grad_down.shape[0], r.grad_down.shape[1]
    half = width // 2
    rows = r.mine.shape[0]
    wide = r.grad_wide.shape[1] // 2
    size = rows // parts

    def sides(at, cols):
        mine, got = r.mine[at, cols], r.got[at, cols]
        return jnp.where(upper, got, mine), jnp.where(upper, mine, got)

    every = slice(0, rows)
    r.grad_wide[:, :wide], r.grad_wide[:, wide:] = sides(every, slice(0, wide))
    r.grad_out[:, :half], r.grad_out[:, half:] = sides(every, slice(wide, wide + half))
    r.gate_part[:, :half], r.gate_part[:, half:] = sides(every, slice(wide + half, wide + 2 * half))
    base = wide + 2 * half
    per = units // rows
    for part in range(parts):
        for piece in range(per):
            at = slice(part * size, (part + 1) * size)
            to = slice((part * per + piece) * size, (part * per + piece + 1) * size)
            first, second = sides(at, slice(base + piece * half, base + (piece + 1) * half))
            r.grad_down[to, :half] = first
            r.grad_down[to, half:] = second


def finish_kernel(r):
    upper = (lax.axis_index(N.batch) & 1) != 0
    wide = r.mine.shape[1]
    first = jnp.where(upper, r.got[SUB:, :], r.mine[SUB:, :])
    second = jnp.where(upper, r.mine[SUB:, :], r.got[SUB:, :])
    gate = r.gate_part.shape[1]
    scan = r.grad_mix.shape[1] - gate
    r.grad_mix[:, :wide] = first
    r.grad_mix[:, wide:scan] = second[:, 2 * wide - scan :]
    r.grad_mix[:, scan:] = r.gate_part[...]
    index = 0
    for name in (N.vec_in, N.vec_out, N.vec_ffn, N.vec_lower, N.vec_fbias, N.vec_phase):
        ref = getattr(r, name)
        for tile in range(ref.shape[0] // LANES):
            rows, lanes = sum_place(wide, index)
            ref[tile * LANES : (tile + 1) * LANES] = r.mine[rows, lanes].reshape(LANES)
            index += 1


def ffn_back_kernel(r):
    rows, width = r.after.shape
    size = row_block(rows, 336)
    r.sums_ffn[...] = jnp.zeros(r.sums_ffn.shape, F32)

    def ffn_back(step):
        at = rows_at(step, size)
        back = dot(r.grad_gu[at, :], r.wgu[...], 1, 1)
        total = r.after[at, :]
        scale = lax.rsqrt(jnp.mean(total * total, axis=-1, keepdims=True) + epsilon)
        normed = total * scale
        r.sums_ffn[...] += fold_rows(back * normed)
        scaled = back * r.vec[2:3, :]
        shared = jnp.mean(scaled * normed, axis=-1, keepdims=True)
        made = r.cot[at, :].astype(F32) + scale * (scaled - normed * shared)
        r.grad_mid[at, :] = made
        r.grad_mid_low[at, :] = made.astype(BF16)

    loop(rows // size, ffn_back)


def mix_back_kernel(shape, r):
    seqs, positions, chans = shape
    tiles = chans // LANES
    steps = positions // SUB
    rows = seqs * positions
    width = 2 * chans
    small = row_block(rows, 144)
    r.sums_out[...] = jnp.zeros(r.sums_out.shape, F32)

    def mix_back(step):
        at = rows_at(step, small)
        back = dot(r.grad_mid_low[at, :], r.wout[...], 1, 1)
        squares = jnp.zeros((small, LANES), F32)
        for tile in range(2 * tiles):
            part = r.states[tile, at, :]
            squares = squares + part * part
        scale = lax.rsqrt(jnp.sum(squares, axis=-1, keepdims=True) / width + epsilon)
        shared = jnp.zeros((small, LANES), F32)
        for tile in range(2 * tiles):
            lanes = slice(tile * LANES, (tile + 1) * LANES)
            gated = r.gate[tile, at, :]
            sigma = sigmoid(gated)
            act = gated * sigma
            normed = r.states[tile, at, :] * scale
            part = back[:, lanes]
            gain = r.vec[1:2, lanes]
            r.grad_gate[at, lanes] = (part * normed * gain * (sigma + act * (1.0 - sigma))).astype(BF16)
            inner = part * act
            product = inner * normed
            r.sums_out[:, lanes] += fold_rows(product)
            shared = shared + product * gain
            r.seeds[tile, at, :] = inner * gain
        mean = jnp.sum(shared, axis=-1, keepdims=True) / width
        for tile in range(2 * tiles):
            normed = r.states[tile, at, :] * scale
            r.seeds[tile, at, :] = scale * (r.seeds[tile, at, :] - normed * mean)

    loop(rows // small, mix_back)

    def scan(seq):
        for tile in range(tiles):
            lanes = slice(tile * LANES, (tile + 1) * LANES)
            low_bound, cos_t, sin_t = r.vec[3:4, lanes], r.vec[4:5, lanes], sine_of(r, lanes)
            flow_r = jnp.zeros((SUB, LANES), F32)
            flow_i = jnp.zeros((SUB, LANES), F32)
            for step in reversed(range(steps)):
                at = pl.ds(seq * positions + step, SUB, stride=steps)
                _, _, _, retain = forget_gate(r.pre[2 * tiles + tile, at, :], low_bound)
                mul_r, mul_i = retain * cos_t, retain * sin_t
                adj_r = r.seeds[tile, at, :] + flow_r
                adj_i = r.seeds[tiles + tile, at, :] + flow_i
                flow_r = mul_r * adj_r + mul_i * adj_i
                flow_i = mul_r * adj_i - mul_i * adj_r
            at = pl.ds(pl.multiple_of(seq * SUB, SUB), SUB)
            r.chunks_back[tile, at, :] = flow_r
            r.chunks_back[tiles + tile, at, :] = flow_i

    r.chunks_back[...] = jnp.zeros(r.chunks_back.shape, F32)
    loop(seqs, scan)
    pad = r.ends_back.shape[2]
    for tile in range(tiles):
        product = jnp.ones((pad, LANES), F32)
        add_r, add_i = jnp.zeros((pad, LANES), F32), jnp.zeros((pad, LANES), F32)
        for chunk in reversed(range(SUB)):
            at = pl.ds(chunk, pad, stride=SUB)
            product = product * r.chunks[tile, at, :]
            _, _, add_r, add_i = chunk_step(r, tiles, tile, at, r.chunks_back, 0, add_r, add_i, True)
        r.ends_back[0, tile] = product
        r.ends_back[0, tiles + tile] = add_r
        r.ends_back[0, 2 * tiles + tile] = add_i


def append_kernel(r):
    count = r.have.shape[0]
    r.both[:count] = r.have[...]
    r.both[count:] = r.got[...]


def enter_kernel(bits, r):
    mine = lax.axis_index(N.seq)
    count = r.have.shape[0]
    tiles = r.have.shape[1] // 3
    r.both[:count] = r.have[...]
    r.both[count:] = r.got[...]
    for tile in range(tiles):
        lanes = slice(tile * LANES, (tile + 1) * LANES)
        chans = r.vec.shape[1] // 2
        turn_r = r.vec[6:7, lanes]
        turn_i = r.vec[6:7, chans + lanes.start : chans + lanes.stop]
        now_r = jnp.zeros(r.have.shape[2:], F32)
        now_i = jnp.zeros(r.have.shape[2:], F32)
        for other in reversed(range(1, 2 * count)):
            index = 0
            for place, bit in enumerate(bits):
                index = index + ((((mine ^ other) & bit) // bit) << place)
            product = r.both[index, tile]
            mul_r, mul_i = product * turn_r, product * turn_i
            next_r = mul_r * now_r + mul_i * now_i + r.both[index, tiles + tile]
            next_i = mul_r * now_i - mul_i * now_r + r.both[index, 2 * tiles + tile]
            now_r = jnp.where(other > mine, next_r, now_r)
            now_i = jnp.where(other > mine, next_i, now_i)
        r.start[tile] = now_r
        r.start[tiles + tile] = now_i


def scan_back_kernel(shape, r):
    seqs, positions, chans = shape
    tiles = chans // LANES
    steps = positions // SUB
    entered(r, tiles, r.chunks_back, 0, r.start, r.entries_back, True)
    r.sums_scan[...] = jnp.zeros(r.sums_scan.shape, F32)
    mine = lax.axis_index(N.batch) & 1
    half = r.turned.shape[1] // 2
    shift = 3 * chans - half
    keep_at = pl.ds(pl.multiple_of(mine * shift, LANES), half)
    send_at = pl.ds(pl.multiple_of((1 - mine) * shift, LANES), half)

    def scan(seq):
        for tile in range(tiles):
            lanes = slice(tile * LANES, (tile + 1) * LANES)
            low_bound, cos_t, sin_t = r.vec[3:4, lanes], r.vec[4:5, lanes], sine_of(r, lanes)
            chunk_at = pl.ds(pl.multiple_of(seq * SUB, SUB), SUB)
            flow_r, flow_i = r.entries_back[tile, chunk_at, :], r.entries_back[tiles + tile, chunk_at, :]
            sum_lower = jnp.zeros((SUB, LANES), F32)
            sum_fbias = jnp.zeros((SUB, LANES), F32)
            sum_phase = jnp.zeros((SUB, LANES), F32)
            for step in reversed(range(steps)):
                at = pl.ds(seq * positions + step, SUB, stride=steps)
                in_r, in_i = r.pre[tile, at, :], r.pre[tiles + tile, at, :]
                opened, shut, intake, retain = forget_gate(r.pre[2 * tiles + tile, at, :], low_bound)
                sig_r, sig_i = sigmoid(in_r), sigmoid(in_i)
                act_r, act_i = in_r * sig_r, in_i * sig_i
                adj_r = r.seeds[tile, at, :] + flow_r
                adj_i = r.seeds[tiles + tile, at, :] + flow_i
                mul_r, mul_i = retain * cos_t, retain * sin_t
                flow_r = mul_r * adj_r + mul_i * adj_i
                flow_i = mul_r * adj_i - mul_i * adj_r
                if step > 0:
                    before = pl.ds(seq * positions + step - 1, SUB, stride=steps)
                    past_r, past_i = r.states[tile, before, :], r.states[tiles + tile, before, :]
                else:
                    past_r, past_i = r.entries[tile, chunk_at, :], r.entries[tiles + tile, chunk_at, :]
                grad_r = adj_r * past_r + adj_i * past_i
                grad_i = adj_i * past_r - adj_r * past_i
                grad_retain = grad_r * cos_t + grad_i * sin_t - (adj_r * act_r + adj_i * act_i)
                sum_phase = sum_phase + retain * (grad_i * cos_t - grad_r * sin_t)
                sum_lower = sum_lower + grad_retain * shut
                grad_forget = grad_retain * intake * opened
                sum_fbias = sum_fbias + grad_forget
                at = pl.ds(step, SUB, stride=steps)
                r.made_pre[tile, at, :] = adj_r * intake * (sig_r + act_r * (1.0 - sig_r))
                r.made_pre[tiles + tile, at, :] = adj_i * intake * (sig_i + act_i * (1.0 - sig_i))
                r.made_pre[2 * tiles + tile, at, :] = grad_forget
            r.sums_scan[0:SUB, lanes] += sum_lower
            r.sums_scan[SUB : 2 * SUB, lanes] += sum_fbias
            r.sums_scan[2 * SUB : 3 * SUB, lanes] += sum_phase
        seq_rows = rows_at(seq, positions)
        for tile in range(3 * tiles):
            r.grad_pre[seq_rows, tile * LANES : (tile + 1) * LANES] = r.made_pre[tile].astype(BF16)
        r.turned[seq_rows, :half] = r.grad_pre[seq_rows, keep_at]
        r.turned[seq_rows, half:] = r.grad_pre[seq_rows, send_at]

    loop(seqs, scan)


def grad_scan_kernel(plan, chans, r):
    kept, sent = block_slots(plan)
    half = r.turned.shape[1] // 2
    size = r.low.shape[1] // plan.made
    tall = min(r.low.shape[1], 384)
    count = tall // size
    for part in range(r.low.shape[1] // tall):
        made = dot(r.low[:, part * tall : (part + 1) * tall], r.turned[...], 0, 0)
        there = slice(part * count, (part + 1) * count)
        store_blocks(r.keep_scan, kept[there], size, slice(0, half), made[:, :half], SUB)
        store_blocks(r.made, sent[there], size, slice(0, half), made[:, half:])
    zero = jnp.zeros((SUB, half), F32)
    r.keep_scan[0:SUB, :] = zero
    index = 0
    for source in (r.sums_in, r.sums_out, r.sums_ffn):
        for tile in range(source.shape[1] // LANES):
            total = jnp.sum(source[:, tile * LANES : (tile + 1) * LANES], axis=0, keepdims=True)
            put_sum(r.keep_scan, index, total)
            index += 1
    for part in range(3):
        for tile in range(chans // LANES):
            block = r.sums_scan[part * SUB : (part + 1) * SUB, tile * LANES : (tile + 1) * LANES]
            put_sum(r.keep_scan, index, jnp.sum(block, axis=0, keepdims=True))
            index += 1
    rows = r.made.shape[0] // PIECES
    r.send_scan0[0:SUB, :] = r.keep_scan[0:SUB, :]
    r.send_scan0[SUB:, :] = r.made[:rows, :]
    for piece in range(1, PIECES):
        getattr(r, "send_scan%d" % piece)[...] = r.made[piece * rows : (piece + 1) * rows, :]


def sum_place(wide, index):
    row, tile = divmod(index, wide // LANES)
    return slice(row, row + 1), slice(tile * LANES, (tile + 1) * LANES)


def put_sum(ref, index, total):
    rows, lanes = sum_place(ref.shape[1], index)
    ref[rows, lanes] = total


def input_back_kernel(r):
    rows, chans3 = r.grad_pre.shape
    size = row_block(rows, 336)
    r.sums_in[...] = jnp.zeros(r.sums_in.shape, F32)

    for step in range(rows // size):
        at = pl.ds(step * size, size)
        back = dot(r.grad_pre[at, :], r.wmix[:, :chans3], 1, 1)
        back = back + dot(r.grad_gate[at, :], r.wmix[:, chans3:], 1, 1)
        inputs = r.tok[at, :].astype(F32)
        scale = lax.rsqrt(jnp.mean(inputs * inputs, axis=-1, keepdims=True) + epsilon)
        normed = inputs * scale
        r.sums_in[...] += fold_rows(back * normed)
        scaled = back * r.vec[0:1, :]
        shared = jnp.mean(scaled * normed, axis=-1, keepdims=True)
        r.made[at, :] = r.grad_mid[at, :] + scale * (scaled - normed * shared)
        r.save(r.made.at[at, :], r.grad_tokens.at[at, :])


def output_kernel(count, r):
    rows, _ = r.output.shape
    r.mark[...] = jnp.zeros(r.mark.shape, F32)
    size = rows // count
    r.wait(N.wdown_in)
    for step in range(count):
        at = pl.ds(step * size, size)
        for name in (N.after_in, N.hidden_in):
            r.wait(name + str(step))
        made = dot(getattr(r, N.hidden_in + str(step))[...], r.wdown_in[...], 1, 0)
        r.made[at, :] = (getattr(r, N.after_in + str(step))[...] + made).astype(BF16)
        r.save(r.made.at[at, :], r.output.at[at, :])


def run(pool, kernel, name, new=(), args=None, fetch=None, load=None, out=(), drop=(), reuse=None, scratch=None, vmem=5, after=(), late=()):
    args, fetch, load, reuse, scratch = args or {}, fetch or {}, load or {}, reuse or {}, scratch or {}
    whole = {key: value for key, value in load.items() if not isinstance(value, tuple)}
    scratch = {**scratch, **{key: pltpu.VMEM(value.shape, value.dtype) for key, value in whole.items()}}
    parts = {key: value for key, value in load.items() if isinstance(value, tuple)}
    load = {key: value for key, value in load.items() if key not in parts}
    incoming = {**fetch, **load}
    for key, (value, count) in parts.items():
        rows = value.shape[0] // count
        for part in range(count):
            scratch[key + str(part)] = pltpu.VMEM((rows,) + value.shape[1:], value.dtype)
    kept = [key for key in pool if key not in drop]
    dropped = [key for key in pool if key in drop]
    new_names = [item[0] for item in new]
    operands = [pool[key] for key in kept + dropped]
    operands += [pltpu.with_memory_space_constraint(value, pltpu.VMEM) for value in args.values()]
    operands += [pltpu.with_memory_space_constraint(value, pltpu.HBM) for value in incoming.values()]
    in_names = kept + dropped + list(args) + ["hbm " + key for key in incoming] + ["after%d" % index for index in range(len(after))]
    operands += list(after)
    in_names += ["hbm " + key for key in parts]
    operands += [pltpu.with_memory_space_constraint(value, pltpu.HBM) for value, _ in parts.values()]
    shapes = [pltpu.VMEM(pool[key].shape, pool[key].dtype) for key in kept]
    shapes += [pltpu.VMEM(shape, kind) for _, shape, kind in new]
    shapes += [pltpu.VMEM(value.shape, value.dtype) for value in fetch.values()]
    shapes += [pltpu.HBM(shape, kind) for _, shape, kind in out]
    out_names = ["out " + key for key in kept] + new_names + list(fetch) + [item[0] for item in out]
    aliases = {index: index for index in range(len(kept))}
    for key, old in reuse.items():
        aliases[in_names.index(old)] = out_names.index(key)
    copies = len(incoming) + sum(count for _, count in parts.values()) + len(out) + 8

    def body(*refs):
        r = types.SimpleNamespace(**dict(zip(in_names + out_names + list(scratch), refs)))
        sems = refs[-1]
        waiting = {}
        for index, key in enumerate(incoming):
            copy = pltpu.make_async_copy(getattr(r, "hbm " + key), getattr(r, key), sems.at[index])
            if key not in late:
                copy.start()
            waiting[key] = copy

        index = len(incoming)
        for part in range(max([count for _, count in parts.values()], default=0)):
            for key, (value, count) in parts.items():
                rows = value.shape[0] // count
                source = getattr(r, "hbm " + key).at[pl.ds(part * rows, rows), :]
                copy = pltpu.make_async_copy(source, getattr(r, key + str(part)), sems.at[index])
                copy.start()
                waiting[key + str(part)] = copy
                index += 1
        taken = index

        def save(source, target):
            index = taken + len([key for key in waiting if key.startswith("save ")])
            copy = pltpu.make_async_copy(source, target, sems.at[index])
            copy.start()
            waiting["save " + str(index)] = copy

        r.wait = lambda key: waiting.pop(key).wait()
        r.save = save
        r.start_late = lambda: [waiting[key].start() for key in late]
        kernel(r)
        for copy in waiting.values():
            copy.wait()

    made = pl.pallas_call(
        body,
        out_shape=shapes,
        in_specs=[pl.BlockSpec(memory_space=pltpu.VMEM)] * (len(kept) + len(dropped) + len(args))
        + [pl.BlockSpec(memory_space=pltpu.HBM)] * len(incoming)
        + [pl.BlockSpec(memory_space=pl.ANY)] * len(after)
        + [pl.BlockSpec(memory_space=pltpu.HBM)] * len(parts),
        out_specs=[pl.BlockSpec(memory_space=pl.ANY)] * len(kept)
        + [pl.BlockSpec(memory_space=pltpu.VMEM)] * (len(new) + len(fetch))
        + [pl.BlockSpec(memory_space=pltpu.HBM)] * len(out),
        scratch_shapes=list(scratch.values()) + [pltpu.SemaphoreType.DMA((copies,))],
        input_output_aliases=aliases,
        compiler_params=pltpu.CompilerParams(vmem_limit_bytes=vmem * MIB),
        cost_estimate=pl.CostEstimate(flops=int(SCALE * TIME.get(name, FOLD if name.startswith(N.fold) else 0.3) * 1.15e9), bytes_accessed=0, transcendentals=0),
        name=name,
    )(*operands)
    pool.clear()
    count = len(kept) + len(new) + len(fetch)
    pool.update(zip(kept + new_names + list(fetch), made[:count]))
    return made[count:]


def combine(earlier, later_part):
    mul_r, mul_i, add_r, add_i = earlier
    new_r, new_i, plus_r, plus_i = later_part
    out_mr = mul_r * new_r - mul_i * new_i
    out_mi = mul_r * new_i + mul_i * new_r
    out_ar = new_r * add_r - new_i * add_i + plus_r
    out_ai = new_r * add_i + new_i * add_r + plus_i
    return (out_mr, out_mi, out_ar, out_ai)


def across(value, axis, bit):
    size = lax.axis_size(axis)
    return lax.ppermute(value, axis, [(at, at ^ bit) for at in range(size)])


def across_by_core(value, dims):
    seq_size, batch_size = lax.axis_size(N.seq), lax.axis_size(N.batch)
    pairs = []
    for seq in range(seq_size):
        for batch in range(batch_size):
            axis, bit = dims[batch & 1]
            to = (seq ^ bit, batch) if axis == N.seq else (seq, batch ^ bit)
            pairs.append((seq * batch_size + batch, to[0] * batch_size + to[1]))
    return lax.ppermute(value, (N.seq, N.batch), pairs)


def make_plan(seq_size, batch_size, width, kind):
    along_seq = [(N.seq, 1 << bit) for bit in range(seq_size.bit_length() - 1)]
    along_batch = [(N.batch, 1 << bit) for bit in range(1, batch_size.bit_length() - 1)]
    near, next_bit, far = along_seq[:1], along_seq[1:2], along_seq[2:]
    rest = batch_size // 2
    places = {"y": near, "z": next_bit, "w": far, "x": along_batch}
    orders = tuple(sum((places[letter] for letter in order), []) for order in ORDERS[kind])
    blocks = seq_size * rest
    in_place = width % (blocks * SUB) == 0
    return types.SimpleNamespace(
        seq_size=seq_size, batch_size=batch_size, orders=orders, blocks=blocks, in_place=in_place, rest=rest,
        made=blocks if in_place else 2 * SUB, steps=list(zip(*orders)),
    )


class Chunk:
    def __init__(self, pool, plan, name, parts=None, head=0):
        self.pool, self.plan, self.name, self.head, self.done = pool, plan, name, head, 0
        self.parts, self.got = parts or (name,), {}

    def begin(self, part=None):
        part = part or self.name
        names = [key for key in self.pool if key.startswith(N.send_ + part)]
        sent = [self.pool.pop(key) for key in names]
        if not self.plan.in_place:
            sent = [self.arranged(jnp.concatenate(sent, axis=0), 1)]
            self.pool[N.keep_ + part] = self.arranged(self.pool[N.keep_ + part], 0)
        for piece, value in enumerate(sent):
            self.got["got_%s%d" % (part, piece)] = across(value, N.batch, 1)

    def arranged(self, values, side):
        seq, batch = lax.axis_index(N.seq), lax.axis_index(N.batch)
        rest = self.plan.rest
        block = np.arange(self.plan.blocks)
        found = []
        for order in self.plan.orders:
            slots = jnp.zeros(block.shape, jnp.int32)
            for place, (axis, bit) in enumerate(order):
                fixed = block // rest if axis == N.seq else (block % rest) * 2
                mine = seq if axis == N.seq else batch
                flag = (((jnp.asarray(fixed, jnp.int32) ^ mine) & bit) != 0).astype(jnp.int32)
                slots = slots + (flag << (len(order) - 1 - place))
            found.append(slots)
        odd = (batch & 1) == 1
        slots = jnp.where(odd, found[1 - side], found[side])
        body = values[self.head :]
        cut = body.reshape((self.plan.blocks, -1) + body.shape[1:])
        body = jnp.take(cut, jnp.argsort(slots), axis=0).reshape(body.shape)
        return jnp.concatenate([values[: self.head], body], axis=0) if self.head else body

    def apart(self):
        names = [N.keep_ + part for part in self.parts] if self.done == 0 else [N.keep_ + self.name]
        self.pool = {name: self.pool.pop(name) for name in names}

    def fold(self, after=()):
        keep, head = N.keep_ + self.name, self.head
        send, later = N.send_ + self.name, N.later_ + self.name
        names = [N.keep_ + part for part in self.parts] if self.done == 0 else [keep]
        rows, cols = self.pool[names[0]].shape[0], sum(self.pool[name].shape[1] for name in names)
        half = (rows - head) // 2
        if half % SUB == 0:
            if self.done == 0:
                pieces = len(self.got) // len(self.parts)
                kernel = functools.partial(fold_first_kernel, self.parts, head, pieces, (send, later))
            else:
                kernel = functools.partial(fold_kernel, (keep, send, later), head)
            run(
                self.pool, kernel, N.fold_ + self.name,
                new=[(send, (head + half, cols), F32), (later, (head + half, cols), F32)], args=self.got, drop=tuple(names),
                vmem=6 if self.plan.in_place else 24, after=after,
            )
            self.pool[keep] = self.pool.pop(later)
            self.sent = self.pool.pop(send)
        else:
            values = [self.pool.pop(name) + got for name, got in zip(names, self.got.values())]
            value = jnp.concatenate(values, axis=1)
            self.sent = jnp.concatenate([value[:head], value[head + half :]], axis=0)
            self.pool[keep] = value[: head + half]

    def send(self):
        self.got = {N.got: across_by_core(self.sent, self.plan.steps[self.done])}
        self.done += 1

    def step(self, after=()):
        self.fold(after)
        self.send()

    def whole(self, after=()):
        run(
            self.pool, functools.partial(sum_kernel, N.keep_ + self.name), N.sum_ + self.name,
            new=[(N.total, self.pool[N.keep_ + self.name].shape, F32)], args=self.got, drop=(N.keep_ + self.name,), after=after,
        )
        return self.pool.pop(N.total)


def carry(pool, total, between):
    size = lax.axis_size(N.seq)
    hops = size.bit_length() - 1
    sent = pool.pop(total)
    for hop in range(hops):
        first, last = hop == 0, hop == hops - 1
        got = across(sent, N.seq, 1 << hop)
        between(hop)
        shape = sent.shape
        if last:
            new = [(N.start, (shape[0] // 2,) + shape[1:], F32)]
        else:
            new = [(N.before_next, shape, F32), (N.total_next, shape, F32)]
        run(
            pool, functools.partial(carry_kernel, 1 << hop, first, last, False), N.carry,
            new=new, args={N.got: got, N.total: sent}, drop=(N.before,),
        )
        if not last:
            sent = pool.pop(N.total_next)
            pool[N.before] = pool.pop(N.before_next)


def carry_back(pool, name, between):
    size = lax.axis_size(N.seq)
    order = [HOPS[place] for place in range(3) if HOPS[place] < size.bit_length() - 1] + list(range(3, size.bit_length() - 1))
    bits = [1 << hop for hop in order]
    sent = pool.pop(name)
    for hop, bit in enumerate(bits):
        got = across(sent, N.seq, bit)
        between(hop)
        shape = sent.shape
        if hop < len(bits) - 1:
            run(pool, append_kernel, N.append, new=[(N.both, (2 * shape[0],) + shape[1:], F32)], args={N.have: sent, N.got: got})
            sent = pool.pop(N.both)
        else:
            run(
                pool, functools.partial(enter_kernel, bits), N.enter,
                new=[(N.start, (2 * shape[1] // 3,) + shape[2:], F32)], args={N.have: sent, N.got: got},
                scratch={N.both: pltpu.VMEM((2 * shape[0],) + shape[1:], F32)},
            )


def per_device(
    tokens, cotangent, gain_in, w_mix, lower, fbias, phase, gain_out, w_out, gain_ffn, w_gu, w_down
):
    seqs, positions, width = tokens.shape
    chans = lower.shape[0]
    units = w_down.shape[0]
    rows = seqs * positions
    tiles = chans // LANES
    shape = (seqs, positions, chans)
    pad = -(-seqs // SUB) * SUB
    seq_size, batch_size = lax.axis_size(N.seq), lax.axis_size(N.batch)
    tokens = tokens.reshape(rows, width)
    cotangent = cotangent.reshape(rows, width)
    wide_plan, down_plan, scan_plan = (
        make_plan(seq_size, batch_size, width, kind) for kind in (N.wide, N.down, N.scan)
    )
    pool = {}
    raw = {N.raw_in: gain_in, N.raw_lower: lower, N.raw_fbias: fbias, N.raw_phase: phase, N.raw_out: gain_out, N.raw_ffn: gain_ffn}
    run(
        pool, functools.partial(project_kernel, shape), N.project,
        new=[(N.vec, (SUB, width), F32), (N.low, (rows, width), BF16), (N.pre, (3 * tiles, rows, LANES), F32), (N.steps, (3 * tiles, rows, LANES), F32),
             (N.chunks, (3 * tiles, pad * SUB, LANES), F32), (N.ends, (4 * tiles, pad, LANES), F32)],
        fetch={N.tok: tokens, N.wmix: w_mix, N.wdown: w_down, N.cot: cotangent}, load=raw, late=(N.wdown, N.cot),
    )

    def between(hop):
        if hop == 0:
            run(
                pool, functools.partial(gate_kernel, chans), N.gate, new=[(N.gate, (2 * tiles, rows, LANES), F32)],
                fetch={N.wout: w_out}, drop=(N.wmix,),
            )
        elif hop <= 2:
            run(
                pool, functools.partial(hidden_back_kernel, (hop - 1) * units // 2, "back%d" % (hop - 1)), N.hidden_back,
                new=[("back%d" % (hop - 1), (rows, units // 2), BF16)], drop=(N.wdown,) if hop == 2 else (),
            )

    carry(pool, N.ends, between)
    run(
        pool, functools.partial(mix_kernel, shape), N.mix,
        new=[(N.states, (2 * tiles, rows, LANES), F32), (N.entries, (2 * tiles, pad * SUB, LANES), F32),
             (N.mixed, (rows, width), BF16), (N.after, (rows, width), F32), (N.ffn_low, (rows, width), BF16)],
        fetch={N.wgu: w_gu}, drop=(N.start, N.wout, N.tok, N.steps),
    )
    away = (N.after, N.mixed, N.low, N.pre, N.states, N.gate)
    kinds = [(key + N._out, pool[key].shape, pool[key].dtype) for key in away]
    stored = run(
        pool, ffn_kernel, N.ffn, new=[(N.hidden, (rows, units), BF16), (N.grad_gu, (rows, 2 * units), BF16)],
        out=kinds, drop=(N.back0, N.back1) + away[1:],
    )
    stored = dict(zip(away, stored))
    wide, down = Chunk(pool, wide_plan, N.wide), Chunk(pool, down_plan, N.down)
    for side, sending in ((N.send_wide, True), (N.keep_wide, False)):
        run(
            pool, functools.partial(grad_wide_kernel, wide_plan, N.ffn_low, N.grad_gu, side, sending, 512), N.grad_gu,
            new=[(side, (width, units), F32)], drop=() if sending else (N.ffn_low,),
        )
        if sending:
            sent = pool.pop(N.send_wide)
    pool[N.send_wide] = sent
    wide.begin()
    (hidden_out,) = run(
        pool, lambda r: (r.save(r.hidden, r.hidden_out),
                         grad_narrow_kernel(down_plan, N.hidden, N.cot, N.keep_down, N.send_down, r)), N.grad_down,
        new=[(N.keep_down, (units, width // 2), F32), (N.send_down, (units, width // 2), F32)],
        out=[(N.hidden_out, (rows, units), BF16)], drop=(N.hidden,),
        scratch={N.turned: pltpu.VMEM((rows, width), BF16)},
    )
    down.begin()
    wide.step()
    run(
        pool, ffn_back_kernel, N.ffn_back,
        new=[(N.grad_mid, (rows, width), F32), (N.grad_mid_low, (rows, width), BF16), (N.sums_ffn, (SUB, width), F32)],
        fetch={N.states: stored[N.states], N.gate: stored[N.gate], N.wout: w_out, N.pre: stored[N.pre]},
        drop=(N.grad_gu, N.wgu, N.after, N.cot), reuse={N.grad_mid: N.after},
    )
    down.step()
    run(
        pool, functools.partial(mix_back_kernel, shape), N.mix_back,
        new=[(N.grad_gate, (rows, width), BF16), (N.seeds, (2 * tiles, rows, LANES), F32),
             (N.chunks_back, (2 * tiles, pad * SUB, LANES), F32), (N.ends_back, (1, 3 * tiles, pad, LANES), F32),
             (N.sums_out, (SUB, width), F32)],
        fetch={N.low: stored[N.low], N.mixed: stored[N.mixed]}, drop=(N.gate, N.wout), reuse={N.seeds: N.gate},
    )
    half = width // 2
    turned = {N.turned: pltpu.VMEM((rows, width), BF16)}
    third = Chunk(pool, down_plan, N.third, (N.out, N.gates))
    hops = seq_size.bit_length() - 1

    def between(hop):
        if hop == 0:
            run(
                pool, functools.partial(grad_narrow_kernel, down_plan, N.mixed, N.grad_mid_low, N.keep_out, N.send_out),
                N.grad_out, new=[(N.keep_out, (width, half), F32), (N.send_out, (width, half), F32)],
                drop=(N.mixed, N.grad_mid_low), scratch=turned,
            )
            third.begin(N.out)
        elif hop == 1:
            run(
                pool, functools.partial(grad_narrow_kernel, down_plan, N.low, N.grad_gate, N.keep_gates, N.send_gates),
                N.grad_gate, new=[(N.keep_gates, (width, half), F32), (N.send_gates, (width, half), F32)], scratch=turned,
            )
            third.begin(N.gates)
            wide.fold()
        if hop == hops - 1:
            wide.send()

    carry_back(pool, N.ends_back, between)
    span = -(-3 * tiles // 2) * LANES
    run(
        pool, functools.partial(scan_back_kernel, shape), N.scan_back,
        new=[(N.grad_pre, (rows, 3 * chans), BF16), (N.sums_scan, (3 * SUB, chans), F32), (N.turned, (rows, 2 * span), BF16)],
        fetch={N.wmix: w_mix, N.tok: tokens}, drop=(N.start, N.seeds, N.chunks, N.chunks_back, N.pre, N.states, N.entries),
        scratch={N.entries_back: pltpu.VMEM((2 * tiles, pad * SUB, LANES), F32),
                 N.made_pre: pltpu.VMEM((3 * tiles, positions, LANES), F32)},
    )
    third.step()
    (grad_tokens,) = run(
        pool, input_back_kernel, N.input_back, new=[(N.sums_in, (SUB, width), F32)],
        out=[(N.grad_tokens, (rows, width), F32)], drop=(N.grad_pre, N.grad_gate, N.wmix, N.tok, N.grad_mid),
        scratch={N.made: pltpu.VMEM((rows, width), F32)}, vmem=9,
    )
    fourth = Chunk(pool, scan_plan, N.scan, head=SUB)
    run(
        pool, functools.partial(grad_scan_kernel, scan_plan, chans), N.grad_scan,
        new=[(N.keep_scan, (SUB + width, span), F32)]
        + [("send_scan%d" % piece, (width // PIECES + (0 if piece else SUB), span), F32) for piece in range(PIECES)],
        scratch={N.made: pltpu.VMEM((width, span), F32)},
        drop=(N.turned, N.low, N.sums_in, N.sums_out, N.sums_ffn, N.sums_scan),
    )
    fourth.begin()
    block = width // wide_plan.blocks
    pair = Chunk({}, down_plan, N.pair)
    sets = {"w": wide, "p": pair, "s": fourth}
    for chunk in (wide, down, third, fourth):
        chunk.apart()

    def begin_pair(before):
        pair.pool = {**down.pool, **third.pool}
        (shape,) = {pair.pool[N.keep_down].shape}
        half = (shape[0] // 2, 2 * shape[1])
        run(
            pair.pool, functools.partial(fold_pair_kernel, down_plan.blocks // 2), N.fold_pair,
            new=[(N.send_pair, half, F32), (N.later_pair, half, F32)],
            args={N.got_down: down.got[N.got], N.got_third: third.got[N.got]}, drop=(N.keep_down, N.keep_third), after=before,
            vmem=5 if down_plan.in_place else 24,
        )
        pair.pool[N.keep_pair] = pair.pool.pop(N.later_pair)
        pair.sent = pair.pool.pop(N.send_pair)
        pair.done = 1
        pair.send()

    found, trail = {}, {}

    def gather_wide(before=()):
        found[N.first] = wide.whole(before)
        found[N.first_got] = across(found[N.first], N.batch, 2)

    def gather_pair(before=()):
        run(
            pair.pool, pack_kernel, N.pack, new=[(N.packed, (block, units), F32)], args=pair.got, drop=(N.keep_pair,), after=before,
        )
        found[N.second] = pair.pool.pop(N.packed)
        found[N.second_got] = across(found[N.second], N.batch, 2)

    def gather_scan():
        found[N.mine] = fourth.whole()
        found[N.got] = across(found[N.mine], N.batch, 2)

    for letter in ROUNDS:
        chunk = sets.get(letter)
        token = letter + str(chunk.done) if chunk else letter
        before = [trail[name] for name in DEPS.get(token, "").split() if name in trail]
        if letter == "o":
            space = {}
            (output,) = run(
                space, functools.partial(output_kernel, 3), N.output, new=[(N.mark, (SUB, LANES), F32)], out=[(N.output, (rows, width), BF16)],
                load={N.wdown_in: w_down, N.after_in: (stored[N.after], 3), N.hidden_in: (hidden_out, 3)},
                scratch={N.made: pltpu.VMEM((rows, width), BF16)}, vmem=14, after=before,
            )
            trail[token] = space[N.mark]
        elif chunk is pair and chunk.done == 0:
            begin_pair(before)
            trail[token] = pair.pool[N.keep_pair]
        elif chunk.done < len(chunk.plan.steps):
            chunk.step(before)
            trail[token] = chunk.pool[N.keep_ + chunk.name]
        elif letter == "w":
            if N.first not in found:
                gather_wide(before)
                trail[token] = found[N.first]
        elif letter == "s":
            if N.mine not in found:
                gather_scan()
                trail[token] = found[N.mine]
        elif N.second not in found:
            gather_pair(before)
    while any(chunk.done < len(chunk.plan.steps) for chunk in sets.values()):
        for chunk in sets.values():
            if chunk.done < len(chunk.plan.steps):
                chunk.step()
    for key, gather in ((N.first, gather_wide), (N.second, gather_pair), (N.mine, gather_scan)):
        if key not in found:
            gather()
    total, total_got = found.pop(N.mine), found.pop(N.got)
    final_rows = 2 * block
    run(
        pool, functools.partial(stack_kernel, N.batch, 2), N.stack, new=[(N.both, (final_rows, 2 * units), F32)],
        args=found, after=(total,),
    )
    packed = pool.pop(N.both)
    packed_got = across(packed, N.batch, 1)
    grad_down, grad_wide, grad_out, gate_part = finish(
        functools.partial(unpack_kernel, batch_size // 2), N.unpack, {N.mine: packed, N.got: packed_got},
        [(N.grad_down, (units // seq_size, width)), (N.grad_wide, (final_rows, 2 * units)), (N.grad_out, (final_rows, width)),
         (N.gate_part, (final_rows, width))],
    )
    run(
        pool, functools.partial(stack_head_kernel, N.batch, 2, SUB), N.stack_scan,
        new=[(N.both, (SUB + final_rows, span), F32)], args={N.mine: total, N.got: total_got}, after=(grad_out,),
    )
    total = pool.pop(N.both)
    total_got = across(total, N.batch, 1)
    grad_mix, *gains = finish(
        finish_kernel, N.finish, {N.mine: total, N.got: total_got, N.gate_part: gate_part},
        [(N.grad_mix, (final_rows, 3 * chans + width)), (N.vec_in, (width,)), (N.vec_out, (width,)), (N.vec_ffn, (width,)),
         (N.vec_lower, (chans,)), (N.vec_fbias, (chans,)), (N.vec_phase, (chans,))],
    )
    return (
        output.reshape(seqs, positions, width),
        grad_tokens.reshape(seqs, positions, width),
        grad_mix,
        grad_out,
        grad_wide,
        grad_down,
        *gains,
    )


def finish(kernel, name, args, outs):
    names = list(args) + [item[0] for item in outs]

    def body(*refs):
        kernel(types.SimpleNamespace(**dict(zip(names, refs))))

    return pl.pallas_call(
        body,
        out_shape=[jax.ShapeDtypeStruct(shape, F32) for _, shape in outs],
        in_specs=[pl.BlockSpec(memory_space=pltpu.VMEM)] * len(args),
        out_specs=[pl.BlockSpec(memory_space=pltpu.VMEM)] * len(outs),
        compiler_params=pltpu.CompilerParams(vmem_limit_bytes=8 * MIB),
        name=name,
    )(*args.values())


def solution(mesh):
    in_specs = (P(N.batch, N.seq, None), P(N.batch, N.seq, None)) + (P(),) * 10
    rows = P(N.seq, None)
    out_specs = (P(N.batch, N.seq, None), P(N.batch, N.seq, None), rows, rows, rows, rows) + (P(),) * 6
    return jax.shard_map(
        per_device, mesh=mesh, in_specs=in_specs, out_specs=out_specs, check_vma=False
    )
```

```python
import functools
import types

import jax
import jax.numpy as jnp
import numpy as np
from jax import lax
from jax.experimental import pallas as pl
from jax.experimental.pallas import tpu as pltpu
from jax.sharding import PartitionSpec as P

epsilon = 1e-06
LANES = 128
SUB = 8
F32 = jnp.float32
BF16 = jnp.bfloat16
MIB = 2**20


class Names:
    def __getattr__(self, name):
        return name


N = Names()
SCALE = 0.2
FOLD = 0.3
HOPS = (2, 1, 0)
ORDERS = {N.wide: (N.xzyw, N.ywzx), N.down: (N.yxzw, N.xywz), N.scan: (N.xywz, N.yxzw)}
ROUNDS = N.wpsposwpswpssp
DEPS = {N.s0: "p0 w2", N.p1: N.s0, "o": N.p1, N.s1: "o", N.w3: N.s1, N.p2: N.s1, N.p3: N.s2, N.w4: N.s2, N.s3: N.w4, N.p4: N.s4}
PIECES = 2
TIME = {
    N.project: 8.0, N.gate: 1.8, N.hidden_back: 1.9, N.mix: 5.9, N.ffn: 7.3, N.grad_gu: 3.2, N.grad_down: 3.6, N.ffn_back: 6.5,
    N.mix_back: 7.0, N.grad_out: 1.6, N.grad_gate: 1.6, N.scan_back: 4.0, N.input_back: 5.6, N.grad_scan: 2.4, N.output: 7.0,
}


def sigmoid(values):
    return 0.5 * jnp.tanh(0.5 * values) + 0.5


def forget_gate(forget, lower):
    decay = jnp.exp(jnp.minimum(-forget, 80.0))
    total = 1.0 + decay
    guess = pl.reciprocal(total, approx=True)
    open_part = guess * (2.0 - total * guess)
    shut_part = decay * open_part
    intake = (1.0 - lower) * shut_part
    return open_part, shut_part, intake, 1.0 - intake


def dot(left, right, left_dim, right_dim):
    return lax.dot_general(
        left, right, (((left_dim,), (right_dim,)), ((), ())), preferred_element_type=F32
    )


def row_block(rows, most):
    best = 16
    for size in range(16, most + 1, 16):
        if rows % size == 0:
            best = size
    return best


def rows_at(step, size):
    return pl.ds(pl.multiple_of(step * size, 16), size)


def tile_of(ref, tile):
    return ref[:, tile * LANES : (tile + 1) * LANES]


def fold_rows(values):
    rows, lanes = values.shape
    return jnp.sum(values.reshape(rows // SUB, SUB, lanes), axis=0)


def loop(count, body):
    lax.fori_loop(0, count, lambda step, _: (body(step), 0)[1], 0)


def project_kernel(shape, r):
    seqs, positions, chans = shape
    tiles = chans // LANES
    steps = positions // SUB
    rows = seqs * positions
    size = row_block(rows, 336)
    width = r.tok.shape[1]
    columns = 3 * chans
    first = pltpu.make_async_copy(r.mix.at[:, :columns], r.wmix.at[:, :columns], r.own.at[0])
    first.start()
    r.vec[...] = jnp.zeros(r.vec.shape, F32)
    for name in (N.raw_in, N.raw_lower, N.raw_fbias, N.raw_phase, N.raw_out, N.raw_ffn):
        r.wait(name)
    for row, name in enumerate((N.raw_in, N.raw_out, N.raw_ffn)):
        r.vec[row : row + 1, :] = getattr(r, name)[...].reshape(1, width)
    phase = r.raw_phase[...].reshape(1, chans)
    r.vec[3:4, :chans] = r.raw_lower[...].reshape(1, chans)
    r.vec[3:4, chans:] = r.raw_fbias[...].reshape(1, chans)
    r.vec[4:5, :chans] = jnp.cos(phase)
    r.vec[4:5, chans:] = jnp.sin(phase)
    r.vec[5:6, :chans] = jnp.cos(phase * steps)
    r.vec[5:6, chans:] = jnp.sin(phase * steps)
    r.vec[6:7, :chans] = jnp.cos(phase * positions)
    r.vec[6:7, chans:] = jnp.sin(phase * positions)
    gain = r.vec[0:1, :]
    fbias = r.vec[3:4, chans:]
    r.wait(N.tok)

    def norm(step):
        at = rows_at(step, size)
        inputs = r.tok[at, :].astype(F32)
        scale = lax.rsqrt(jnp.mean(inputs * inputs, axis=-1, keepdims=True) + epsilon)
        r.low[at, :] = (inputs * scale * gain).astype(BF16)

    loop(rows // size, norm)
    rest = pltpu.make_async_copy(r.mix.at[:, columns:], r.wmix.at[:, columns:], r.own.at[1])
    first.wait()
    rest.start()
    r.start_late()

    def project(step):
        at = rows_at(step, size)
        for part in range(3):
            made = dot(r.low[at, :], r.wmix[:, part * chans : (part + 1) * chans], 1, 0)
            if part == 2:
                made = made + fbias
            for tile in range(tiles):
                r.pre[part * tiles + tile, at, :] = made[:, tile * LANES : (tile + 1) * LANES]

    loop(rows // size, project)

    def scan(seq):
        for tile in range(tiles):
            lanes = slice(tile * LANES, (tile + 1) * LANES)
            low_bound, cos_t, sin_t = r.vec[3:4, lanes], r.vec[4:5, lanes], sine_of(r, lanes)
            product = jnp.ones((SUB, LANES), F32)
            state_r = jnp.zeros((SUB, LANES), F32)
            state_i = jnp.zeros((SUB, LANES), F32)
            for step in range(steps):
                at = pl.ds(seq * positions + step, SUB, stride=steps)
                in_r, in_i = r.pre[tile, at, :], r.pre[tiles + tile, at, :]
                _, _, intake, retain = forget_gate(r.pre[2 * tiles + tile, at, :], low_bound)
                mul_r, mul_i = retain * cos_t, retain * sin_t
                add_r, add_i = intake * (in_r * sigmoid(in_r)), intake * (in_i * sigmoid(in_i))
                state_r, state_i = (
                    mul_r * state_r - mul_i * state_i + add_r,
                    mul_r * state_i + mul_i * state_r + add_i,
                )
                product = product * retain
                r.decay[tile, at, :] = retain
                r.adds[tile, at, :] = add_r
                r.adds[tiles + tile, at, :] = add_i
            at = pl.ds(pl.multiple_of(seq * SUB, SUB), SUB)
            r.chunks[tile, at, :] = product
            r.chunks[tiles + tile, at, :] = state_r
            r.chunks[2 * tiles + tile, at, :] = state_i

    r.chunks[...] = jnp.zeros(r.chunks.shape, F32)
    loop(seqs, scan)
    joined(r, tiles, r.chunks, tiles, r.ends, False)
    rest.wait()


def sine_of(r, lanes):
    chans = r.vec.shape[1] // 2
    return r.vec[4:5, chans + lanes.start : chans + lanes.stop]


def chunk_step(r, tiles, tile, at, added, base, now_r, now_i, backward):
    lanes = slice(tile * LANES, (tile + 1) * LANES)
    chans = r.vec.shape[1] // 2
    product = r.chunks[tile, at, :]
    new_r = product * r.vec[5:6, lanes]
    new_i = product * r.vec[5:6, chans + lanes.start : chans + lanes.stop]
    if backward:
        new_i = -new_i
    return (
        new_r,
        new_i,
        new_r * now_r - new_i * now_i + added[base + tile, at, :],
        new_r * now_i + new_i * now_r + added[base + tiles + tile, at, :],
    )


def joined(r, tiles, added, base, ends, backward):
    pad = ends.shape[1]
    for tile in range(tiles):
        mul_r, mul_i = jnp.ones((pad, LANES), F32), jnp.zeros((pad, LANES), F32)
        add_r, add_i = jnp.zeros((pad, LANES), F32), jnp.zeros((pad, LANES), F32)
        for chunk in reversed(range(SUB)) if backward else range(SUB):
            at = pl.ds(chunk, pad, stride=SUB)
            new_r, new_i, add_r, add_i = chunk_step(r, tiles, tile, at, added, base, add_r, add_i, backward)
            mul_r, mul_i = mul_r * new_r - mul_i * new_i, mul_r * new_i + mul_i * new_r
        ends[tile] = mul_r
        ends[tiles + tile] = mul_i
        ends[2 * tiles + tile] = add_r
        ends[3 * tiles + tile] = add_i


def entered(r, tiles, added, base, start, entries, backward):
    pad = start.shape[1]
    for tile in range(tiles):
        now_r, now_i = start[tile], start[tiles + tile]
        for chunk in reversed(range(SUB)) if backward else range(SUB):
            at = pl.ds(chunk, pad, stride=SUB)
            entries[tile, at, :] = now_r
            entries[tiles + tile, at, :] = now_i
            _, _, now_r, now_i = chunk_step(r, tiles, tile, at, added, base, now_r, now_i, backward)


def carry_kernel(bit, first, last, backward, r):
    tiles = r.total.shape[0] // 4
    later = (lax.axis_index(N.seq) & bit) != 0
    if backward:
        later = jnp.logical_not(later)
    for tile in range(tiles):
        parts = [part * tiles + tile for part in range(4)]
        mine = tuple(r.total[part] for part in parts)
        got = tuple(r.got[part] for part in parts)
        one, zero = jnp.ones(mine[0].shape, F32), jnp.zeros(mine[0].shape, F32)
        before = (one, zero, zero, zero) if first else tuple(r.before[part] for part in parts)
        longer = combine(got, before)
        before = [jnp.where(later, new, old) for new, old in zip(longer, before)]
        if last:
            r.start[tile] = before[2]
            r.start[tiles + tile] = before[3]
        else:
            ahead = [jnp.where(later, b, a) for a, b in zip(mine, got)]
            behind = [jnp.where(later, a, b) for a, b in zip(mine, got)]
            for part, new, total in zip(parts, before, combine(ahead, behind)):
                r.before_next[part] = new
                r.total_next[part] = total


def gate_kernel(chans, r):
    tiles, rows, _ = r.gate.shape
    size = row_block(rows, 336)

    def step_of(step):
        at = rows_at(step, size)
        made = dot(r.low[at, :], r.wmix[:, 3 * chans :], 1, 0)
        for tile in range(tiles):
            r.gate[tile, at, :] = made[:, tile * LANES : (tile + 1) * LANES]

    loop(rows // size, step_of)


def hidden_back_kernel(first, name, r):
    made = getattr(r, name)
    rows, units = made.shape
    size = row_block(rows, 336)

    def step_of(step):
        at = rows_at(step, size)
        for part in range(units // 256):
            cols = slice(part * 256, (part + 1) * 256)
            weight = r.wdown[first + part * 256 : first + (part + 1) * 256, :]
            made[at, cols] = dot(r.cot[at, :], weight, 1, 1).astype(BF16)

    loop(rows // size, step_of)


def mix_kernel(shape, r):
    seqs, positions, chans = shape
    tiles = chans // LANES
    steps = positions // SUB
    rows = seqs * positions
    width = 2 * chans
    size = row_block(rows, 144)
    entered(r, tiles, r.chunks, tiles, r.start, r.entries, False)

    def scan(seq):
        for tile in range(tiles):
            lanes = slice(tile * LANES, (tile + 1) * LANES)
            cos_t, sin_t = r.vec[4:5, lanes], sine_of(r, lanes)
            at = pl.ds(pl.multiple_of(seq * SUB, SUB), SUB)
            state_r, state_i = r.entries[tile, at, :], r.entries[tiles + tile, at, :]
            for step in range(steps):
                at = pl.ds(seq * positions + step, SUB, stride=steps)
                retain = r.decay[tile, at, :]
                add_r, add_i = r.adds[tile, at, :], r.adds[tiles + tile, at, :]
                mul_r, mul_i = retain * cos_t, retain * sin_t
                state_r, state_i = (
                    mul_r * state_r - mul_i * state_i + add_r,
                    mul_r * state_i + mul_i * state_r + add_i,
                )
                r.states[tile, at, :] = state_r
                r.states[tiles + tile, at, :] = state_i

    loop(seqs, scan)

    def mix(step):
        at = rows_at(step, size)
        squares = jnp.zeros((size, LANES), F32)
        for tile in range(2 * tiles):
            part = r.states[tile, at, :]
            squares = squares + part * part
        scale = lax.rsqrt(jnp.sum(squares, axis=-1, keepdims=True) / width + epsilon)
        for tile in range(2 * tiles):
            lanes = slice(tile * LANES, (tile + 1) * LANES)
            gated = r.gate[tile, at, :]
            part = r.states[tile, at, :] * scale * r.vec[1:2, lanes] * (gated * sigmoid(gated))
            r.mixed[at, lanes] = part.astype(BF16)
        total = r.tok[at, :].astype(F32) + dot(r.mixed[at, :], r.wout[...], 1, 0)
        r.after[at, :] = total
        scale = lax.rsqrt(jnp.mean(total * total, axis=-1, keepdims=True) + epsilon)
        r.ffn_low[at, :] = (total * scale * r.vec[2:3, :]).astype(BF16)

    loop(rows // size, mix)


def ffn_kernel(r):
    rows, units = r.hidden.shape
    for name in (N.after, N.mixed, N.low, N.pre, N.states, N.gate):
        r.save(getattr(r, name), getattr(r, name + N._out))
    size = row_block(rows, 336)
    wide = 256

    def step_of(step):
        at = rows_at(step, size)
        block = r.ffn_low[at, :]
        for part in range(units // wide):
            cols = slice(part * wide, (part + 1) * wide)
            later = slice(units + part * wide, units + (part + 1) * wide)
            gate = dot(block, r.wgu[:, cols], 1, 0)
            up = dot(block, r.wgu[:, later], 1, 0)
            side, at_side = (r.back0, part) if 2 * part * wide < units else (r.back1, part - units // wide // 2)
            back = side[at, at_side * wide : (at_side + 1) * wide].astype(F32)
            sigma = sigmoid(gate)
            act = gate * sigma
            r.hidden[at, cols] = (act * up).astype(BF16)
            r.grad_gu[at, cols] = (back * up * (sigma + act * (1.0 - sigma))).astype(BF16)
            r.grad_gu[at, later] = (back * act).astype(BF16)

    loop(rows // size, step_of)


def block_slots(plan):
    if not plan.in_place:
        return list(range(plan.made)), list(range(plan.made))
    seq, batch = lax.axis_index(N.seq), lax.axis_index(N.batch)
    odd = (batch & 1) == 1
    rest = plan.rest

    def place(order, seq_bits, batch_bits):
        total = 0
        for index, (axis, bit) in enumerate(order):
            value = seq_bits if axis == N.seq else batch_bits
            total = total + (((value & bit) // bit) << (len(order) - 1 - index))
        return total

    mine = [place(order, seq, batch) for order in plan.orders]
    keep, send = [], []
    for block in range(plan.blocks):
        fixed = [place(order, block // rest, (block % rest) * 2) for order in plan.orders]
        first, second = fixed[0] ^ mine[0], fixed[1] ^ mine[1]
        keep.append(jnp.where(odd, second, first))
        send.append(jnp.where(odd, first, second))
    return keep, send


def store_blocks(ref, slots, size, cols, values, base=0):
    for block, slot in enumerate(slots):
        at = base + slot * size if isinstance(slot, int) else pl.multiple_of(base + slot * size, SUB)
        ref[pl.ds(at, size), cols] = values[block * size : (block + 1) * size, :]


def grad_narrow_kernel(plan, left, right, keep, send, r):
    left, right, keep, send = (getattr(r, name) for name in (left, right, keep, send))
    mine = lax.axis_index(N.batch) & 1
    kept, sent = block_slots(plan)
    half = right.shape[1] // 2
    r.turned[:, :half] = right[:, pl.ds(pl.multiple_of(mine * half, LANES), half)]
    r.turned[:, half:] = right[:, pl.ds(pl.multiple_of((1 - mine) * half, LANES), half)]
    size = left.shape[1] // plan.made
    tall = min(left.shape[1], 384)
    cols = slice(0, half)
    count = tall // size
    for part in range(left.shape[1] // tall):
        made = dot(left[:, part * tall : (part + 1) * tall], r.turned[...], 0, 0)
        there = slice(part * count, (part + 1) * count)
        store_blocks(keep, kept[there], size, cols, made[:, :half])
        store_blocks(send, sent[there], size, cols, made[:, half:])


def grad_wide_kernel(plan, left, right, made_name, sending, wide, r):
    left, right, out = getattr(r, left), getattr(r, right), getattr(r, made_name)
    mine = lax.axis_index(N.batch) & 1
    owner = 1 - mine if sending else mine
    slots = block_slots(plan)[1 if sending else 0]
    half = right.shape[1] // 2
    size = left.shape[1] // plan.made

    def step_of(part):
        cols = pl.ds(pl.multiple_of(part * wide, LANES), wide)
        source = pl.ds(pl.multiple_of(owner * half + part * wide, LANES), wide)
        store_blocks(out, slots, size, cols, dot(left[...], right[:, source], 0, 0))

    loop(half // wide, step_of)


def fold_kernel(names, head, r):
    keep, got = getattr(r, names[0]), r.got
    send_next, keep_next = getattr(r, names[1]), getattr(r, names[2])
    half = (keep.shape[0] - head) // 2
    send_next[head:, :] = keep[head + half :, :] + got[head + half :, :]
    keep_next[head:, :] = keep[head : head + half, :] + got[head : head + half, :]
    if head:
        both = keep[:head, :] + got[:head, :]
        send_next[:head, :] = both
        keep_next[:head, :] = both


def fold_first_kernel(parts, head, pieces, names, r):
    send_next, keep_next = getattr(r, names[0]), getattr(r, names[1])
    start = 0
    for part in parts:
        keep = getattr(r, N.keep_ + part)
        rows = keep.shape[0] - head
        half = rows // 2
        cols = slice(start, start + keep.shape[1])
        start = cols.stop
        count = max(pieces, 2)
        size = rows // count
        for piece in range(count):
            at = piece * size
            if pieces == 1:
                got = getattr(r, "got_%s0" % part)[head + at : head + at + size, :]
            else:
                first = head if piece == 0 else 0
                got = getattr(r, "got_%s%d" % (part, piece))[first : first + size, :]
            value = keep[head + at : head + at + size, :] + got
            if at < half:
                keep_next[head + at : head + at + size, cols] = value
            else:
                send_next[head + at - half : head + at - half + size, cols] = value
        if head:
            both = keep[:head, :] + getattr(r, "got_%s0" % part)[:head, :]
            send_next[:head, cols] = both
            keep_next[:head, cols] = both


def sum_kernel(name, r):
    r.total[...] = getattr(r, name)[...] + r.got[...]


def fold_pair_kernel(slots, r):
    per, wide = r.keep_down.shape[0] // slots, r.keep_down.shape[1]
    rows = r.keep_third.shape[0] // slots
    for slot in range(slots):
        out = r.later_pair if 2 * slot < slots else r.send_pair
        to = slot % (slots // 2) * per
        at = slice(slot * per, (slot + 1) * per)
        out[to : to + per, :wide] = r.keep_down[at, :] + r.got_down[at, :]
        at = slice(slot * rows, (slot + 1) * rows)
        value = r.keep_third[at, :] + r.got_third[at, :]
        out[to : to + rows, wide:] = value[:, :wide]
        out[to + rows : to + per, wide:] = value[:, wide:]


def pack_kernel(r):
    rows, wide = r.packed.shape[0], r.keep_pair.shape[1] // 2
    total = r.keep_pair[...] + r.got[...]
    r.packed[:, :wide] = total[:rows, wide:]
    r.packed[:, wide : 2 * wide] = total[rows:, wide:]
    r.packed[:, 2 * wide : 3 * wide] = total[:rows, :wide]
    r.packed[:, 3 * wide :] = total[rows:, :wide]


def stack_kernel(axis, bit, r):
    upper = (lax.axis_index(axis) & bit) != 0
    start = 0
    for mine, got in ((r.first, r.first_got), (r.second, r.second_got)):
        rows, wide = mine.shape
        cols = slice(start, start + wide)
        start = cols.stop
        r.both[:rows, cols] = jnp.where(upper, got[...], mine[...])
        r.both[rows:, cols] = jnp.where(upper, mine[...], got[...])


def stack_head_kernel(axis, bit, head, r):
    upper = (lax.axis_index(axis) & bit) != 0
    rows = r.mine.shape[0]
    r.both[:head, :] = r.mine[:head, :]
    r.both[head:rows, :] = jnp.where(upper, r.got[head:, :], r.mine[head:, :])
    r.both[rows:, :] = jnp.where(upper, r.mine[head:, :], r.got[head:, :])


def unpack_kernel(parts, r):
    upper = (lax.axis_index(N.batch) & 1) != 0
    units, width = r.grad_down.shape[0], r.grad_down.shape[1]
    half = width // 2
    rows = r.mine.shape[0]
    wide = r.grad_wide.shape[1] // 2
    size = rows // parts

    def sides(at, cols):
        mine, got = r.mine[at, cols], r.got[at, cols]
        return jnp.where(upper, got, mine), jnp.where(upper, mine, got)

    every = slice(0, rows)
    r.grad_wide[:, :wide], r.grad_wide[:, wide:] = sides(every, slice(0, wide))
    r.grad_out[:, :half], r.grad_out[:, half:] = sides(every, slice(wide, wide + half))
    r.gate_part[:, :half], r.gate_part[:, half:] = sides(every, slice(wide + half, wide + 2 * half))
    base = wide + 2 * half
    per = units // rows
    for part in range(parts):
        for piece in range(per):
            at = slice(part * size, (part + 1) * size)
            to = slice((part * per + piece) * size, (part * per + piece + 1) * size)
            first, second = sides(at, slice(base + piece * half, base + (piece + 1) * half))
            r.grad_down[to, :half] = first
            r.grad_down[to, half:] = second


def finish_kernel(r):
    upper = (lax.axis_index(N.batch) & 1) != 0
    wide = r.mine.shape[1]
    first = jnp.where(upper, r.got[SUB:, :], r.mine[SUB:, :])
    second = jnp.where(upper, r.mine[SUB:, :], r.got[SUB:, :])
    gate = r.gate_part.shape[1]
    scan = r.grad_mix.shape[1] - gate
    r.grad_mix[:, :wide] = first
    r.grad_mix[:, wide:scan] = second[:, 2 * wide - scan :]
    r.grad_mix[:, scan:] = r.gate_part[...]
    index = 0
    for name in (N.vec_in, N.vec_out, N.vec_ffn, N.vec_lower, N.vec_fbias, N.vec_phase):
        ref = getattr(r, name)
        for tile in range(ref.shape[0] // LANES):
            rows, lanes = sum_place(wide, index)
            ref[tile * LANES : (tile + 1) * LANES] = r.mine[rows, lanes].reshape(LANES)
            index += 1


def ffn_back_kernel(r):
    rows, width = r.after.shape
    size = row_block(rows, 336)
    r.sums_ffn[...] = jnp.zeros(r.sums_ffn.shape, F32)

    def ffn_back(step):
        at = rows_at(step, size)
        back = dot(r.grad_gu[at, :], r.wgu[...], 1, 1)
        total = r.after[at, :]
        scale = lax.rsqrt(jnp.mean(total * total, axis=-1, keepdims=True) + epsilon)
        normed = total * scale
        r.sums_ffn[...] += fold_rows(back * normed)
        scaled = back * r.vec[2:3, :]
        shared = jnp.mean(scaled * normed, axis=-1, keepdims=True)
        made = r.cot[at, :].astype(F32) + scale * (scaled - normed * shared)
        r.grad_mid[at, :] = made
        r.grad_mid_low[at, :] = made.astype(BF16)

    loop(rows // size, ffn_back)


def mix_back_kernel(shape, r):
    seqs, positions, chans = shape
    tiles = chans // LANES
    steps = positions // SUB
    rows = seqs * positions
    width = 2 * chans
    small = row_block(rows, 144)
    r.sums_out[...] = jnp.zeros(r.sums_out.shape, F32)

    def mix_back(step):
        at = rows_at(step, small)
        back = dot(r.grad_mid_low[at, :], r.wout[...], 1, 1)
        squares = jnp.zeros((small, LANES), F32)
        for tile in range(2 * tiles):
            part = r.states[tile, at, :]
            squares = squares + part * part
        scale = lax.rsqrt(jnp.sum(squares, axis=-1, keepdims=True) / width + epsilon)
        shared = jnp.zeros((small, LANES), F32)
        for tile in range(2 * tiles):
            lanes = slice(tile * LANES, (tile + 1) * LANES)
            gated = r.gate[tile, at, :]
            sigma = sigmoid(gated)
            act = gated * sigma
            normed = r.states[tile, at, :] * scale
            part = back[:, lanes]
            gain = r.vec[1:2, lanes]
            r.grad_gate[at, lanes] = (part * normed * gain * (sigma + act * (1.0 - sigma))).astype(BF16)
            inner = part * act
            product = inner * normed
            r.sums_out[:, lanes] += fold_rows(product)
            shared = shared + product * gain
            r.seeds[tile, at, :] = inner * gain
        mean = jnp.sum(shared, axis=-1, keepdims=True) / width
        for tile in range(2 * tiles):
            normed = r.states[tile, at, :] * scale
            r.seeds[tile, at, :] = scale * (r.seeds[tile, at, :] - normed * mean)

    loop(rows // small, mix_back)

    def scan(seq):
        for tile in range(tiles):
            lanes = slice(tile * LANES, (tile + 1) * LANES)
            low_bound, cos_t, sin_t = r.vec[3:4, lanes], r.vec[4:5, lanes], sine_of(r, lanes)
            flow_r = jnp.zeros((SUB, LANES), F32)
            flow_i = jnp.zeros((SUB, LANES), F32)
            for step in reversed(range(steps)):
                at = pl.ds(seq * positions + step, SUB, stride=steps)
                _, _, _, retain = forget_gate(r.pre[2 * tiles + tile, at, :], low_bound)
                mul_r, mul_i = retain * cos_t, retain * sin_t
                adj_r = r.seeds[tile, at, :] + flow_r
                adj_i = r.seeds[tiles + tile, at, :] + flow_i
                flow_r = mul_r * adj_r + mul_i * adj_i
                flow_i = mul_r * adj_i - mul_i * adj_r
            at = pl.ds(pl.multiple_of(seq * SUB, SUB), SUB)
            r.chunks_back[tile, at, :] = flow_r
            r.chunks_back[tiles + tile, at, :] = flow_i

    r.chunks_back[...] = jnp.zeros(r.chunks_back.shape, F32)
    loop(seqs, scan)
    pad = r.ends_back.shape[2]
    for tile in range(tiles):
        product = jnp.ones((pad, LANES), F32)
        add_r, add_i = jnp.zeros((pad, LANES), F32), jnp.zeros((pad, LANES), F32)
        for chunk in reversed(range(SUB)):
            at = pl.ds(chunk, pad, stride=SUB)
            product = product * r.chunks[tile, at, :]
            _, _, add_r, add_i = chunk_step(r, tiles, tile, at, r.chunks_back, 0, add_r, add_i, True)
        r.ends_back[0, tile] = product
        r.ends_back[0, tiles + tile] = add_r
        r.ends_back[0, 2 * tiles + tile] = add_i


def append_kernel(r):
    count = r.have.shape[0]
    r.both[:count] = r.have[...]
    r.both[count:] = r.got[...]


def enter_kernel(bits, r):
    mine = lax.axis_index(N.seq)
    count = r.have.shape[0]
    tiles = r.have.shape[1] // 3
    r.both[:count] = r.have[...]
    r.both[count:] = r.got[...]
    for tile in range(tiles):
        lanes = slice(tile * LANES, (tile + 1) * LANES)
        chans = r.vec.shape[1] // 2
        turn_r = r.vec[6:7, lanes]
        turn_i = r.vec[6:7, chans + lanes.start : chans + lanes.stop]
        now_r = jnp.zeros(r.have.shape[2:], F32)
        now_i = jnp.zeros(r.have.shape[2:], F32)
        for other in reversed(range(1, 2 * count)):
            index = 0
            for place, bit in enumerate(bits):
                index = index + ((((mine ^ other) & bit) // bit) << place)
            product = r.both[index, tile]
            mul_r, mul_i = product * turn_r, product * turn_i
            next_r = mul_r * now_r + mul_i * now_i + r.both[index, tiles + tile]
            next_i = mul_r * now_i - mul_i * now_r + r.both[index, 2 * tiles + tile]
            now_r = jnp.where(other > mine, next_r, now_r)
            now_i = jnp.where(other > mine, next_i, now_i)
        r.start[tile] = now_r
        r.start[tiles + tile] = now_i


def scan_back_kernel(shape, r):
    seqs, positions, chans = shape
    tiles = chans // LANES
    steps = positions // SUB
    entered(r, tiles, r.chunks_back, 0, r.start, r.entries_back, True)
    r.sums_scan[...] = jnp.zeros(r.sums_scan.shape, F32)
    mine = lax.axis_index(N.batch) & 1
    half = r.turned.shape[1] // 2
    shift = 3 * chans - half
    keep_at = pl.ds(pl.multiple_of(mine * shift, LANES), half)
    send_at = pl.ds(pl.multiple_of((1 - mine) * shift, LANES), half)

    def scan(seq):
        for tile in range(tiles):
            lanes = slice(tile * LANES, (tile + 1) * LANES)
            low_bound, cos_t, sin_t = r.vec[3:4, lanes], r.vec[4:5, lanes], sine_of(r, lanes)
            chunk_at = pl.ds(pl.multiple_of(seq * SUB, SUB), SUB)
            flow_r, flow_i = r.entries_back[tile, chunk_at, :], r.entries_back[tiles + tile, chunk_at, :]
            sum_lower = jnp.zeros((SUB, LANES), F32)
            sum_fbias = jnp.zeros((SUB, LANES), F32)
            sum_phase = jnp.zeros((SUB, LANES), F32)
            for step in reversed(range(steps)):
                at = pl.ds(seq * positions + step, SUB, stride=steps)
                in_r, in_i = r.pre[tile, at, :], r.pre[tiles + tile, at, :]
                opened, shut, intake, retain = forget_gate(r.pre[2 * tiles + tile, at, :], low_bound)
                sig_r, sig_i = sigmoid(in_r), sigmoid(in_i)
                act_r, act_i = in_r * sig_r, in_i * sig_i
                adj_r = r.seeds[tile, at, :] + flow_r
                adj_i = r.seeds[tiles + tile, at, :] + flow_i
                mul_r, mul_i = retain * cos_t, retain * sin_t
                flow_r = mul_r * adj_r + mul_i * adj_i
                flow_i = mul_r * adj_i - mul_i * adj_r
                if step > 0:
                    before = pl.ds(seq * positions + step - 1, SUB, stride=steps)
                    past_r, past_i = r.states[tile, before, :], r.states[tiles + tile, before, :]
                else:
                    past_r, past_i = r.entries[tile, chunk_at, :], r.entries[tiles + tile, chunk_at, :]
                grad_r = adj_r * past_r + adj_i * past_i
                grad_i = adj_i * past_r - adj_r * past_i
                grad_retain = grad_r * cos_t + grad_i * sin_t - (adj_r * act_r + adj_i * act_i)
                sum_phase = sum_phase + retain * (grad_i * cos_t - grad_r * sin_t)
                sum_lower = sum_lower + grad_retain * shut
                grad_forget = grad_retain * intake * opened
                sum_fbias = sum_fbias + grad_forget
                at = pl.ds(step, SUB, stride=steps)
                r.made_pre[tile, at, :] = adj_r * intake * (sig_r + act_r * (1.0 - sig_r))
                r.made_pre[tiles + tile, at, :] = adj_i * intake * (sig_i + act_i * (1.0 - sig_i))
                r.made_pre[2 * tiles + tile, at, :] = grad_forget
            r.sums_scan[0:SUB, lanes] += sum_lower
            r.sums_scan[SUB : 2 * SUB, lanes] += sum_fbias
            r.sums_scan[2 * SUB : 3 * SUB, lanes] += sum_phase
        seq_rows = rows_at(seq, positions)
        for tile in range(3 * tiles):
            r.grad_pre[seq_rows, tile * LANES : (tile + 1) * LANES] = r.made_pre[tile].astype(BF16)
        r.turned[seq_rows, :half] = r.grad_pre[seq_rows, keep_at]
        r.turned[seq_rows, half:] = r.grad_pre[seq_rows, send_at]

    loop(seqs, scan)


def grad_scan_kernel(plan, chans, r):
    kept, sent = block_slots(plan)
    half = r.turned.shape[1] // 2
    size = r.low.shape[1] // plan.made
    tall = min(r.low.shape[1], 384)
    count = tall // size
    for part in range(r.low.shape[1] // tall):
        made = dot(r.low[:, part * tall : (part + 1) * tall], r.turned[...], 0, 0)
        there = slice(part * count, (part + 1) * count)
        store_blocks(r.keep_scan, kept[there], size, slice(0, half), made[:, :half], SUB)
        store_blocks(r.made, sent[there], size, slice(0, half), made[:, half:])
    zero = jnp.zeros((SUB, half), F32)
    r.keep_scan[0:SUB, :] = zero
    index = 0
    for source in (r.sums_in, r.sums_out, r.sums_ffn):
        for tile in range(source.shape[1] // LANES):
            total = jnp.sum(source[:, tile * LANES : (tile + 1) * LANES], axis=0, keepdims=True)
            put_sum(r.keep_scan, index, total)
            index += 1
    for part in range(3):
        for tile in range(chans // LANES):
            block = r.sums_scan[part * SUB : (part + 1) * SUB, tile * LANES : (tile + 1) * LANES]
            put_sum(r.keep_scan, index, jnp.sum(block, axis=0, keepdims=True))
            index += 1
    rows = r.made.shape[0] // PIECES
    r.send_scan0[0:SUB, :] = r.keep_scan[0:SUB, :]
    r.send_scan0[SUB:, :] = r.made[:rows, :]
    for piece in range(1, PIECES):
        getattr(r, "send_scan%d" % piece)[...] = r.made[piece * rows : (piece + 1) * rows, :]


def sum_place(wide, index):
    row, tile = divmod(index, wide // LANES)
    return slice(row, row + 1), slice(tile * LANES, (tile + 1) * LANES)


def put_sum(ref, index, total):
    rows, lanes = sum_place(ref.shape[1], index)
    ref[rows, lanes] = total


def input_back_kernel(r):
    rows, chans3 = r.grad_pre.shape
    size = row_block(rows, 336)
    r.sums_in[...] = jnp.zeros(r.sums_in.shape, F32)

    for step in range(rows // size):
        at = pl.ds(step * size, size)
        back = dot(r.grad_pre[at, :], r.wmix[:, :chans3], 1, 1)
        back = back + dot(r.grad_gate[at, :], r.wmix[:, chans3:], 1, 1)
        inputs = r.tok[at, :].astype(F32)
        scale = lax.rsqrt(jnp.mean(inputs * inputs, axis=-1, keepdims=True) + epsilon)
        normed = inputs * scale
        r.sums_in[...] += fold_rows(back * normed)
        scaled = back * r.vec[0:1, :]
        shared = jnp.mean(scaled * normed, axis=-1, keepdims=True)
        r.made[at, :] = r.grad_mid[at, :] + scale * (scaled - normed * shared)
        r.save(r.made.at[at, :], r.grad_tokens.at[at, :])


def output_kernel(count, r):
    rows, _ = r.output.shape
    r.mark[...] = jnp.zeros(r.mark.shape, F32)
    size = rows // count
    r.wait(N.wdown_in)
    for step in range(count):
        at = pl.ds(step * size, size)
        for name in (N.after_in, N.hidden_in):
            r.wait(name + str(step))
        made = dot(getattr(r, N.hidden_in + str(step))[...], r.wdown_in[...], 1, 0)
        r.made[at, :] = (getattr(r, N.after_in + str(step))[...] + made).astype(BF16)
        r.save(r.made.at[at, :], r.output.at[at, :])


def run(pool, kernel, name, new=(), args=None, fetch=None, load=None, out=(), drop=(), reuse=None, scratch=None, vmem=5, after=(), late=(), raw=None):
    args, fetch, load, reuse, scratch = args or {}, fetch or {}, load or {}, reuse or {}, scratch or {}
    whole = {key: value for key, value in load.items() if not isinstance(value, tuple)}
    scratch = {**scratch, **{key: pltpu.VMEM(value.shape, value.dtype) for key, value in whole.items()}}
    parts = {key: value for key, value in load.items() if isinstance(value, tuple)}
    load = {key: value for key, value in load.items() if key not in parts}
    incoming = {**fetch, **load}
    for key, (value, count) in parts.items():
        rows = value.shape[0] // count
        for part in range(count):
            scratch[key + str(part)] = pltpu.VMEM((rows,) + value.shape[1:], value.dtype)
    kept = [key for key in pool if key not in drop]
    dropped = [key for key in pool if key in drop]
    new_names = [item[0] for item in new]
    operands = [pool[key] for key in kept + dropped]
    operands += [pltpu.with_memory_space_constraint(value, pltpu.VMEM) for value in args.values()]
    operands += [pltpu.with_memory_space_constraint(value, pltpu.HBM) for value in incoming.values()]
    in_names = kept + dropped + list(args) + ["hbm " + key for key in incoming] + ["after%d" % index for index in range(len(after))]
    operands += list(after)
    in_names += ["hbm " + key for key in parts] + list(raw or {})
    operands += [pltpu.with_memory_space_constraint(value, pltpu.HBM) for value, _ in parts.values()]
    operands += [pltpu.with_memory_space_constraint(value, pltpu.HBM) for value in (raw or {}).values()]
    shapes = [pltpu.VMEM(pool[key].shape, pool[key].dtype) for key in kept]
    shapes += [pltpu.VMEM(shape, kind) for _, shape, kind in new]
    shapes += [pltpu.VMEM(value.shape, value.dtype) for value in fetch.values()]
    shapes += [pltpu.HBM(shape, kind) for _, shape, kind in out]
    out_names = ["out " + key for key in kept] + new_names + list(fetch) + [item[0] for item in out]
    aliases = {index: index for index in range(len(kept))}
    for key, old in reuse.items():
        aliases[in_names.index(old)] = out_names.index(key)
    copies = len(incoming) + sum(count for _, count in parts.values()) + len(out) + 8

    def body(*refs):
        r = types.SimpleNamespace(**dict(zip(in_names + out_names + list(scratch), refs)))
        sems = refs[-1]
        waiting = {}
        for index, key in enumerate(incoming):
            copy = pltpu.make_async_copy(getattr(r, "hbm " + key), getattr(r, key), sems.at[index])
            if key not in late:
                copy.start()
            waiting[key] = copy

        index = len(incoming)
        for part in range(max([count for _, count in parts.values()], default=0)):
            for key, (value, count) in parts.items():
                rows = value.shape[0] // count
                source = getattr(r, "hbm " + key).at[pl.ds(part * rows, rows), :]
                copy = pltpu.make_async_copy(source, getattr(r, key + str(part)), sems.at[index])
                copy.start()
                waiting[key + str(part)] = copy
                index += 1
        taken = index

        def save(source, target):
            index = taken + len([key for key in waiting if key.startswith("save ")])
            copy = pltpu.make_async_copy(source, target, sems.at[index])
            copy.start()
            waiting["save " + str(index)] = copy

        r.wait = lambda key: waiting.pop(key).wait()
        r.save = save
        r.start_late = lambda: [waiting[key].start() for key in late]
        kernel(r)
        for copy in waiting.values():
            copy.wait()

    made = pl.pallas_call(
        body,
        out_shape=shapes,
        in_specs=[pl.BlockSpec(memory_space=pltpu.VMEM)] * (len(kept) + len(dropped) + len(args))
        + [pl.BlockSpec(memory_space=pltpu.HBM)] * len(incoming)
        + [pl.BlockSpec(memory_space=pl.ANY)] * len(after)
        + [pl.BlockSpec(memory_space=pltpu.HBM)] * (len(parts) + len(raw or {})),
        out_specs=[pl.BlockSpec(memory_space=pl.ANY)] * len(kept)
        + [pl.BlockSpec(memory_space=pltpu.VMEM)] * (len(new) + len(fetch))
        + [pl.BlockSpec(memory_space=pltpu.HBM)] * len(out),
        scratch_shapes=list(scratch.values()) + [pltpu.SemaphoreType.DMA((copies,))],
        input_output_aliases=aliases,
        compiler_params=pltpu.CompilerParams(vmem_limit_bytes=vmem * MIB),
        cost_estimate=pl.CostEstimate(flops=int(SCALE * TIME.get(name, FOLD if name.startswith(N.fold) else 0.3) * 1.15e9), bytes_accessed=0, transcendentals=0),
        name=name,
    )(*operands)
    pool.clear()
    count = len(kept) + len(new) + len(fetch)
    pool.update(zip(kept + new_names + list(fetch), made[:count]))
    return made[count:]


def combine(earlier, later_part):
    mul_r, mul_i, add_r, add_i = earlier
    new_r, new_i, plus_r, plus_i = later_part
    out_mr = mul_r * new_r - mul_i * new_i
    out_mi = mul_r * new_i + mul_i * new_r
    out_ar = new_r * add_r - new_i * add_i + plus_r
    out_ai = new_r * add_i + new_i * add_r + plus_i
    return (out_mr, out_mi, out_ar, out_ai)


def across(value, axis, bit):
    size = lax.axis_size(axis)
    return lax.ppermute(value, axis, [(at, at ^ bit) for at in range(size)])


def across_by_core(value, dims):
    seq_size, batch_size = lax.axis_size(N.seq), lax.axis_size(N.batch)
    pairs = []
    for seq in range(seq_size):
        for batch in range(batch_size):
            axis, bit = dims[batch & 1]
            to = (seq ^ bit, batch) if axis == N.seq else (seq, batch ^ bit)
            pairs.append((seq * batch_size + batch, to[0] * batch_size + to[1]))
    return lax.ppermute(value, (N.seq, N.batch), pairs)


def make_plan(seq_size, batch_size, width, kind):
    along_seq = [(N.seq, 1 << bit) for bit in range(seq_size.bit_length() - 1)]
    along_batch = [(N.batch, 1 << bit) for bit in range(1, batch_size.bit_length() - 1)]
    near, next_bit, far = along_seq[:1], along_seq[1:2], along_seq[2:]
    rest = batch_size // 2
    places = {"y": near, "z": next_bit, "w": far, "x": along_batch}
    orders = tuple(sum((places[letter] for letter in order), []) for order in ORDERS[kind])
    blocks = seq_size * rest
    in_place = width % (blocks * SUB) == 0
    return types.SimpleNamespace(
        seq_size=seq_size, batch_size=batch_size, orders=orders, blocks=blocks, in_place=in_place, rest=rest,
        made=blocks if in_place else 2 * SUB, steps=list(zip(*orders)),
    )


class Chunk:
    def __init__(self, pool, plan, name, parts=None, head=0):
        self.pool, self.plan, self.name, self.head, self.done = pool, plan, name, head, 0
        self.parts, self.got = parts or (name,), {}

    def begin(self, part=None):
        part = part or self.name
        names = [key for key in self.pool if key.startswith(N.send_ + part)]
        sent = [self.pool.pop(key) for key in names]
        if not self.plan.in_place:
            sent = [self.arranged(jnp.concatenate(sent, axis=0), 1)]
            self.pool[N.keep_ + part] = self.arranged(self.pool[N.keep_ + part], 0)
        for piece, value in enumerate(sent):
            self.got["got_%s%d" % (part, piece)] = across(value, N.batch, 1)

    def arranged(self, values, side):
        seq, batch = lax.axis_index(N.seq), lax.axis_index(N.batch)
        rest = self.plan.rest
        block = np.arange(self.plan.blocks)
        found = []
        for order in self.plan.orders:
            slots = jnp.zeros(block.shape, jnp.int32)
            for place, (axis, bit) in enumerate(order):
                fixed = block // rest if axis == N.seq else (block % rest) * 2
                mine = seq if axis == N.seq else batch
                flag = (((jnp.asarray(fixed, jnp.int32) ^ mine) & bit) != 0).astype(jnp.int32)
                slots = slots + (flag << (len(order) - 1 - place))
            found.append(slots)
        odd = (batch & 1) == 1
        slots = jnp.where(odd, found[1 - side], found[side])
        body = values[self.head :]
        cut = body.reshape((self.plan.blocks, -1) + body.shape[1:])
        body = jnp.take(cut, jnp.argsort(slots), axis=0).reshape(body.shape)
        return jnp.concatenate([values[: self.head], body], axis=0) if self.head else body

    def apart(self):
        names = [N.keep_ + part for part in self.parts] if self.done == 0 else [N.keep_ + self.name]
        self.pool = {name: self.pool.pop(name) for name in names}

    def fold(self, after=()):
        keep, head = N.keep_ + self.name, self.head
        send, later = N.send_ + self.name, N.later_ + self.name
        names = [N.keep_ + part for part in self.parts] if self.done == 0 else [keep]
        rows, cols = self.pool[names[0]].shape[0], sum(self.pool[name].shape[1] for name in names)
        half = (rows - head) // 2
        if half % SUB == 0:
            if self.done == 0:
                pieces = len(self.got) // len(self.parts)
                kernel = functools.partial(fold_first_kernel, self.parts, head, pieces, (send, later))
            else:
                kernel = functools.partial(fold_kernel, (keep, send, later), head)
            run(
                self.pool, kernel, N.fold_ + self.name,
                new=[(send, (head + half, cols), F32), (later, (head + half, cols), F32)], args=self.got, drop=tuple(names),
                vmem=6 if self.plan.in_place else 24, after=after,
            )
            self.pool[keep] = self.pool.pop(later)
            self.sent = self.pool.pop(send)
        else:
            values = [self.pool.pop(name) + got for name, got in zip(names, self.got.values())]
            value = jnp.concatenate(values, axis=1)
            self.sent = jnp.concatenate([value[:head], value[head + half :]], axis=0)
            self.pool[keep] = value[: head + half]

    def send(self):
        self.got = {N.got: across_by_core(self.sent, self.plan.steps[self.done])}
        self.done += 1

    def step(self, after=()):
        self.fold(after)
        self.send()

    def whole(self, after=()):
        run(
            self.pool, functools.partial(sum_kernel, N.keep_ + self.name), N.sum_ + self.name,
            new=[(N.total, self.pool[N.keep_ + self.name].shape, F32)], args=self.got, drop=(N.keep_ + self.name,), after=after,
        )
        return self.pool.pop(N.total)


def carry(pool, total, between):
    size = lax.axis_size(N.seq)
    hops = size.bit_length() - 1
    sent = pool.pop(total)
    for hop in range(hops):
        first, last = hop == 0, hop == hops - 1
        got = across(sent, N.seq, 1 << hop)
        between(hop)
        shape = sent.shape
        if last:
            new = [(N.start, (shape[0] // 2,) + shape[1:], F32)]
        else:
            new = [(N.before_next, shape, F32), (N.total_next, shape, F32)]
        run(
            pool, functools.partial(carry_kernel, 1 << hop, first, last, False), N.carry,
            new=new, args={N.got: got, N.total: sent}, drop=(N.before,),
        )
        if not last:
            sent = pool.pop(N.total_next)
            pool[N.before] = pool.pop(N.before_next)


def carry_back(pool, name, between):
    size = lax.axis_size(N.seq)
    order = [HOPS[place] for place in range(3) if HOPS[place] < size.bit_length() - 1] + list(range(3, size.bit_length() - 1))
    bits = [1 << hop for hop in order]
    sent = pool.pop(name)
    for hop, bit in enumerate(bits):
        got = across(sent, N.seq, bit)
        between(hop)
        shape = sent.shape
        if hop < len(bits) - 1:
            run(pool, append_kernel, N.append, new=[(N.both, (2 * shape[0],) + shape[1:], F32)], args={N.have: sent, N.got: got})
            sent = pool.pop(N.both)
        else:
            run(
                pool, functools.partial(enter_kernel, bits), N.enter,
                new=[(N.start, (2 * shape[1] // 3,) + shape[2:], F32)], args={N.have: sent, N.got: got},
                scratch={N.both: pltpu.VMEM((2 * shape[0],) + shape[1:], F32)},
            )


def per_device(
    tokens, cotangent, gain_in, w_mix, lower, fbias, phase, gain_out, w_out, gain_ffn, w_gu, w_down
):
    seqs, positions, width = tokens.shape
    chans = lower.shape[0]
    units = w_down.shape[0]
    rows = seqs * positions
    tiles = chans // LANES
    shape = (seqs, positions, chans)
    pad = -(-seqs // SUB) * SUB
    seq_size, batch_size = lax.axis_size(N.seq), lax.axis_size(N.batch)
    tokens = tokens.reshape(rows, width)
    cotangent = cotangent.reshape(rows, width)
    wide_plan, down_plan, scan_plan = (
        make_plan(seq_size, batch_size, width, kind) for kind in (N.wide, N.down, N.scan)
    )
    pool = {}
    raw = {N.raw_in: gain_in, N.raw_lower: lower, N.raw_fbias: fbias, N.raw_phase: phase, N.raw_out: gain_out, N.raw_ffn: gain_ffn}
    run(
        pool, functools.partial(project_kernel, shape), N.project,
        new=[(N.vec, (SUB, width), F32), (N.wmix, w_mix.shape, BF16), (N.low, (rows, width), BF16), (N.pre, (3 * tiles, rows, LANES), F32), (N.decay, (tiles, rows, LANES), F32), (N.adds, (2 * tiles, rows, LANES), F32),
             (N.chunks, (3 * tiles, pad * SUB, LANES), F32), (N.ends, (4 * tiles, pad, LANES), F32)],
        fetch={N.tok: tokens, N.wdown: w_down, N.cot: cotangent}, load=raw, late=(N.wdown, N.cot), raw={N.mix: w_mix},
        scratch={N.own: pltpu.SemaphoreType.DMA((2,))},
    )

    def between(hop):
        if hop == 0:
            run(
                pool, functools.partial(gate_kernel, chans), N.gate, new=[(N.gate, (2 * tiles, rows, LANES), F32)],
                fetch={N.wout: w_out}, drop=(N.wmix,),
            )
        elif hop <= 2:
            run(
                pool, functools.partial(hidden_back_kernel, (hop - 1) * units // 2, "back%d" % (hop - 1)), N.hidden_back,
                new=[("back%d" % (hop - 1), (rows, units // 2), BF16)], drop=(N.wdown,) if hop == 2 else (),
            )

    carry(pool, N.ends, between)
    run(
        pool, functools.partial(mix_kernel, shape), N.mix,
        new=[(N.states, (2 * tiles, rows, LANES), F32), (N.entries, (2 * tiles, pad * SUB, LANES), F32),
             (N.mixed, (rows, width), BF16), (N.after, (rows, width), F32), (N.ffn_low, (rows, width), BF16)],
        fetch={N.wgu: w_gu}, drop=(N.start, N.wout, N.tok, N.decay, N.adds),
    )
    away = (N.after, N.mixed, N.low, N.pre, N.states, N.gate)
    kinds = [(key + N._out, pool[key].shape, pool[key].dtype) for key in away]
    stored = run(
        pool, ffn_kernel, N.ffn, new=[(N.hidden, (rows, units), BF16), (N.grad_gu, (rows, 2 * units), BF16)],
        out=kinds, drop=(N.back0, N.back1) + away[1:],
    )
    stored = dict(zip(away, stored))
    wide, down = Chunk(pool, wide_plan, N.wide), Chunk(pool, down_plan, N.down)
    for side, sending in ((N.send_wide, True), (N.keep_wide, False)):
        run(
            pool, functools.partial(grad_wide_kernel, wide_plan, N.ffn_low, N.grad_gu, side, sending, 512), N.grad_gu,
            new=[(side, (width, units), F32)], drop=() if sending else (N.ffn_low,),
        )
        if sending:
            sent = pool.pop(N.send_wide)
    pool[N.send_wide] = sent
    wide.begin()
    (hidden_out,) = run(
        pool, lambda r: (r.save(r.hidden, r.hidden_out),
                         grad_narrow_kernel(down_plan, N.hidden, N.cot, N.keep_down, N.send_down, r)), N.grad_down,
        new=[(N.keep_down, (units, width // 2), F32), (N.send_down, (units, width // 2), F32)],
        out=[(N.hidden_out, (rows, units), BF16)], drop=(N.hidden,),
        scratch={N.turned: pltpu.VMEM((rows, width), BF16)},
    )
    down.begin()
    wide.step()
    run(
        pool, ffn_back_kernel, N.ffn_back,
        new=[(N.grad_mid, (rows, width), F32), (N.grad_mid_low, (rows, width), BF16), (N.sums_ffn, (SUB, width), F32)],
        fetch={N.states: stored[N.states], N.gate: stored[N.gate], N.wout: w_out, N.pre: stored[N.pre]},
        drop=(N.grad_gu, N.wgu, N.after, N.cot), reuse={N.grad_mid: N.after},
    )
    down.step()
    run(
        pool, functools.partial(mix_back_kernel, shape), N.mix_back,
        new=[(N.grad_gate, (rows, width), BF16), (N.seeds, (2 * tiles, rows, LANES), F32),
             (N.chunks_back, (2 * tiles, pad * SUB, LANES), F32), (N.ends_back, (1, 3 * tiles, pad, LANES), F32),
             (N.sums_out, (SUB, width), F32)],
        fetch={N.low: stored[N.low], N.mixed: stored[N.mixed]}, drop=(N.gate, N.wout), reuse={N.seeds: N.gate},
    )
    half = width // 2
    turned = {N.turned: pltpu.VMEM((rows, width), BF16)}
    third = Chunk(pool, down_plan, N.third, (N.out, N.gates))
    hops = seq_size.bit_length() - 1

    def between(hop):
        if hop == 0:
            run(
                pool, functools.partial(grad_narrow_kernel, down_plan, N.mixed, N.grad_mid_low, N.keep_out, N.send_out),
                N.grad_out, new=[(N.keep_out, (width, half), F32), (N.send_out, (width, half), F32)],
                drop=(N.mixed, N.grad_mid_low), scratch=turned,
            )
            third.begin(N.out)
        elif hop == 1:
            run(
                pool, functools.partial(grad_narrow_kernel, down_plan, N.low, N.grad_gate, N.keep_gates, N.send_gates),
                N.grad_gate, new=[(N.keep_gates, (width, half), F32), (N.send_gates, (width, half), F32)], scratch=turned,
            )
            third.begin(N.gates)
            wide.fold()
        if hop == hops - 1:
            wide.send()

    carry_back(pool, N.ends_back, between)
    span = -(-3 * tiles // 2) * LANES
    run(
        pool, functools.partial(scan_back_kernel, shape), N.scan_back,
        new=[(N.grad_pre, (rows, 3 * chans), BF16), (N.sums_scan, (3 * SUB, chans), F32), (N.turned, (rows, 2 * span), BF16)],
        fetch={N.wmix: w_mix, N.tok: tokens}, drop=(N.start, N.seeds, N.chunks, N.chunks_back, N.pre, N.states, N.entries),
        scratch={N.entries_back: pltpu.VMEM((2 * tiles, pad * SUB, LANES), F32),
                 N.made_pre: pltpu.VMEM((3 * tiles, positions, LANES), F32)},
    )
    third.step()
    (grad_tokens,) = run(
        pool, input_back_kernel, N.input_back, new=[(N.sums_in, (SUB, width), F32)],
        out=[(N.grad_tokens, (rows, width), F32)], drop=(N.grad_pre, N.grad_gate, N.wmix, N.tok, N.grad_mid),
        scratch={N.made: pltpu.VMEM((rows, width), F32)}, vmem=9,
    )
    fourth = Chunk(pool, scan_plan, N.scan, head=SUB)
    run(
        pool, functools.partial(grad_scan_kernel, scan_plan, chans), N.grad_scan,
        new=[(N.keep_scan, (SUB + width, span), F32)]
        + [("send_scan%d" % piece, (width // PIECES + (0 if piece else SUB), span), F32) for piece in range(PIECES)],
        scratch={N.made: pltpu.VMEM((width, span), F32)},
        drop=(N.turned, N.low, N.sums_in, N.sums_out, N.sums_ffn, N.sums_scan),
    )
    fourth.begin()
    block = width // wide_plan.blocks
    pair = Chunk({}, down_plan, N.pair)
    sets = {"w": wide, "p": pair, "s": fourth}
    for chunk in (wide, down, third, fourth):
        chunk.apart()

    def begin_pair(before):
        pair.pool = {**down.pool, **third.pool}
        (shape,) = {pair.pool[N.keep_down].shape}
        half = (shape[0] // 2, 2 * shape[1])
        run(
            pair.pool, functools.partial(fold_pair_kernel, down_plan.blocks // 2), N.fold_pair,
            new=[(N.send_pair, half, F32), (N.later_pair, half, F32)],
            args={N.got_down: down.got[N.got], N.got_third: third.got[N.got]}, drop=(N.keep_down, N.keep_third), after=before,
            vmem=5 if down_plan.in_place else 24,
        )
        pair.pool[N.keep_pair] = pair.pool.pop(N.later_pair)
        pair.sent = pair.pool.pop(N.send_pair)
        pair.done = 1
        pair.send()

    found, trail = {}, {}

    def gather_wide(before=()):
        found[N.first] = wide.whole(before)
        found[N.first_got] = across(found[N.first], N.batch, 2)

    def gather_pair(before=()):
        run(
            pair.pool, pack_kernel, N.pack, new=[(N.packed, (block, units), F32)], args=pair.got, drop=(N.keep_pair,), after=before,
        )
        found[N.second] = pair.pool.pop(N.packed)
        found[N.second_got] = across(found[N.second], N.batch, 2)

    def gather_scan():
        found[N.mine] = fourth.whole()
        found[N.got] = across(found[N.mine], N.batch, 2)

    for letter in ROUNDS:
        chunk = sets.get(letter)
        token = letter + str(chunk.done) if chunk else letter
        before = [trail[name] for name in DEPS.get(token, "").split() if name in trail]
        if letter == "o":
            space = {}
            (output,) = run(
                space, functools.partial(output_kernel, 3), N.output, new=[(N.mark, (SUB, LANES), F32)], out=[(N.output, (rows, width), BF16)],
                load={N.wdown_in: w_down, N.after_in: (stored[N.after], 3), N.hidden_in: (hidden_out, 3)},
                scratch={N.made: pltpu.VMEM((rows, width), BF16)}, vmem=14, after=before,
            )
            trail[token] = space[N.mark]
        elif chunk is pair and chunk.done == 0:
            begin_pair(before)
            trail[token] = pair.pool[N.keep_pair]
        elif chunk.done < len(chunk.plan.steps):
            chunk.step(before)
            trail[token] = chunk.pool[N.keep_ + chunk.name]
        elif letter == "w":
            if N.first not in found:
                gather_wide(before)
                trail[token] = found[N.first]
        elif letter == "s":
            if N.mine not in found:
                gather_scan()
                trail[token] = found[N.mine]
        elif N.second not in found:
            gather_pair(before)
    while any(chunk.done < len(chunk.plan.steps) for chunk in sets.values()):
        for chunk in sets.values():
            if chunk.done < len(chunk.plan.steps):
                chunk.step()
    for key, gather in ((N.first, gather_wide), (N.second, gather_pair), (N.mine, gather_scan)):
        if key not in found:
            gather()
    total, total_got = found.pop(N.mine), found.pop(N.got)
    final_rows = 2 * block
    run(
        pool, functools.partial(stack_kernel, N.batch, 2), N.stack, new=[(N.both, (final_rows, 2 * units), F32)],
        args=found, after=(total,),
    )
    packed = pool.pop(N.both)
    packed_got = across(packed, N.batch, 1)
    grad_down, grad_wide, grad_out, gate_part = finish(
        functools.partial(unpack_kernel, batch_size // 2), N.unpack, {N.mine: packed, N.got: packed_got},
        [(N.grad_down, (units // seq_size, width)), (N.grad_wide, (final_rows, 2 * units)), (N.grad_out, (final_rows, width)),
         (N.gate_part, (final_rows, width))], local=(N.gate_part,),
    )
    run(
        pool, functools.partial(stack_head_kernel, N.batch, 2, SUB), N.stack_scan,
        new=[(N.both, (SUB + final_rows, span), F32)], args={N.mine: total, N.got: total_got}, after=(gate_part,),
    )
    total = pool.pop(N.both)
    total_got = across(total, N.batch, 1)
    grad_mix, *gains = finish(
        finish_kernel, N.finish, {N.mine: total, N.got: total_got, N.gate_part: gate_part},
        [(N.grad_mix, (final_rows, 3 * chans + width)), (N.vec_in, (width,)), (N.vec_out, (width,)), (N.vec_ffn, (width,)),
         (N.vec_lower, (chans,)), (N.vec_fbias, (chans,)), (N.vec_phase, (chans,))],
    )
    return (
        output.reshape(seqs, positions, width),
        grad_tokens.reshape(seqs, positions, width),
        grad_mix,
        grad_out,
        grad_wide,
        grad_down,
        *gains,
    )


def finish(kernel, name, args, outs, local=()):
    names = list(args) + [item[0] for item in outs]

    def body(*refs):
        kernel(types.SimpleNamespace(**dict(zip(names, refs))))

    return pl.pallas_call(
        body,
        out_shape=[
            pltpu.VMEM(shape, F32) if key in local else jax.ShapeDtypeStruct(shape, F32) for key, shape in outs
        ],
        in_specs=[pl.BlockSpec(memory_space=pltpu.VMEM)] * len(args),
        out_specs=[pl.BlockSpec(memory_space=pltpu.VMEM)] * len(outs),
        compiler_params=pltpu.CompilerParams(vmem_limit_bytes=8 * MIB),
        name=name,
    )(*args.values())


def solution(mesh):
    in_specs = (P(N.batch, N.seq, None), P(N.batch, N.seq, None)) + (P(),) * 10
    rows = P(N.seq, None)
    out_specs = (P(N.batch, N.seq, None), P(N.batch, N.seq, None), rows, rows, rows, rows) + (P(),) * 6
    return jax.shard_map(
        per_device, mesh=mesh, in_specs=in_specs, out_specs=out_specs, check_vma=False
    )
```

```python
import functools
import types

import jax
import jax.numpy as jnp
import numpy as np
from jax import lax
from jax.experimental import pallas as pl
from jax.experimental.pallas import tpu as pltpu
from jax.sharding import PartitionSpec as P

epsilon = 1e-06
LANES = 128
SUB = 8
F32 = jnp.float32
BF16 = jnp.bfloat16
MIB = 2**20


class Names:
    def __getattr__(self, name):
        return name


N = Names()
SCALE = 0.2
FOLD = 0.3
HOPS = (2, 1, 0)
ORDERS = {N.wide: (N.xzyw, N.ywzx), N.down: (N.yxzw, N.xywz), N.scan: (N.xywz, N.yxzw)}
ROUNDS = N.wpsposwpswpssp
DEPS = {N.s0: "p0 w2", N.p1: N.s0, "o": N.p1, N.s1: "o", N.w3: N.s1, N.p2: N.s1, N.p3: N.s2, N.w4: N.s2, N.s3: N.w4, N.p4: N.s4}
PIECES = 2
TIME = {
    N.project: 8.0, N.gate: 1.8, N.hidden_back: 1.9, N.mix: 5.9, N.ffn: 7.3, N.grad_gu: 3.2, N.grad_down: 3.6, N.ffn_back: 6.5,
    N.mix_back: 7.0, N.grad_out: 1.6, N.grad_gate: 1.6, N.scan_back: 4.0, N.input_back: 5.6, N.grad_scan: 2.4, N.output: 7.0,
}


def sigmoid(values):
    return 0.5 * jnp.tanh(0.5 * values) + 0.5


def forget_gate(forget, lower):
    decay = jnp.exp(jnp.minimum(-forget, 80.0))
    total = 1.0 + decay
    guess = pl.reciprocal(total, approx=True)
    open_part = guess * (2.0 - total * guess)
    shut_part = decay * open_part
    intake = (1.0 - lower) * shut_part
    return open_part, shut_part, intake, 1.0 - intake


def dot(left, right, left_dim, right_dim):
    return lax.dot_general(
        left, right, (((left_dim,), (right_dim,)), ((), ())), preferred_element_type=F32
    )


def row_block(rows, most):
    best = 16
    for size in range(16, most + 1, 16):
        if rows % size == 0:
            best = size
    return best


def rows_at(step, size):
    return pl.ds(pl.multiple_of(step * size, 16), size)


def tile_of(ref, tile):
    return ref[:, tile * LANES : (tile + 1) * LANES]


def fold_rows(values):
    rows, lanes = values.shape
    return jnp.sum(values.reshape(rows // SUB, SUB, lanes), axis=0)


def loop(count, body):
    lax.fori_loop(0, count, lambda step, _: (body(step), 0)[1], 0)


def project_kernel(shape, r):
    seqs, positions, chans = shape
    tiles = chans // LANES
    steps = positions // SUB
    rows = seqs * positions
    size = row_block(rows, 336)
    width = r.tok.shape[1]
    columns = 3 * chans
    first = pltpu.make_async_copy(r.mix.at[:, :columns], r.wmix.at[:, :columns], r.own.at[0])
    first.start()
    r.vec[...] = jnp.zeros(r.vec.shape, F32)
    for name in (N.raw_in, N.raw_lower, N.raw_fbias, N.raw_phase, N.raw_out, N.raw_ffn):
        r.wait(name)
    for row, name in enumerate((N.raw_in, N.raw_out, N.raw_ffn)):
        r.vec[row : row + 1, :] = getattr(r, name)[...].reshape(1, width)
    phase = r.raw_phase[...].reshape(1, chans)
    r.vec[3:4, :chans] = r.raw_lower[...].reshape(1, chans)
    r.vec[3:4, chans:] = r.raw_fbias[...].reshape(1, chans)
    r.vec[4:5, :chans] = jnp.cos(phase)
    r.vec[4:5, chans:] = jnp.sin(phase)
    r.vec[5:6, :chans] = jnp.cos(phase * steps)
    r.vec[5:6, chans:] = jnp.sin(phase * steps)
    r.vec[6:7, :chans] = jnp.cos(phase * positions)
    r.vec[6:7, chans:] = jnp.sin(phase * positions)
    gain = r.vec[0:1, :]
    fbias = r.vec[3:4, chans:]
    r.wait(N.tok)

    def norm(step):
        at = rows_at(step, size)
        inputs = r.tok[at, :].astype(F32)
        scale = lax.rsqrt(jnp.mean(inputs * inputs, axis=-1, keepdims=True) + epsilon)
        r.low[at, :] = (inputs * scale * gain).astype(BF16)

    loop(rows // size, norm)
    rest = pltpu.make_async_copy(r.mix.at[:, columns:], r.wmix.at[:, columns:], r.own.at[1])
    first.wait()
    rest.start()
    r.start_late()

    def project(step):
        at = rows_at(step, size)
        for part in range(3):
            made = dot(r.low[at, :], r.wmix[:, part * chans : (part + 1) * chans], 1, 0)
            if part == 2:
                made = made + fbias
            for tile in range(tiles):
                r.pre[part * tiles + tile, at, :] = made[:, tile * LANES : (tile + 1) * LANES]

    loop(rows // size, project)

    def scan(seq):
        for tile in range(tiles):
            lanes = slice(tile * LANES, (tile + 1) * LANES)
            low_bound, cos_t, sin_t = r.vec[3:4, lanes], r.vec[4:5, lanes], sine_of(r, lanes)
            product = jnp.ones((SUB, LANES), F32)
            state_r = jnp.zeros((SUB, LANES), F32)
            state_i = jnp.zeros((SUB, LANES), F32)
            for step in range(steps):
                at = pl.ds(seq * positions + step, SUB, stride=steps)
                in_r, in_i = r.pre[tile, at, :], r.pre[tiles + tile, at, :]
                _, _, intake, retain = forget_gate(r.pre[2 * tiles + tile, at, :], low_bound)
                mul_r, mul_i = retain * cos_t, retain * sin_t
                add_r, add_i = intake * (in_r * sigmoid(in_r)), intake * (in_i * sigmoid(in_i))
                state_r, state_i = (
                    mul_r * state_r - mul_i * state_i + add_r,
                    mul_r * state_i + mul_i * state_r + add_i,
                )
                product = product * retain
                r.decay[tile, at, :] = retain
                r.adds[tile, at, :] = add_r
                r.adds[tiles + tile, at, :] = add_i
            at = pl.ds(pl.multiple_of(seq * SUB, SUB), SUB)
            r.chunks[tile, at, :] = product
            r.chunks[tiles + tile, at, :] = state_r
            r.chunks[2 * tiles + tile, at, :] = state_i

    r.chunks[...] = jnp.zeros(r.chunks.shape, F32)
    loop(seqs, scan)
    joined(r, tiles, r.chunks, tiles, r.ends, False)
    rest.wait()


def sine_of(r, lanes):
    chans = r.vec.shape[1] // 2
    return r.vec[4:5, chans + lanes.start : chans + lanes.stop]


def chunk_step(r, tiles, tile, at, added, base, now_r, now_i, backward):
    lanes = slice(tile * LANES, (tile + 1) * LANES)
    chans = r.vec.shape[1] // 2
    product = r.chunks[tile, at, :]
    new_r = product * r.vec[5:6, lanes]
    new_i = product * r.vec[5:6, chans + lanes.start : chans + lanes.stop]
    if backward:
        new_i = -new_i
    return (
        new_r,
        new_i,
        new_r * now_r - new_i * now_i + added[base + tile, at, :],
        new_r * now_i + new_i * now_r + added[base + tiles + tile, at, :],
    )


def joined(r, tiles, added, base, ends, backward):
    pad = ends.shape[1]
    for tile in range(tiles):
        mul_r, mul_i = jnp.ones((pad, LANES), F32), jnp.zeros((pad, LANES), F32)
        add_r, add_i = jnp.zeros((pad, LANES), F32), jnp.zeros((pad, LANES), F32)
        for chunk in reversed(range(SUB)) if backward else range(SUB):
            at = pl.ds(chunk, pad, stride=SUB)
            new_r, new_i, add_r, add_i = chunk_step(r, tiles, tile, at, added, base, add_r, add_i, backward)
            mul_r, mul_i = mul_r * new_r - mul_i * new_i, mul_r * new_i + mul_i * new_r
        ends[tile] = mul_r
        ends[tiles + tile] = mul_i
        ends[2 * tiles + tile] = add_r
        ends[3 * tiles + tile] = add_i


def entered(r, tiles, added, base, start, entries, backward):
    pad = start.shape[1]
    for tile in range(tiles):
        now_r, now_i = start[tile], start[tiles + tile]
        for chunk in reversed(range(SUB)) if backward else range(SUB):
            at = pl.ds(chunk, pad, stride=SUB)
            entries[tile, at, :] = now_r
            entries[tiles + tile, at, :] = now_i
            _, _, now_r, now_i = chunk_step(r, tiles, tile, at, added, base, now_r, now_i, backward)


def carry_kernel(bit, first, last, backward, r):
    tiles = r.total.shape[0] // 4
    later = (lax.axis_index(N.seq) & bit) != 0
    if backward:
        later = jnp.logical_not(later)
    for tile in range(tiles):
        parts = [part * tiles + tile for part in range(4)]
        mine = tuple(r.total[part] for part in parts)
        got = tuple(r.got[part] for part in parts)
        one, zero = jnp.ones(mine[0].shape, F32), jnp.zeros(mine[0].shape, F32)
        before = (one, zero, zero, zero) if first else tuple(r.before[part] for part in parts)
        longer = combine(got, before)
        before = [jnp.where(later, new, old) for new, old in zip(longer, before)]
        if last:
            r.start[tile] = before[2]
            r.start[tiles + tile] = before[3]
        else:
            ahead = [jnp.where(later, b, a) for a, b in zip(mine, got)]
            behind = [jnp.where(later, a, b) for a, b in zip(mine, got)]
            for part, new, total in zip(parts, before, combine(ahead, behind)):
                r.before_next[part] = new
                r.total_next[part] = total


def gate_kernel(chans, r):
    tiles, rows, _ = r.gate.shape
    size = row_block(rows, 336)

    def step_of(step):
        at = rows_at(step, size)
        made = dot(r.low[at, :], r.wmix[:, 3 * chans :], 1, 0)
        for tile in range(tiles):
            r.gate[tile, at, :] = made[:, tile * LANES : (tile + 1) * LANES]

    loop(rows // size, step_of)


def hidden_back_kernel(first, name, r):
    made = getattr(r, name)
    rows, units = made.shape
    size = row_block(rows, 336)

    def step_of(step):
        at = rows_at(step, size)
        for part in range(units // 256):
            cols = slice(part * 256, (part + 1) * 256)
            weight = r.wdown[first + part * 256 : first + (part + 1) * 256, :]
            made[at, cols] = dot(r.cot[at, :], weight, 1, 1).astype(BF16)

    loop(rows // size, step_of)


def mix_kernel(shape, r):
    seqs, positions, chans = shape
    tiles = chans // LANES
    steps = positions // SUB
    rows = seqs * positions
    width = 2 * chans
    size = row_block(rows, 336)
    entered(r, tiles, r.chunks, tiles, r.start, r.entries, False)

    def scan(seq):
        for tile in range(tiles):
            lanes = slice(tile * LANES, (tile + 1) * LANES)
            cos_t, sin_t = r.vec[4:5, lanes], sine_of(r, lanes)
            at = pl.ds(pl.multiple_of(seq * SUB, SUB), SUB)
            state_r, state_i = r.entries[tile, at, :], r.entries[tiles + tile, at, :]
            for step in range(steps):
                at = pl.ds(seq * positions + step, SUB, stride=steps)
                retain = r.decay[tile, at, :]
                add_r, add_i = r.adds[tile, at, :], r.adds[tiles + tile, at, :]
                mul_r, mul_i = retain * cos_t, retain * sin_t
                state_r, state_i = (
                    mul_r * state_r - mul_i * state_i + add_r,
                    mul_r * state_i + mul_i * state_r + add_i,
                )
                r.states[tile, at, :] = state_r
                r.states[tiles + tile, at, :] = state_i

    loop(seqs, scan)

    def mix(step):
        at = rows_at(step, size)
        squares = jnp.zeros((size, LANES), F32)
        for tile in range(2 * tiles):
            part = r.states[tile, at, :]
            squares = squares + part * part
        scale = lax.rsqrt(jnp.sum(squares, axis=-1, keepdims=True) / width + epsilon)
        for tile in range(2 * tiles):
            lanes = slice(tile * LANES, (tile + 1) * LANES)
            gated = r.gate[tile, at, :]
            part = r.states[tile, at, :] * scale * r.vec[1:2, lanes] * (gated * sigmoid(gated))
            r.mixed[at, lanes] = part.astype(BF16)
        total = r.tok[at, :].astype(F32) + dot(r.mixed[at, :], r.wout[...], 1, 0)
        r.after[at, :] = total
        scale = lax.rsqrt(jnp.mean(total * total, axis=-1, keepdims=True) + epsilon)
        r.ffn_low[at, :] = (total * scale * r.vec[2:3, :]).astype(BF16)

    loop(rows // size, mix)


def ffn_kernel(r):
    rows, units = r.hidden.shape
    for name in (N.after, N.mixed, N.low, N.pre, N.states, N.gate):
        r.save(getattr(r, name), getattr(r, name + N._out))
    size = row_block(rows, 336)
    wide = 256

    def step_of(step):
        at = rows_at(step, size)
        block = r.ffn_low[at, :]
        for part in range(units // wide):
            cols = slice(part * wide, (part + 1) * wide)
            later = slice(units + part * wide, units + (part + 1) * wide)
            gate = dot(block, r.wgu[:, cols], 1, 0)
            up = dot(block, r.wgu[:, later], 1, 0)
            side, at_side = (r.back0, part) if 2 * part * wide < units else (r.back1, part - units // wide // 2)
            back = side[at, at_side * wide : (at_side + 1) * wide].astype(F32)
            sigma = sigmoid(gate)
            act = gate * sigma
            r.hidden[at, cols] = (act * up).astype(BF16)
            r.grad_gu[at, cols] = (back * up * (sigma + act * (1.0 - sigma))).astype(BF16)
            r.grad_gu[at, later] = (back * act).astype(BF16)

    loop(rows // size, step_of)


def block_slots(plan):
    if not plan.in_place:
        return list(range(plan.made)), list(range(plan.made))
    seq, batch = lax.axis_index(N.seq), lax.axis_index(N.batch)
    odd = (batch & 1) == 1
    rest = plan.rest

    def place(order, seq_bits, batch_bits):
        total = 0
        for index, (axis, bit) in enumerate(order):
            value = seq_bits if axis == N.seq else batch_bits
            total = total + (((value & bit) // bit) << (len(order) - 1 - index))
        return total

    mine = [place(order, seq, batch) for order in plan.orders]
    keep, send = [], []
    for block in range(plan.blocks):
        fixed = [place(order, block // rest, (block % rest) * 2) for order in plan.orders]
        first, second = fixed[0] ^ mine[0], fixed[1] ^ mine[1]
        keep.append(jnp.where(odd, second, first))
        send.append(jnp.where(odd, first, second))
    return keep, send


def store_blocks(ref, slots, size, cols, values, base=0):
    for block, slot in enumerate(slots):
        at = base + slot * size if isinstance(slot, int) else pl.multiple_of(base + slot * size, SUB)
        ref[pl.ds(at, size), cols] = values[block * size : (block + 1) * size, :]


def grad_narrow_kernel(plan, left, right, keep, send, r):
    left, right, keep, send = (getattr(r, name) for name in (left, right, keep, send))
    mine = lax.axis_index(N.batch) & 1
    kept, sent = block_slots(plan)
    half = right.shape[1] // 2
    r.turned[:, :half] = right[:, pl.ds(pl.multiple_of(mine * half, LANES), half)]
    r.turned[:, half:] = right[:, pl.ds(pl.multiple_of((1 - mine) * half, LANES), half)]
    size = left.shape[1] // plan.made
    tall = min(left.shape[1], 384)
    cols = slice(0, half)
    count = tall // size
    for part in range(left.shape[1] // tall):
        made = dot(left[:, part * tall : (part + 1) * tall], r.turned[...], 0, 0)
        there = slice(part * count, (part + 1) * count)
        store_blocks(keep, kept[there], size, cols, made[:, :half])
        store_blocks(send, sent[there], size, cols, made[:, half:])


def grad_wide_kernel(plan, left, right, made_name, sending, wide, r):
    left, right, out = getattr(r, left), getattr(r, right), getattr(r, made_name)
    mine = lax.axis_index(N.batch) & 1
    owner = 1 - mine if sending else mine
    slots = block_slots(plan)[1 if sending else 0]
    half = right.shape[1] // 2
    size = left.shape[1] // plan.made

    def step_of(part):
        cols = pl.ds(pl.multiple_of(part * wide, LANES), wide)
        source = pl.ds(pl.multiple_of(owner * half + part * wide, LANES), wide)
        store_blocks(out, slots, size, cols, dot(left[...], right[:, source], 0, 0))

    loop(half // wide, step_of)


def fold_kernel(names, head, r):
    keep, got = getattr(r, names[0]), r.got
    send_next, keep_next = getattr(r, names[1]), getattr(r, names[2])
    half = (keep.shape[0] - head) // 2
    send_next[head:, :] = keep[head + half :, :] + got[head + half :, :]
    keep_next[head:, :] = keep[head : head + half, :] + got[head : head + half, :]
    if head:
        both = keep[:head, :] + got[:head, :]
        send_next[:head, :] = both
        keep_next[:head, :] = both


def fold_first_kernel(parts, head, pieces, names, r):
    send_next, keep_next = getattr(r, names[0]), getattr(r, names[1])
    start = 0
    for part in parts:
        keep = getattr(r, N.keep_ + part)
        rows = keep.shape[0] - head
        half = rows // 2
        cols = slice(start, start + keep.shape[1])
        start = cols.stop
        count = max(pieces, 2)
        size = rows // count
        for piece in range(count):
            at = piece * size
            if pieces == 1:
                got = getattr(r, "got_%s0" % part)[head + at : head + at + size, :]
            else:
                first = head if piece == 0 else 0
                got = getattr(r, "got_%s%d" % (part, piece))[first : first + size, :]
            value = keep[head + at : head + at + size, :] + got
            if at < half:
                keep_next[head + at : head + at + size, cols] = value
            else:
                send_next[head + at - half : head + at - half + size, cols] = value
        if head:
            both = keep[:head, :] + getattr(r, "got_%s0" % part)[:head, :]
            send_next[:head, cols] = both
            keep_next[:head, cols] = both


def sum_kernel(name, r):
    r.total[...] = getattr(r, name)[...] + r.got[...]


def fold_pair_kernel(slots, r):
    per, wide = r.keep_down.shape[0] // slots, r.keep_down.shape[1]
    rows = r.keep_third.shape[0] // slots
    for slot in range(slots):
        out = r.later_pair if 2 * slot < slots else r.send_pair
        to = slot % (slots // 2) * per
        at = slice(slot * per, (slot + 1) * per)
        out[to : to + per, :wide] = r.keep_down[at, :] + r.got_down[at, :]
        at = slice(slot * rows, (slot + 1) * rows)
        value = r.keep_third[at, :] + r.got_third[at, :]
        out[to : to + rows, wide:] = value[:, :wide]
        out[to + rows : to + per, wide:] = value[:, wide:]


def pack_kernel(r):
    rows, wide = r.packed.shape[0], r.keep_pair.shape[1] // 2
    total = r.keep_pair[...] + r.got[...]
    r.packed[:, :wide] = total[:rows, wide:]
    r.packed[:, wide : 2 * wide] = total[rows:, wide:]
    r.packed[:, 2 * wide : 3 * wide] = total[:rows, :wide]
    r.packed[:, 3 * wide :] = total[rows:, :wide]


def stack_kernel(axis, bit, r):
    upper = (lax.axis_index(axis) & bit) != 0
    start = 0
    for mine, got in ((r.first, r.first_got), (r.second, r.second_got)):
        rows, wide = mine.shape
        cols = slice(start, start + wide)
        start = cols.stop
        r.both[:rows, cols] = jnp.where(upper, got[...], mine[...])
        r.both[rows:, cols] = jnp.where(upper, mine[...], got[...])


def stack_head_kernel(axis, bit, head, r):
    upper = (lax.axis_index(axis) & bit) != 0
    rows = r.mine.shape[0]
    r.both[:head, :] = r.mine[:head, :]
    r.both[head:rows, :] = jnp.where(upper, r.got[head:, :], r.mine[head:, :])
    r.both[rows:, :] = jnp.where(upper, r.mine[head:, :], r.got[head:, :])


def unpack_kernel(parts, r):
    upper = (lax.axis_index(N.batch) & 1) != 0
    units, width = r.grad_down.shape[0], r.grad_down.shape[1]
    half = width // 2
    rows = r.mine.shape[0]
    wide = r.grad_wide.shape[1] // 2
    size = rows // parts

    def sides(at, cols):
        mine, got = r.mine[at, cols], r.got[at, cols]
        return jnp.where(upper, got, mine), jnp.where(upper, mine, got)

    every = slice(0, rows)
    r.grad_wide[:, :wide], r.grad_wide[:, wide:] = sides(every, slice(0, wide))
    r.grad_out[:, :half], r.grad_out[:, half:] = sides(every, slice(wide, wide + half))
    r.gate_part[:, :half], r.gate_part[:, half:] = sides(every, slice(wide + half, wide + 2 * half))
    base = wide + 2 * half
    per = units // rows
    for part in range(parts):
        for piece in range(per):
            at = slice(part * size, (part + 1) * size)
            to = slice((part * per + piece) * size, (part * per + piece + 1) * size)
            first, second = sides(at, slice(base + piece * half, base + (piece + 1) * half))
            r.grad_down[to, :half] = first
            r.grad_down[to, half:] = second


def finish_kernel(r):
    upper = (lax.axis_index(N.batch) & 1) != 0
    wide = r.mine.shape[1]
    first = jnp.where(upper, r.got[SUB:, :], r.mine[SUB:, :])
    second = jnp.where(upper, r.mine[SUB:, :], r.got[SUB:, :])
    gate = r.gate_part.shape[1]
    scan = r.grad_mix.shape[1] - gate
    r.grad_mix[:, :wide] = first
    r.grad_mix[:, wide:scan] = second[:, 2 * wide - scan :]
    r.grad_mix[:, scan:] = r.gate_part[...]
    index = 0
    for name in (N.vec_in, N.vec_out, N.vec_ffn, N.vec_lower, N.vec_fbias, N.vec_phase):
        ref = getattr(r, name)
        for tile in range(ref.shape[0] // LANES):
            rows, lanes = sum_place(wide, index)
            ref[tile * LANES : (tile + 1) * LANES] = r.mine[rows, lanes].reshape(LANES)
            index += 1


def ffn_back_kernel(r):
    rows, width = r.after.shape
    size = row_block(rows, 336)
    r.sums_ffn[...] = jnp.zeros(r.sums_ffn.shape, F32)

    def ffn_back(step):
        at = rows_at(step, size)
        back = dot(r.grad_gu[at, :], r.wgu[...], 1, 1)
        total = r.after[at, :]
        scale = lax.rsqrt(jnp.mean(total * total, axis=-1, keepdims=True) + epsilon)
        normed = total * scale
        r.sums_ffn[...] += fold_rows(back * normed)
        scaled = back * r.vec[2:3, :]
        shared = jnp.mean(scaled * normed, axis=-1, keepdims=True)
        made = r.cot[at, :].astype(F32) + scale * (scaled - normed * shared)
        r.grad_mid[at, :] = made
        r.grad_mid_low[at, :] = made.astype(BF16)

    loop(rows // size, ffn_back)


def mix_back_kernel(shape, r):
    seqs, positions, chans = shape
    tiles = chans // LANES
    steps = positions // SUB
    rows = seqs * positions
    width = 2 * chans
    small = row_block(rows, 144)
    r.sums_out[...] = jnp.zeros(r.sums_out.shape, F32)

    def mix_back(step):
        at = rows_at(step, small)
        back = dot(r.grad_mid_low[at, :], r.wout[...], 1, 1)
        squares = jnp.zeros((small, LANES), F32)
        for tile in range(2 * tiles):
            part = r.states[tile, at, :]
            squares = squares + part * part
        scale = lax.rsqrt(jnp.sum(squares, axis=-1, keepdims=True) / width + epsilon)
        shared = jnp.zeros((small, LANES), F32)
        for tile in range(2 * tiles):
            lanes = slice(tile * LANES, (tile + 1) * LANES)
            gated = r.gate[tile, at, :]
            sigma = sigmoid(gated)
            act = gated * sigma
            normed = r.states[tile, at, :] * scale
            part = back[:, lanes]
            gain = r.vec[1:2, lanes]
            r.grad_gate[at, lanes] = (part * normed * gain * (sigma + act * (1.0 - sigma))).astype(BF16)
            inner = part * act
            product = inner * normed
            r.sums_out[:, lanes] += fold_rows(product)
            shared = shared + product * gain
            r.seeds[tile, at, :] = inner * gain
        mean = jnp.sum(shared, axis=-1, keepdims=True) / width
        for tile in range(2 * tiles):
            normed = r.states[tile, at, :] * scale
            r.seeds[tile, at, :] = scale * (r.seeds[tile, at, :] - normed * mean)

    loop(rows // small, mix_back)

    def scan(seq):
        for tile in range(tiles):
            lanes = slice(tile * LANES, (tile + 1) * LANES)
            low_bound, cos_t, sin_t = r.vec[3:4, lanes], r.vec[4:5, lanes], sine_of(r, lanes)
            flow_r = jnp.zeros((SUB, LANES), F32)
            flow_i = jnp.zeros((SUB, LANES), F32)
            for step in reversed(range(steps)):
                at = pl.ds(seq * positions + step, SUB, stride=steps)
                _, _, _, retain = forget_gate(r.pre[2 * tiles + tile, at, :], low_bound)
                mul_r, mul_i = retain * cos_t, retain * sin_t
                adj_r = r.seeds[tile, at, :] + flow_r
                adj_i = r.seeds[tiles + tile, at, :] + flow_i
                flow_r = mul_r * adj_r + mul_i * adj_i
                flow_i = mul_r * adj_i - mul_i * adj_r
            at = pl.ds(pl.multiple_of(seq * SUB, SUB), SUB)
            r.chunks_back[tile, at, :] = flow_r
            r.chunks_back[tiles + tile, at, :] = flow_i

    r.chunks_back[...] = jnp.zeros(r.chunks_back.shape, F32)
    loop(seqs, scan)
    pad = r.ends_back.shape[2]
    for tile in range(tiles):
        product = jnp.ones((pad, LANES), F32)
        add_r, add_i = jnp.zeros((pad, LANES), F32), jnp.zeros((pad, LANES), F32)
        for chunk in reversed(range(SUB)):
            at = pl.ds(chunk, pad, stride=SUB)
            product = product * r.chunks[tile, at, :]
            _, _, add_r, add_i = chunk_step(r, tiles, tile, at, r.chunks_back, 0, add_r, add_i, True)
        r.ends_back[0, tile] = product
        r.ends_back[0, tiles + tile] = add_r
        r.ends_back[0, 2 * tiles + tile] = add_i


def append_kernel(r):
    count = r.have.shape[0]
    r.both[:count] = r.have[...]
    r.both[count:] = r.got[...]


def enter_kernel(bits, r):
    mine = lax.axis_index(N.seq)
    count = r.have.shape[0]
    tiles = r.have.shape[1] // 3
    r.both[:count] = r.have[...]
    r.both[count:] = r.got[...]
    for tile in range(tiles):
        lanes = slice(tile * LANES, (tile + 1) * LANES)
        chans = r.vec.shape[1] // 2
        turn_r = r.vec[6:7, lanes]
        turn_i = r.vec[6:7, chans + lanes.start : chans + lanes.stop]
        now_r = jnp.zeros(r.have.shape[2:], F32)
        now_i = jnp.zeros(r.have.shape[2:], F32)
        for other in reversed(range(1, 2 * count)):
            index = 0
            for place, bit in enumerate(bits):
                index = index + ((((mine ^ other) & bit) // bit) << place)
            product = r.both[index, tile]
            mul_r, mul_i = product * turn_r, product * turn_i
            next_r = mul_r * now_r + mul_i * now_i + r.both[index, tiles + tile]
            next_i = mul_r * now_i - mul_i * now_r + r.both[index, 2 * tiles + tile]
            now_r = jnp.where(other > mine, next_r, now_r)
            now_i = jnp.where(other > mine, next_i, now_i)
        r.start[tile] = now_r
        r.start[tiles + tile] = now_i


def scan_back_kernel(shape, r):
    seqs, positions, chans = shape
    tiles = chans // LANES
    steps = positions // SUB
    entered(r, tiles, r.chunks_back, 0, r.start, r.entries_back, True)
    r.sums_scan[...] = jnp.zeros(r.sums_scan.shape, F32)
    mine = lax.axis_index(N.batch) & 1
    half = r.turned.shape[1] // 2
    shift = 3 * chans - half
    keep_at = pl.ds(pl.multiple_of(mine * shift, LANES), half)
    send_at = pl.ds(pl.multiple_of((1 - mine) * shift, LANES), half)

    def scan(seq):
        for tile in range(tiles):
            lanes = slice(tile * LANES, (tile + 1) * LANES)
            low_bound, cos_t, sin_t = r.vec[3:4, lanes], r.vec[4:5, lanes], sine_of(r, lanes)
            chunk_at = pl.ds(pl.multiple_of(seq * SUB, SUB), SUB)
            flow_r, flow_i = r.entries_back[tile, chunk_at, :], r.entries_back[tiles + tile, chunk_at, :]
            sum_lower = jnp.zeros((SUB, LANES), F32)
            sum_fbias = jnp.zeros((SUB, LANES), F32)
            sum_phase = jnp.zeros((SUB, LANES), F32)
            for step in reversed(range(steps)):
                at = pl.ds(seq * positions + step, SUB, stride=steps)
                in_r, in_i = r.pre[tile, at, :], r.pre[tiles + tile, at, :]
                opened, shut, intake, retain = forget_gate(r.pre[2 * tiles + tile, at, :], low_bound)
                sig_r, sig_i = sigmoid(in_r), sigmoid(in_i)
                act_r, act_i = in_r * sig_r, in_i * sig_i
                adj_r = r.seeds[tile, at, :] + flow_r
                adj_i = r.seeds[tiles + tile, at, :] + flow_i
                mul_r, mul_i = retain * cos_t, retain * sin_t
                flow_r = mul_r * adj_r + mul_i * adj_i
                flow_i = mul_r * adj_i - mul_i * adj_r
                if step > 0:
                    before = pl.ds(seq * positions + step - 1, SUB, stride=steps)
                    past_r, past_i = r.states[tile, before, :], r.states[tiles + tile, before, :]
                else:
                    past_r, past_i = r.entries[tile, chunk_at, :], r.entries[tiles + tile, chunk_at, :]
                grad_r = adj_r * past_r + adj_i * past_i
                grad_i = adj_i * past_r - adj_r * past_i
                grad_retain = grad_r * cos_t + grad_i * sin_t - (adj_r * act_r + adj_i * act_i)
                sum_phase = sum_phase + retain * (grad_i * cos_t - grad_r * sin_t)
                sum_lower = sum_lower + grad_retain * shut
                grad_forget = grad_retain * intake * opened
                sum_fbias = sum_fbias + grad_forget
                at = pl.ds(step, SUB, stride=steps)
                r.made_pre[tile, at, :] = adj_r * intake * (sig_r + act_r * (1.0 - sig_r))
                r.made_pre[tiles + tile, at, :] = adj_i * intake * (sig_i + act_i * (1.0 - sig_i))
                r.made_pre[2 * tiles + tile, at, :] = grad_forget
            r.sums_scan[0:SUB, lanes] += sum_lower
            r.sums_scan[SUB : 2 * SUB, lanes] += sum_fbias
            r.sums_scan[2 * SUB : 3 * SUB, lanes] += sum_phase
        seq_rows = rows_at(seq, positions)
        for tile in range(3 * tiles):
            r.grad_pre[seq_rows, tile * LANES : (tile + 1) * LANES] = r.made_pre[tile].astype(BF16)
        r.turned[seq_rows, :half] = r.grad_pre[seq_rows, keep_at]
        r.turned[seq_rows, half:] = r.grad_pre[seq_rows, send_at]

    loop(seqs, scan)


def grad_scan_kernel(plan, chans, r):
    kept, sent = block_slots(plan)
    half = r.turned.shape[1] // 2
    size = r.low.shape[1] // plan.made
    tall = min(r.low.shape[1], 384)
    count = tall // size
    for part in range(r.low.shape[1] // tall):
        made = dot(r.low[:, part * tall : (part + 1) * tall], r.turned[...], 0, 0)
        there = slice(part * count, (part + 1) * count)
        store_blocks(r.keep_scan, kept[there], size, slice(0, half), made[:, :half], SUB)
        store_blocks(r.made, sent[there], size, slice(0, half), made[:, half:])
    zero = jnp.zeros((SUB, half), F32)
    r.keep_scan[0:SUB, :] = zero
    index = 0
    for source in (r.sums_in, r.sums_out, r.sums_ffn):
        for tile in range(source.shape[1] // LANES):
            total = jnp.sum(source[:, tile * LANES : (tile + 1) * LANES], axis=0, keepdims=True)
            put_sum(r.keep_scan, index, total)
            index += 1
    for part in range(3):
        for tile in range(chans // LANES):
            block = r.sums_scan[part * SUB : (part + 1) * SUB, tile * LANES : (tile + 1) * LANES]
            put_sum(r.keep_scan, index, jnp.sum(block, axis=0, keepdims=True))
            index += 1
    rows = r.made.shape[0] // PIECES
    r.send_scan0[0:SUB, :] = r.keep_scan[0:SUB, :]
    r.send_scan0[SUB:, :] = r.made[:rows, :]
    for piece in range(1, PIECES):
        getattr(r, "send_scan%d" % piece)[...] = r.made[piece * rows : (piece + 1) * rows, :]


def sum_place(wide, index):
    row, tile = divmod(index, wide // LANES)
    return slice(row, row + 1), slice(tile * LANES, (tile + 1) * LANES)


def put_sum(ref, index, total):
    rows, lanes = sum_place(ref.shape[1], index)
    ref[rows, lanes] = total


def input_back_kernel(r):
    rows, chans3 = r.grad_pre.shape
    size = row_block(rows, 336)
    r.sums_in[...] = jnp.zeros(r.sums_in.shape, F32)

    for step in range(rows // size):
        at = pl.ds(step * size, size)
        back = dot(r.grad_pre[at, :], r.wmix[:, :chans3], 1, 1)
        back = back + dot(r.grad_gate[at, :], r.wmix[:, chans3:], 1, 1)
        inputs = r.tok[at, :].astype(F32)
        scale = lax.rsqrt(jnp.mean(inputs * inputs, axis=-1, keepdims=True) + epsilon)
        normed = inputs * scale
        r.sums_in[...] += fold_rows(back * normed)
        scaled = back * r.vec[0:1, :]
        shared = jnp.mean(scaled * normed, axis=-1, keepdims=True)
        r.made[at, :] = r.grad_mid[at, :] + scale * (scaled - normed * shared)
        r.save(r.made.at[at, :], r.grad_tokens.at[at, :])


def output_kernel(count, r):
    rows, _ = r.output.shape
    r.mark[...] = jnp.zeros(r.mark.shape, F32)
    size = rows // count
    r.wait(N.wdown_in)
    for step in range(count):
        at = pl.ds(step * size, size)
        for name in (N.after_in, N.hidden_in):
            r.wait(name + str(step))
        made = dot(getattr(r, N.hidden_in + str(step))[...], r.wdown_in[...], 1, 0)
        r.made[at, :] = (getattr(r, N.after_in + str(step))[...] + made).astype(BF16)
        r.save(r.made.at[at, :], r.output.at[at, :])


def run(pool, kernel, name, new=(), args=None, fetch=None, load=None, out=(), drop=(), reuse=None, scratch=None, vmem=5, after=(), late=(), raw=None):
    args, fetch, load, reuse, scratch = args or {}, fetch or {}, load or {}, reuse or {}, scratch or {}
    whole = {key: value for key, value in load.items() if not isinstance(value, tuple)}
    scratch = {**scratch, **{key: pltpu.VMEM(value.shape, value.dtype) for key, value in whole.items()}}
    parts = {key: value for key, value in load.items() if isinstance(value, tuple)}
    load = {key: value for key, value in load.items() if key not in parts}
    incoming = {**fetch, **load}
    for key, (value, count) in parts.items():
        rows = value.shape[0] // count
        for part in range(count):
            scratch[key + str(part)] = pltpu.VMEM((rows,) + value.shape[1:], value.dtype)
    kept = [key for key in pool if key not in drop]
    dropped = [key for key in pool if key in drop]
    new_names = [item[0] for item in new]
    operands = [pool[key] for key in kept + dropped]
    operands += [pltpu.with_memory_space_constraint(value, pltpu.VMEM) for value in args.values()]
    operands += [pltpu.with_memory_space_constraint(value, pltpu.HBM) for value in incoming.values()]
    in_names = kept + dropped + list(args) + ["hbm " + key for key in incoming] + ["after%d" % index for index in range(len(after))]
    operands += list(after)
    in_names += ["hbm " + key for key in parts] + list(raw or {})
    operands += [pltpu.with_memory_space_constraint(value, pltpu.HBM) for value, _ in parts.values()]
    operands += [pltpu.with_memory_space_constraint(value, pltpu.HBM) for value in (raw or {}).values()]
    shapes = [pltpu.VMEM(pool[key].shape, pool[key].dtype) for key in kept]
    shapes += [pltpu.VMEM(shape, kind) for _, shape, kind in new]
    shapes += [pltpu.VMEM(value.shape, value.dtype) for value in fetch.values()]
    shapes += [pltpu.HBM(shape, kind) for _, shape, kind in out]
    out_names = ["out " + key for key in kept] + new_names + list(fetch) + [item[0] for item in out]
    aliases = {index: index for index in range(len(kept))}
    for key, old in reuse.items():
        aliases[in_names.index(old)] = out_names.index(key)
    copies = len(incoming) + sum(count for _, count in parts.values()) + len(out) + 8

    def body(*refs):
        r = types.SimpleNamespace(**dict(zip(in_names + out_names + list(scratch), refs)))
        sems = refs[-1]
        waiting = {}
        for index, key in enumerate(incoming):
            copy = pltpu.make_async_copy(getattr(r, "hbm " + key), getattr(r, key), sems.at[index])
            if key not in late:
                copy.start()
            waiting[key] = copy

        index = len(incoming)
        for part in range(max([count for _, count in parts.values()], default=0)):
            for key, (value, count) in parts.items():
                rows = value.shape[0] // count
                source = getattr(r, "hbm " + key).at[pl.ds(part * rows, rows), :]
                copy = pltpu.make_async_copy(source, getattr(r, key + str(part)), sems.at[index])
                copy.start()
                waiting[key + str(part)] = copy
                index += 1
        taken = index

        def save(source, target):
            index = taken + len([key for key in waiting if key.startswith("save ")])
            copy = pltpu.make_async_copy(source, target, sems.at[index])
            copy.start()
            waiting["save " + str(index)] = copy

        r.wait = lambda key: waiting.pop(key).wait()
        r.save = save
        r.start_late = lambda: [waiting[key].start() for key in late]
        kernel(r)
        for copy in waiting.values():
            copy.wait()

    made = pl.pallas_call(
        body,
        out_shape=shapes,
        in_specs=[pl.BlockSpec(memory_space=pltpu.VMEM)] * (len(kept) + len(dropped) + len(args))
        + [pl.BlockSpec(memory_space=pltpu.HBM)] * len(incoming)
        + [pl.BlockSpec(memory_space=pl.ANY)] * len(after)
        + [pl.BlockSpec(memory_space=pltpu.HBM)] * (len(parts) + len(raw or {})),
        out_specs=[pl.BlockSpec(memory_space=pl.ANY)] * len(kept)
        + [pl.BlockSpec(memory_space=pltpu.VMEM)] * (len(new) + len(fetch))
        + [pl.BlockSpec(memory_space=pltpu.HBM)] * len(out),
        scratch_shapes=list(scratch.values()) + [pltpu.SemaphoreType.DMA((copies,))],
        input_output_aliases=aliases,
        compiler_params=pltpu.CompilerParams(vmem_limit_bytes=vmem * MIB),
        cost_estimate=pl.CostEstimate(flops=int(SCALE * TIME.get(name, FOLD if name.startswith(N.fold) else 0.3) * 1.15e9), bytes_accessed=0, transcendentals=0),
        name=name,
    )(*operands)
    pool.clear()
    count = len(kept) + len(new) + len(fetch)
    pool.update(zip(kept + new_names + list(fetch), made[:count]))
    return made[count:]


def combine(earlier, later_part):
    mul_r, mul_i, add_r, add_i = earlier
    new_r, new_i, plus_r, plus_i = later_part
    out_mr = mul_r * new_r - mul_i * new_i
    out_mi = mul_r * new_i + mul_i * new_r
    out_ar = new_r * add_r - new_i * add_i + plus_r
    out_ai = new_r * add_i + new_i * add_r + plus_i
    return (out_mr, out_mi, out_ar, out_ai)


def across(value, axis, bit):
    size = lax.axis_size(axis)
    return lax.ppermute(value, axis, [(at, at ^ bit) for at in range(size)])


def across_by_core(value, dims):
    seq_size, batch_size = lax.axis_size(N.seq), lax.axis_size(N.batch)
    pairs = []
    for seq in range(seq_size):
        for batch in range(batch_size):
            axis, bit = dims[batch & 1]
            to = (seq ^ bit, batch) if axis == N.seq else (seq, batch ^ bit)
            pairs.append((seq * batch_size + batch, to[0] * batch_size + to[1]))
    return lax.ppermute(value, (N.seq, N.batch), pairs)


def make_plan(seq_size, batch_size, width, kind):
    along_seq = [(N.seq, 1 << bit) for bit in range(seq_size.bit_length() - 1)]
    along_batch = [(N.batch, 1 << bit) for bit in range(1, batch_size.bit_length() - 1)]
    near, next_bit, far = along_seq[:1], along_seq[1:2], along_seq[2:]
    rest = batch_size // 2
    places = {"y": near, "z": next_bit, "w": far, "x": along_batch}
    orders = tuple(sum((places[letter] for letter in order), []) for order in ORDERS[kind])
    blocks = seq_size * rest
    in_place = width % (blocks * SUB) == 0
    return types.SimpleNamespace(
        seq_size=seq_size, batch_size=batch_size, orders=orders, blocks=blocks, in_place=in_place, rest=rest,
        made=blocks if in_place else 2 * SUB, steps=list(zip(*orders)),
    )


class Chunk:
    def __init__(self, pool, plan, name, parts=None, head=0):
        self.pool, self.plan, self.name, self.head, self.done = pool, plan, name, head, 0
        self.parts, self.got = parts or (name,), {}

    def begin(self, part=None):
        part = part or self.name
        names = [key for key in self.pool if key.startswith(N.send_ + part)]
        sent = [self.pool.pop(key) for key in names]
        if not self.plan.in_place:
            sent = [self.arranged(jnp.concatenate(sent, axis=0), 1)]
            self.pool[N.keep_ + part] = self.arranged(self.pool[N.keep_ + part], 0)
        for piece, value in enumerate(sent):
            self.got["got_%s%d" % (part, piece)] = across(value, N.batch, 1)

    def arranged(self, values, side):
        seq, batch = lax.axis_index(N.seq), lax.axis_index(N.batch)
        rest = self.plan.rest
        block = np.arange(self.plan.blocks)
        found = []
        for order in self.plan.orders:
            slots = jnp.zeros(block.shape, jnp.int32)
            for place, (axis, bit) in enumerate(order):
                fixed = block // rest if axis == N.seq else (block % rest) * 2
                mine = seq if axis == N.seq else batch
                flag = (((jnp.asarray(fixed, jnp.int32) ^ mine) & bit) != 0).astype(jnp.int32)
                slots = slots + (flag << (len(order) - 1 - place))
            found.append(slots)
        odd = (batch & 1) == 1
        slots = jnp.where(odd, found[1 - side], found[side])
        body = values[self.head :]
        cut = body.reshape((self.plan.blocks, -1) + body.shape[1:])
        body = jnp.take(cut, jnp.argsort(slots), axis=0).reshape(body.shape)
        return jnp.concatenate([values[: self.head], body], axis=0) if self.head else body

    def apart(self):
        names = [N.keep_ + part for part in self.parts] if self.done == 0 else [N.keep_ + self.name]
        self.pool = {name: self.pool.pop(name) for name in names}

    def fold(self, after=()):
        keep, head = N.keep_ + self.name, self.head
        send, later = N.send_ + self.name, N.later_ + self.name
        names = [N.keep_ + part for part in self.parts] if self.done == 0 else [keep]
        rows, cols = self.pool[names[0]].shape[0], sum(self.pool[name].shape[1] for name in names)
        half = (rows - head) // 2
        if half % SUB == 0:
            if self.done == 0:
                pieces = len(self.got) // len(self.parts)
                kernel = functools.partial(fold_first_kernel, self.parts, head, pieces, (send, later))
            else:
                kernel = functools.partial(fold_kernel, (keep, send, later), head)
            run(
                self.pool, kernel, N.fold_ + self.name,
                new=[(send, (head + half, cols), F32), (later, (head + half, cols), F32)], args=self.got, drop=tuple(names),
                vmem=6 if self.plan.in_place else 24, after=after,
            )
            self.pool[keep] = self.pool.pop(later)
            self.sent = self.pool.pop(send)
        else:
            values = [self.pool.pop(name) + got for name, got in zip(names, self.got.values())]
            value = jnp.concatenate(values, axis=1)
            self.sent = jnp.concatenate([value[:head], value[head + half :]], axis=0)
            self.pool[keep] = value[: head + half]

    def send(self):
        self.got = {N.got: across_by_core(self.sent, self.plan.steps[self.done])}
        self.done += 1

    def step(self, after=()):
        self.fold(after)
        self.send()

    def whole(self, after=()):
        run(
            self.pool, functools.partial(sum_kernel, N.keep_ + self.name), N.sum_ + self.name,
            new=[(N.total, self.pool[N.keep_ + self.name].shape, F32)], args=self.got, drop=(N.keep_ + self.name,), after=after,
        )
        return self.pool.pop(N.total)


def carry(pool, total, between):
    size = lax.axis_size(N.seq)
    hops = size.bit_length() - 1
    sent = pool.pop(total)
    for hop in range(hops):
        first, last = hop == 0, hop == hops - 1
        got = across(sent, N.seq, 1 << hop)
        between(hop)
        shape = sent.shape
        if last:
            new = [(N.start, (shape[0] // 2,) + shape[1:], F32)]
        else:
            new = [(N.before_next, shape, F32), (N.total_next, shape, F32)]
        run(
            pool, functools.partial(carry_kernel, 1 << hop, first, last, False), N.carry,
            new=new, args={N.got: got, N.total: sent}, drop=(N.before,),
        )
        if not last:
            sent = pool.pop(N.total_next)
            pool[N.before] = pool.pop(N.before_next)


def carry_back(pool, name, between):
    size = lax.axis_size(N.seq)
    order = [HOPS[place] for place in range(3) if HOPS[place] < size.bit_length() - 1] + list(range(3, size.bit_length() - 1))
    bits = [1 << hop for hop in order]
    sent = pool.pop(name)
    for hop, bit in enumerate(bits):
        got = across(sent, N.seq, bit)
        between(hop)
        shape = sent.shape
        if hop < len(bits) - 1:
            run(pool, append_kernel, N.append, new=[(N.both, (2 * shape[0],) + shape[1:], F32)], args={N.have: sent, N.got: got})
            sent = pool.pop(N.both)
        else:
            run(
                pool, functools.partial(enter_kernel, bits), N.enter,
                new=[(N.start, (2 * shape[1] // 3,) + shape[2:], F32)], args={N.have: sent, N.got: got},
                scratch={N.both: pltpu.VMEM((2 * shape[0],) + shape[1:], F32)},
            )


def per_device(
    tokens, cotangent, gain_in, w_mix, lower, fbias, phase, gain_out, w_out, gain_ffn, w_gu, w_down
):
    seqs, positions, width = tokens.shape
    chans = lower.shape[0]
    units = w_down.shape[0]
    rows = seqs * positions
    tiles = chans // LANES
    shape = (seqs, positions, chans)
    pad = -(-seqs // SUB) * SUB
    seq_size, batch_size = lax.axis_size(N.seq), lax.axis_size(N.batch)
    tokens = tokens.reshape(rows, width)
    cotangent = cotangent.reshape(rows, width)
    wide_plan, down_plan, scan_plan = (
        make_plan(seq_size, batch_size, width, kind) for kind in (N.wide, N.down, N.scan)
    )
    pool = {}
    raw = {N.raw_in: gain_in, N.raw_lower: lower, N.raw_fbias: fbias, N.raw_phase: phase, N.raw_out: gain_out, N.raw_ffn: gain_ffn}
    run(
        pool, functools.partial(project_kernel, shape), N.project,
        new=[(N.vec, (SUB, width), F32), (N.wmix, w_mix.shape, BF16), (N.low, (rows, width), BF16), (N.pre, (3 * tiles, rows, LANES), F32), (N.decay, (tiles, rows, LANES), F32), (N.adds, (2 * tiles, rows, LANES), F32),
             (N.chunks, (3 * tiles, pad * SUB, LANES), F32), (N.ends, (4 * tiles, pad, LANES), F32)],
        fetch={N.tok: tokens, N.wdown: w_down, N.cot: cotangent}, load=raw, late=(N.wdown, N.cot), raw={N.mix: w_mix},
        scratch={N.own: pltpu.SemaphoreType.DMA((2,))},
    )

    def between(hop):
        if hop == 0:
            run(
                pool, functools.partial(gate_kernel, chans), N.gate, new=[(N.gate, (2 * tiles, rows, LANES), F32)],
                fetch={N.wout: w_out}, drop=(N.wmix,),
            )
        elif hop <= 2:
            run(
                pool, functools.partial(hidden_back_kernel, (hop - 1) * units // 2, "back%d" % (hop - 1)), N.hidden_back,
                new=[("back%d" % (hop - 1), (rows, units // 2), BF16)], drop=(N.wdown,) if hop == 2 else (),
            )

    carry(pool, N.ends, between)
    run(
        pool, functools.partial(mix_kernel, shape), N.mix,
        new=[(N.states, (2 * tiles, rows, LANES), F32), (N.entries, (2 * tiles, pad * SUB, LANES), F32),
             (N.mixed, (rows, width), BF16), (N.after, (rows, width), F32), (N.ffn_low, (rows, width), BF16)],
        fetch={N.wgu: w_gu}, drop=(N.start, N.wout, N.tok, N.decay, N.adds),
    )
    away = (N.after, N.mixed, N.low, N.pre, N.states, N.gate)
    kinds = [(key + N._out, pool[key].shape, pool[key].dtype) for key in away]
    stored = run(
        pool, ffn_kernel, N.ffn, new=[(N.hidden, (rows, units), BF16), (N.grad_gu, (rows, 2 * units), BF16)],
        out=kinds, drop=(N.back0, N.back1) + away[1:],
    )
    stored = dict(zip(away, stored))
    wide, down = Chunk(pool, wide_plan, N.wide), Chunk(pool, down_plan, N.down)
    for side, sending in ((N.send_wide, True), (N.keep_wide, False)):
        run(
            pool, functools.partial(grad_wide_kernel, wide_plan, N.ffn_low, N.grad_gu, side, sending, 512), N.grad_gu,
            new=[(side, (width, units), F32)], drop=() if sending else (N.ffn_low,),
        )
        if sending:
            sent = pool.pop(N.send_wide)
    pool[N.send_wide] = sent
    wide.begin()
    (hidden_out,) = run(
        pool, lambda r: (r.save(r.hidden, r.hidden_out),
                         grad_narrow_kernel(down_plan, N.hidden, N.cot, N.keep_down, N.send_down, r)), N.grad_down,
        new=[(N.send_down, (units, width // 2), F32), (N.keep_down, (units, width // 2), F32)],
        out=[(N.hidden_out, (rows, units), BF16)], drop=(N.hidden,),
        scratch={N.turned: pltpu.VMEM((rows, width), BF16)},
    )
    down.begin()
    wide.step()
    run(
        pool, ffn_back_kernel, N.ffn_back,
        new=[(N.grad_mid, (rows, width), F32), (N.grad_mid_low, (rows, width), BF16), (N.sums_ffn, (SUB, width), F32)],
        fetch={N.states: stored[N.states], N.gate: stored[N.gate], N.wout: w_out, N.pre: stored[N.pre]},
        drop=(N.grad_gu, N.wgu, N.after, N.cot), reuse={N.grad_mid: N.after},
    )
    down.step()
    run(
        pool, functools.partial(mix_back_kernel, shape), N.mix_back,
        new=[(N.grad_gate, (rows, width), BF16), (N.seeds, (2 * tiles, rows, LANES), F32),
             (N.chunks_back, (2 * tiles, pad * SUB, LANES), F32), (N.ends_back, (1, 3 * tiles, pad, LANES), F32),
             (N.sums_out, (SUB, width), F32)],
        fetch={N.low: stored[N.low], N.mixed: stored[N.mixed]}, drop=(N.gate, N.wout), reuse={N.seeds: N.gate},
    )
    half = width // 2
    turned = {N.turned: pltpu.VMEM((rows, width), BF16)}
    third = Chunk(pool, down_plan, N.third, (N.out, N.gates))
    hops = seq_size.bit_length() - 1

    def between(hop):
        if hop == 0:
            run(
                pool, functools.partial(grad_narrow_kernel, down_plan, N.mixed, N.grad_mid_low, N.keep_out, N.send_out),
                N.grad_out, new=[(N.keep_out, (width, half), F32), (N.send_out, (width, half), F32)],
                drop=(N.mixed, N.grad_mid_low), scratch=turned,
            )
            third.begin(N.out)
        elif hop == 1:
            run(
                pool, functools.partial(grad_narrow_kernel, down_plan, N.low, N.grad_gate, N.keep_gates, N.send_gates),
                N.grad_gate, new=[(N.keep_gates, (width, half), F32), (N.send_gates, (width, half), F32)], scratch=turned,
            )
            third.begin(N.gates)
            wide.fold()
        if hop == hops - 1:
            wide.send()

    carry_back(pool, N.ends_back, between)
    span = -(-3 * tiles // 2) * LANES
    run(
        pool, functools.partial(scan_back_kernel, shape), N.scan_back,
        new=[(N.grad_pre, (rows, 3 * chans), BF16), (N.sums_scan, (3 * SUB, chans), F32), (N.turned, (rows, 2 * span), BF16)],
        fetch={N.wmix: w_mix, N.tok: tokens}, drop=(N.start, N.seeds, N.chunks, N.chunks_back, N.pre, N.states, N.entries),
        scratch={N.entries_back: pltpu.VMEM((2 * tiles, pad * SUB, LANES), F32),
                 N.made_pre: pltpu.VMEM((3 * tiles, positions, LANES), F32)},
    )
    third.step()
    (grad_tokens,) = run(
        pool, input_back_kernel, N.input_back, new=[(N.sums_in, (SUB, width), F32)],
        out=[(N.grad_tokens, (rows, width), F32)], drop=(N.grad_pre, N.grad_gate, N.wmix, N.tok, N.grad_mid),
        scratch={N.made: pltpu.VMEM((rows, width), F32)}, vmem=9,
    )
    fourth = Chunk(pool, scan_plan, N.scan, head=SUB)
    run(
        pool, functools.partial(grad_scan_kernel, scan_plan, chans), N.grad_scan,
        new=[(N.keep_scan, (SUB + width, span), F32)]
        + [("send_scan%d" % piece, (width // PIECES + (0 if piece else SUB), span), F32) for piece in range(PIECES)],
        scratch={N.made: pltpu.VMEM((width, span), F32)},
        drop=(N.turned, N.low, N.sums_in, N.sums_out, N.sums_ffn, N.sums_scan),
    )
    fourth.begin()
    block = width // wide_plan.blocks
    pair = Chunk({}, down_plan, N.pair)
    sets = {"w": wide, "p": pair, "s": fourth}
    for chunk in (wide, down, third, fourth):
        chunk.apart()

    def begin_pair(before):
        pair.pool = {**down.pool, **third.pool}
        (shape,) = {pair.pool[N.keep_down].shape}
        half = (shape[0] // 2, 2 * shape[1])
        run(
            pair.pool, functools.partial(fold_pair_kernel, down_plan.blocks // 2), N.fold_pair,
            new=[(N.send_pair, half, F32), (N.later_pair, half, F32)],
            args={N.got_down: down.got[N.got], N.got_third: third.got[N.got]}, drop=(N.keep_down, N.keep_third), after=before,
            vmem=5 if down_plan.in_place else 24,
        )
        pair.pool[N.keep_pair] = pair.pool.pop(N.later_pair)
        pair.sent = pair.pool.pop(N.send_pair)
        pair.done = 1
        pair.send()

    found, trail = {}, {}

    def gather_wide(before=()):
        found[N.first] = wide.whole(before)
        found[N.first_got] = across(found[N.first], N.batch, 2)

    def gather_pair(before=()):
        run(
            pair.pool, pack_kernel, N.pack, new=[(N.packed, (block, units), F32)], args=pair.got, drop=(N.keep_pair,), after=before,
        )
        found[N.second] = pair.pool.pop(N.packed)
        found[N.second_got] = across(found[N.second], N.batch, 2)

    def gather_scan():
        found[N.mine] = fourth.whole()
        found[N.got] = across(found[N.mine], N.batch, 2)

    for letter in ROUNDS:
        chunk = sets.get(letter)
        token = letter + str(chunk.done) if chunk else letter
        before = [trail[name] for name in DEPS.get(token, "").split() if name in trail]
        if letter == "o":
            space = {}
            (output,) = run(
                space, functools.partial(output_kernel, 3), N.output, new=[(N.mark, (SUB, LANES), F32)], out=[(N.output, (rows, width), BF16)],
                load={N.wdown_in: w_down, N.after_in: (stored[N.after], 3), N.hidden_in: (hidden_out, 3)},
                scratch={N.made: pltpu.VMEM((rows, width), BF16)}, vmem=14, after=before,
            )
            trail[token] = space[N.mark]
        elif chunk is pair and chunk.done == 0:
            begin_pair(before)
            trail[token] = pair.pool[N.keep_pair]
        elif chunk.done < len(chunk.plan.steps):
            chunk.step(before)
            trail[token] = chunk.pool[N.keep_ + chunk.name]
        elif letter == "w":
            if N.first not in found:
                gather_wide(before)
                trail[token] = found[N.first]
        elif letter == "s":
            if N.mine not in found:
                gather_scan()
                trail[token] = found[N.mine]
        elif N.second not in found:
            gather_pair(before)
    while any(chunk.done < len(chunk.plan.steps) for chunk in sets.values()):
        for chunk in sets.values():
            if chunk.done < len(chunk.plan.steps):
                chunk.step()
    for key, gather in ((N.first, gather_wide), (N.second, gather_pair), (N.mine, gather_scan)):
        if key not in found:
            gather()
    total, total_got = found.pop(N.mine), found.pop(N.got)
    final_rows = 2 * block
    run(
        pool, functools.partial(stack_kernel, N.batch, 2), N.stack, new=[(N.both, (final_rows, 2 * units), F32)],
        args=found, after=(total,),
    )
    packed = pool.pop(N.both)
    packed_got = across(packed, N.batch, 1)
    grad_down, grad_wide, grad_out, gate_part = finish(
        functools.partial(unpack_kernel, batch_size // 2), N.unpack, {N.mine: packed, N.got: packed_got},
        [(N.grad_down, (units // seq_size, width)), (N.grad_wide, (final_rows, 2 * units)), (N.grad_out, (final_rows, width)),
         (N.gate_part, (final_rows, width))], local=(N.gate_part,),
    )
    run(
        pool, functools.partial(stack_head_kernel, N.batch, 2, SUB), N.stack_scan,
        new=[(N.both, (SUB + final_rows, span), F32)], args={N.mine: total, N.got: total_got}, after=(gate_part,),
    )
    total = pool.pop(N.both)
    total_got = across(total, N.batch, 1)
    grad_mix, *gains = finish(
        finish_kernel, N.finish, {N.mine: total, N.got: total_got, N.gate_part: gate_part},
        [(N.grad_mix, (final_rows, 3 * chans + width)), (N.vec_in, (width,)), (N.vec_out, (width,)), (N.vec_ffn, (width,)),
         (N.vec_lower, (chans,)), (N.vec_fbias, (chans,)), (N.vec_phase, (chans,))],
    )
    return (
        output.reshape(seqs, positions, width),
        grad_tokens.reshape(seqs, positions, width),
        grad_mix,
        grad_out,
        grad_wide,
        grad_down,
        *gains,
    )


def finish(kernel, name, args, outs, local=()):
    names = list(args) + [item[0] for item in outs]

    def body(*refs):
        kernel(types.SimpleNamespace(**dict(zip(names, refs))))

    return pl.pallas_call(
        body,
        out_shape=[
            pltpu.VMEM(shape, F32) if key in local else jax.ShapeDtypeStruct(shape, F32) for key, shape in outs
        ],
        in_specs=[pl.BlockSpec(memory_space=pltpu.VMEM)] * len(args),
        out_specs=[pl.BlockSpec(memory_space=pltpu.VMEM)] * len(outs),
        compiler_params=pltpu.CompilerParams(vmem_limit_bytes=8 * MIB),
        name=name,
    )(*args.values())


def solution(mesh):
    in_specs = (P(N.batch, N.seq, None), P(N.batch, N.seq, None)) + (P(),) * 10
    rows = P(N.seq, None)
    out_specs = (P(N.batch, N.seq, None), P(N.batch, N.seq, None), rows, rows, rows, rows) + (P(),) * 6
    return jax.shard_map(
        per_device, mesh=mesh, in_specs=in_specs, out_specs=out_specs, check_vma=False
    )
```

```python
import functools
import types

import jax
import jax.numpy as jnp
import numpy as np
from jax import lax
from jax.experimental import pallas as pl
from jax.experimental.pallas import tpu as pltpu
from jax.sharding import PartitionSpec as P

epsilon = 1e-06
LANES = 128
SUB = 8
F32 = jnp.float32
BF16 = jnp.bfloat16
MIB = 2**20


class Names:
    def __getattr__(self, name):
        return name


N = Names()
SCALE = 0.2
FOLD = 0.3
HOPS = (2, 1, 0)
ORDERS = {N.wide: (N.xzyw, N.ywzx), N.down: (N.yxzw, N.xywz), N.scan: (N.xywz, N.yxzw)}
ROUNDS = N.wpsposwpswpssp
DEPS = {N.s0: "p0 w2", N.p1: N.s0, "o": N.p1, N.s1: "o", N.w3: N.s1, N.p2: N.s1, N.p3: N.s2, N.w4: N.s2, N.s3: N.w4, N.p4: N.s4}
PIECES = 2
TIME = {
    N.project: 8.0, N.gate: 1.8, N.hidden_back: 1.9, N.mix: 5.9, N.ffn: 7.3, N.grad_gu: 3.2, N.grad_down: 3.6, N.ffn_back: 6.5,
    N.mix_back: 7.0, N.grad_out: 1.6, N.grad_gate: 1.6, N.scan_back: 4.0, N.input_back: 5.6, N.grad_scan: 2.4, N.output: 7.0,
}


def sigmoid(values):
    return 0.5 * jnp.tanh(0.5 * values) + 0.5


def forget_gate(forget, lower):
    decay = jnp.exp(jnp.minimum(-forget, 80.0))
    total = 1.0 + decay
    guess = pl.reciprocal(total, approx=True)
    open_part = guess * (2.0 - total * guess)
    shut_part = decay * open_part
    intake = (1.0 - lower) * shut_part
    return open_part, shut_part, intake, 1.0 - intake


def dot(left, right, left_dim, right_dim):
    return lax.dot_general(
        left, right, (((left_dim,), (right_dim,)), ((), ())), preferred_element_type=F32
    )


def row_block(rows, most):
    best = 16
    for size in range(16, most + 1, 16):
        if rows % size == 0:
            best = size
    return best


def rows_at(step, size):
    return pl.ds(pl.multiple_of(step * size, 16), size)


def tile_of(ref, tile):
    return ref[:, tile * LANES : (tile + 1) * LANES]


def fold_rows(values):
    rows, lanes = values.shape
    return jnp.sum(values.reshape(rows // SUB, SUB, lanes), axis=0)


def loop(count, body):
    lax.fori_loop(0, count, lambda step, _: (body(step), 0)[1], 0)


def project_kernel(shape, r):
    seqs, positions, chans = shape
    tiles = chans // LANES
    steps = positions // SUB
    rows = seqs * positions
    size = row_block(rows, 336)
    width = r.tok.shape[1]
    columns = 3 * chans
    first = pltpu.make_async_copy(r.mix.at[:, :columns], r.wmix.at[:, :columns], r.own.at[0])
    first.start()
    r.vec[...] = jnp.zeros(r.vec.shape, F32)
    for name in (N.raw_in, N.raw_lower, N.raw_fbias, N.raw_phase, N.raw_out, N.raw_ffn):
        r.wait(name)
    for row, name in enumerate((N.raw_in, N.raw_out, N.raw_ffn)):
        r.vec[row : row + 1, :] = getattr(r, name)[...].reshape(1, width)
    phase = r.raw_phase[...].reshape(1, chans)
    r.vec[3:4, :chans] = r.raw_lower[...].reshape(1, chans)
    r.vec[3:4, chans:] = r.raw_fbias[...].reshape(1, chans)
    r.vec[4:5, :chans] = jnp.cos(phase)
    r.vec[4:5, chans:] = jnp.sin(phase)
    r.vec[5:6, :chans] = jnp.cos(phase * steps)
    r.vec[5:6, chans:] = jnp.sin(phase * steps)
    r.vec[6:7, :chans] = jnp.cos(phase * positions)
    r.vec[6:7, chans:] = jnp.sin(phase * positions)
    gain = r.vec[0:1, :]
    fbias = r.vec[3:4, chans:]
    r.wait(N.tok)

    def norm(step):
        at = rows_at(step, size)
        inputs = r.tok[at, :].astype(F32)
        scale = lax.rsqrt(jnp.mean(inputs * inputs, axis=-1, keepdims=True) + epsilon)
        r.low[at, :] = (inputs * scale * gain).astype(BF16)

    loop(rows // size, norm)
    rest = pltpu.make_async_copy(r.mix.at[:, columns:], r.wmix.at[:, columns:], r.own.at[1])
    first.wait()
    rest.start()
    r.start_late()

    def project(step):
        at = rows_at(step, size)
        made = dot(r.low[at, :], r.wmix[:, : 3 * chans], 1, 0)
        for part in range(3):
            for tile in range(tiles):
                start = part * chans + tile * LANES
                value = made[:, start : start + LANES]
                if part == 2:
                    value = value + fbias[:, tile * LANES : (tile + 1) * LANES]
                r.pre[part * tiles + tile, at, :] = value

    loop(rows // size, project)

    def scan(seq):
        for tile in range(tiles):
            lanes = slice(tile * LANES, (tile + 1) * LANES)
            low_bound, cos_t, sin_t = r.vec[3:4, lanes], r.vec[4:5, lanes], sine_of(r, lanes)
            product = jnp.ones((SUB, LANES), F32)
            state_r = jnp.zeros((SUB, LANES), F32)
            state_i = jnp.zeros((SUB, LANES), F32)
            for step in range(steps):
                at = pl.ds(seq * positions + step, SUB, stride=steps)
                in_r, in_i = r.pre[tile, at, :], r.pre[tiles + tile, at, :]
                _, _, intake, retain = forget_gate(r.pre[2 * tiles + tile, at, :], low_bound)
                mul_r, mul_i = retain * cos_t, retain * sin_t
                add_r, add_i = intake * (in_r * sigmoid(in_r)), intake * (in_i * sigmoid(in_i))
                state_r, state_i = (
                    mul_r * state_r - mul_i * state_i + add_r,
                    mul_r * state_i + mul_i * state_r + add_i,
                )
                product = product * retain
                r.decay[tile, at, :] = retain
                r.adds[tile, at, :] = add_r
                r.adds[tiles + tile, at, :] = add_i
            at = pl.ds(pl.multiple_of(seq * SUB, SUB), SUB)
            r.chunks[tile, at, :] = product
            r.chunks[tiles + tile, at, :] = state_r
            r.chunks[2 * tiles + tile, at, :] = state_i

    r.chunks[...] = jnp.zeros(r.chunks.shape, F32)
    loop(seqs, scan)
    joined(r, tiles, r.chunks, tiles, r.ends, False)
    rest.wait()


def sine_of(r, lanes):
    chans = r.vec.shape[1] // 2
    return r.vec[4:5, chans + lanes.start : chans + lanes.stop]


def chunk_step(r, tiles, tile, at, added, base, now_r, now_i, backward):
    lanes = slice(tile * LANES, (tile + 1) * LANES)
    chans = r.vec.shape[1] // 2
    product = r.chunks[tile, at, :]
    new_r = product * r.vec[5:6, lanes]
    new_i = product * r.vec[5:6, chans + lanes.start : chans + lanes.stop]
    if backward:
        new_i = -new_i
    return (
        new_r,
        new_i,
        new_r * now_r - new_i * now_i + added[base + tile, at, :],
        new_r * now_i + new_i * now_r + added[base + tiles + tile, at, :],
    )


def joined(r, tiles, added, base, ends, backward):
    pad = ends.shape[1]
    for tile in range(tiles):
        mul_r, mul_i = jnp.ones((pad, LANES), F32), jnp.zeros((pad, LANES), F32)
        add_r, add_i = jnp.zeros((pad, LANES), F32), jnp.zeros((pad, LANES), F32)
        for chunk in reversed(range(SUB)) if backward else range(SUB):
            at = pl.ds(chunk, pad, stride=SUB)
            new_r, new_i, add_r, add_i = chunk_step(r, tiles, tile, at, added, base, add_r, add_i, backward)
            mul_r, mul_i = mul_r * new_r - mul_i * new_i, mul_r * new_i + mul_i * new_r
        ends[tile] = mul_r
        ends[tiles + tile] = mul_i
        ends[2 * tiles + tile] = add_r
        ends[3 * tiles + tile] = add_i


def entered(r, tiles, added, base, start, entries, backward):
    pad = start.shape[1]
    for tile in range(tiles):
        now_r, now_i = start[tile], start[tiles + tile]
        for chunk in reversed(range(SUB)) if backward else range(SUB):
            at = pl.ds(chunk, pad, stride=SUB)
            entries[tile, at, :] = now_r
            entries[tiles + tile, at, :] = now_i
            _, _, now_r, now_i = chunk_step(r, tiles, tile, at, added, base, now_r, now_i, backward)


def carry_kernel(bit, first, last, backward, r):
    tiles = r.total.shape[0] // 4
    later = (lax.axis_index(N.seq) & bit) != 0
    if backward:
        later = jnp.logical_not(later)
    for tile in range(tiles):
        parts = [part * tiles + tile for part in range(4)]
        mine = tuple(r.total[part] for part in parts)
        got = tuple(r.got[part] for part in parts)
        one, zero = jnp.ones(mine[0].shape, F32), jnp.zeros(mine[0].shape, F32)
        before = (one, zero, zero, zero) if first else tuple(r.before[part] for part in parts)
        longer = combine(got, before)
        before = [jnp.where(later, new, old) for new, old in zip(longer, before)]
        if last:
            r.start[tile] = before[2]
            r.start[tiles + tile] = before[3]
        else:
            ahead = [jnp.where(later, b, a) for a, b in zip(mine, got)]
            behind = [jnp.where(later, a, b) for a, b in zip(mine, got)]
            for part, new, total in zip(parts, before, combine(ahead, behind)):
                r.before_next[part] = new
                r.total_next[part] = total


def gate_kernel(chans, r):
    tiles, rows, _ = r.gate.shape
    size = row_block(rows, 336)

    def step_of(step):
        at = rows_at(step, size)
        made = dot(r.low[at, :], r.wmix[:, 3 * chans :], 1, 0)
        for tile in range(tiles):
            r.gate[tile, at, :] = made[:, tile * LANES : (tile + 1) * LANES]

    loop(rows // size, step_of)


def hidden_back_kernel(first, name, r):
    made = getattr(r, name)
    rows, units = made.shape
    size = row_block(rows, 336)

    def step_of(step):
        at = rows_at(step, size)
        for part in range(units // 256):
            cols = slice(part * 256, (part + 1) * 256)
            weight = r.wdown[first + part * 256 : first + (part + 1) * 256, :]
            made[at, cols] = dot(r.cot[at, :], weight, 1, 1).astype(BF16)

    loop(rows // size, step_of)


def mix_kernel(shape, r):
    seqs, positions, chans = shape
    tiles = chans // LANES
    steps = positions // SUB
    rows = seqs * positions
    width = 2 * chans
    size = row_block(rows, 336)
    entered(r, tiles, r.chunks, tiles, r.start, r.entries, False)

    def scan(seq):
        for tile in range(tiles):
            lanes = slice(tile * LANES, (tile + 1) * LANES)
            cos_t, sin_t = r.vec[4:5, lanes], sine_of(r, lanes)
            at = pl.ds(pl.multiple_of(seq * SUB, SUB), SUB)
            state_r, state_i = r.entries[tile, at, :], r.entries[tiles + tile, at, :]
            for step in range(steps):
                at = pl.ds(seq * positions + step, SUB, stride=steps)
                retain = r.decay[tile, at, :]
                add_r, add_i = r.adds[tile, at, :], r.adds[tiles + tile, at, :]
                mul_r, mul_i = retain * cos_t, retain * sin_t
                state_r, state_i = (
                    mul_r * state_r - mul_i * state_i + add_r,
                    mul_r * state_i + mul_i * state_r + add_i,
                )
                r.states[tile, at, :] = state_r
                r.states[tiles + tile, at, :] = state_i

    loop(seqs, scan)

    def mix(step):
        at = rows_at(step, size)
        squares = jnp.zeros((size, LANES), F32)
        for tile in range(2 * tiles):
            part = r.states[tile, at, :]
            squares = squares + part * part
        scale = lax.rsqrt(jnp.sum(squares, axis=-1, keepdims=True) / width + epsilon)
        for tile in range(2 * tiles):
            lanes = slice(tile * LANES, (tile + 1) * LANES)
            gated = r.gate[tile, at, :]
            part = r.states[tile, at, :] * scale * r.vec[1:2, lanes] * (gated * sigmoid(gated))
            r.mixed[at, lanes] = part.astype(BF16)
        total = r.tok[at, :].astype(F32) + dot(r.mixed[at, :], r.wout[...], 1, 0)
        r.after[at, :] = total
        scale = lax.rsqrt(jnp.mean(total * total, axis=-1, keepdims=True) + epsilon)
        r.ffn_low[at, :] = (total * scale * r.vec[2:3, :]).astype(BF16)

    loop(rows // size, mix)


def ffn_kernel(r):
    rows, units = r.hidden.shape
    for name in (N.after, N.mixed, N.low, N.pre, N.states, N.gate):
        r.save(getattr(r, name), getattr(r, name + N._out))
    size = row_block(rows, 336)
    wide = 256

    def step_of(step):
        at = rows_at(step, size)
        block = r.ffn_low[at, :]
        for part in range(units // wide):
            cols = slice(part * wide, (part + 1) * wide)
            later = slice(units + part * wide, units + (part + 1) * wide)
            gate = dot(block, r.wgu[:, cols], 1, 0)
            up = dot(block, r.wgu[:, later], 1, 0)
            side, at_side = (r.back0, part) if 2 * part * wide < units else (r.back1, part - units // wide // 2)
            back = side[at, at_side * wide : (at_side + 1) * wide].astype(F32)
            sigma = sigmoid(gate)
            act = gate * sigma
            r.hidden[at, cols] = (act * up).astype(BF16)
            r.grad_gu[at, cols] = (back * up * (sigma + act * (1.0 - sigma))).astype(BF16)
            r.grad_gu[at, later] = (back * act).astype(BF16)

    loop(rows // size, step_of)


def block_slots(plan):
    if not plan.in_place:
        return list(range(plan.made)), list(range(plan.made))
    seq, batch = lax.axis_index(N.seq), lax.axis_index(N.batch)
    odd = (batch & 1) == 1
    rest = plan.rest

    def place(order, seq_bits, batch_bits):
        total = 0
        for index, (axis, bit) in enumerate(order):
            value = seq_bits if axis == N.seq else batch_bits
            total = total + (((value & bit) // bit) << (len(order) - 1 - index))
        return total

    mine = [place(order, seq, batch) for order in plan.orders]
    keep, send = [], []
    for block in range(plan.blocks):
        fixed = [place(order, block // rest, (block % rest) * 2) for order in plan.orders]
        first, second = fixed[0] ^ mine[0], fixed[1] ^ mine[1]
        keep.append(jnp.where(odd, second, first))
        send.append(jnp.where(odd, first, second))
    return keep, send


def store_blocks(ref, slots, size, cols, values, base=0):
    for block, slot in enumerate(slots):
        at = base + slot * size if isinstance(slot, int) else pl.multiple_of(base + slot * size, SUB)
        ref[pl.ds(at, size), cols] = values[block * size : (block + 1) * size, :]


def grad_narrow_kernel(plan, left, right, keep, send, r):
    left, right, keep, send = (getattr(r, name) for name in (left, right, keep, send))
    mine = lax.axis_index(N.batch) & 1
    kept, sent = block_slots(plan)
    half = right.shape[1] // 2
    r.turned[:, :half] = right[:, pl.ds(pl.multiple_of(mine * half, LANES), half)]
    r.turned[:, half:] = right[:, pl.ds(pl.multiple_of((1 - mine) * half, LANES), half)]
    size = left.shape[1] // plan.made
    tall = min(left.shape[1], 384)
    cols = slice(0, half)
    count = tall // size
    for part in range(left.shape[1] // tall):
        made = dot(left[:, part * tall : (part + 1) * tall], r.turned[...], 0, 0)
        there = slice(part * count, (part + 1) * count)
        store_blocks(keep, kept[there], size, cols, made[:, :half])
        store_blocks(send, sent[there], size, cols, made[:, half:])


def grad_wide_kernel(plan, left, right, made_name, sending, wide, r):
    left, right, out = getattr(r, left), getattr(r, right), getattr(r, made_name)
    mine = lax.axis_index(N.batch) & 1
    owner = 1 - mine if sending else mine
    slots = block_slots(plan)[1 if sending else 0]
    half = right.shape[1] // 2
    size = left.shape[1] // plan.made

    def step_of(part):
        cols = pl.ds(pl.multiple_of(part * wide, LANES), wide)
        source = pl.ds(pl.multiple_of(owner * half + part * wide, LANES), wide)
        store_blocks(out, slots, size, cols, dot(left[...], right[:, source], 0, 0))

    loop(half // wide, step_of)


def fold_kernel(names, head, r):
    keep, got = getattr(r, names[0]), r.got
    send_next, keep_next = getattr(r, names[1]), getattr(r, names[2])
    half = (keep.shape[0] - head) // 2
    send_next[head:, :] = keep[head + half :, :] + got[head + half :, :]
    keep_next[head:, :] = keep[head : head + half, :] + got[head : head + half, :]
    if head:
        both = keep[:head, :] + got[:head, :]
        send_next[:head, :] = both
        keep_next[:head, :] = both


def fold_first_kernel(parts, head, pieces, names, r):
    send_next, keep_next = getattr(r, names[0]), getattr(r, names[1])
    start = 0
    for part in parts:
        keep = getattr(r, N.keep_ + part)
        rows = keep.shape[0] - head
        half = rows // 2
        cols = slice(start, start + keep.shape[1])
        start = cols.stop
        count = max(pieces, 2)
        size = rows // count
        for piece in range(count):
            at = piece * size
            if pieces == 1:
                got = getattr(r, "got_%s0" % part)[head + at : head + at + size, :]
            else:
                first = head if piece == 0 else 0
                got = getattr(r, "got_%s%d" % (part, piece))[first : first + size, :]
            value = keep[head + at : head + at + size, :] + got
            if at < half:
                keep_next[head + at : head + at + size, cols] = value
            else:
                send_next[head + at - half : head + at - half + size, cols] = value
        if head:
            both = keep[:head, :] + getattr(r, "got_%s0" % part)[:head, :]
            send_next[:head, cols] = both
            keep_next[:head, cols] = both


def sum_kernel(name, r):
    r.total[...] = getattr(r, name)[...] + r.got[...]


def fold_pair_kernel(slots, r):
    per, wide = r.keep_down.shape[0] // slots, r.keep_down.shape[1]
    rows = r.keep_third.shape[0] // slots
    for slot in range(slots):
        out = r.later_pair if 2 * slot < slots else r.send_pair
        to = slot % (slots // 2) * per
        at = slice(slot * per, (slot + 1) * per)
        out[to : to + per, :wide] = r.keep_down[at, :] + r.got_down[at, :]
        at = slice(slot * rows, (slot + 1) * rows)
        value = r.keep_third[at, :] + r.got_third[at, :]
        out[to : to + rows, wide:] = value[:, :wide]
        out[to + rows : to + per, wide:] = value[:, wide:]


def pack_kernel(r):
    rows, wide = r.packed.shape[0], r.keep_pair.shape[1] // 2
    total = r.keep_pair[...] + r.got[...]
    r.packed[:, :wide] = total[:rows, wide:]
    r.packed[:, wide : 2 * wide] = total[rows:, wide:]
    r.packed[:, 2 * wide : 3 * wide] = total[:rows, :wide]
    r.packed[:, 3 * wide :] = total[rows:, :wide]


def stack_kernel(axis, bit, r):
    upper = (lax.axis_index(axis) & bit) != 0
    start = 0
    for mine, got in ((r.first, r.first_got), (r.second, r.second_got)):
        rows, wide = mine.shape
        cols = slice(start, start + wide)
        start = cols.stop
        r.both[:rows, cols] = jnp.where(upper, got[...], mine[...])
        r.both[rows:, cols] = jnp.where(upper, mine[...], got[...])


def stack_head_kernel(axis, bit, head, r):
    upper = (lax.axis_index(axis) & bit) != 0
    rows = r.mine.shape[0]
    r.both[:head, :] = r.mine[:head, :]
    r.both[head:rows, :] = jnp.where(upper, r.got[head:, :], r.mine[head:, :])
    r.both[rows:, :] = jnp.where(upper, r.mine[head:, :], r.got[head:, :])


def unpack_kernel(parts, r):
    upper = (lax.axis_index(N.batch) & 1) != 0
    units, width = r.grad_down.shape[0], r.grad_down.shape[1]
    half = width // 2
    rows = r.mine.shape[0]
    wide = r.grad_wide.shape[1] // 2
    size = rows // parts

    def sides(at, cols):
        mine, got = r.mine[at, cols], r.got[at, cols]
        return jnp.where(upper, got, mine), jnp.where(upper, mine, got)

    every = slice(0, rows)
    r.grad_wide[:, :wide], r.grad_wide[:, wide:] = sides(every, slice(0, wide))
    r.grad_out[:, :half], r.grad_out[:, half:] = sides(every, slice(wide, wide + half))
    r.gate_part[:, :half], r.gate_part[:, half:] = sides(every, slice(wide + half, wide + 2 * half))
    base = wide + 2 * half
    per = units // rows
    for part in range(parts):
        for piece in range(per):
            at = slice(part * size, (part + 1) * size)
            to = slice((part * per + piece) * size, (part * per + piece + 1) * size)
            first, second = sides(at, slice(base + piece * half, base + (piece + 1) * half))
            r.grad_down[to, :half] = first
            r.grad_down[to, half:] = second


def finish_kernel(r):
    upper = (lax.axis_index(N.batch) & 1) != 0
    wide = r.mine.shape[1]
    first = jnp.where(upper, r.got[SUB:, :], r.mine[SUB:, :])
    second = jnp.where(upper, r.mine[SUB:, :], r.got[SUB:, :])
    gate = r.gate_part.shape[1]
    scan = r.grad_mix.shape[1] - gate
    r.grad_mix[:, :wide] = first
    r.grad_mix[:, wide:scan] = second[:, 2 * wide - scan :]
    r.grad_mix[:, scan:] = r.gate_part[...]
    index = 0
    for name in (N.vec_in, N.vec_out, N.vec_ffn, N.vec_lower, N.vec_fbias, N.vec_phase):
        ref = getattr(r, name)
        for tile in range(ref.shape[0] // LANES):
            rows, lanes = sum_place(wide, index)
            ref[tile * LANES : (tile + 1) * LANES] = r.mine[rows, lanes].reshape(LANES)
            index += 1


def ffn_back_kernel(r):
    rows, width = r.after.shape
    size = row_block(rows, 336)
    r.sums_ffn[...] = jnp.zeros(r.sums_ffn.shape, F32)

    def ffn_back(step):
        at = rows_at(step, size)
        back = dot(r.grad_gu[at, :], r.wgu[...], 1, 1)
        total = r.after[at, :]
        scale = lax.rsqrt(jnp.mean(total * total, axis=-1, keepdims=True) + epsilon)
        normed = total * scale
        r.sums_ffn[...] += fold_rows(back * normed)
        scaled = back * r.vec[2:3, :]
        shared = jnp.mean(scaled * normed, axis=-1, keepdims=True)
        made = r.cot[at, :].astype(F32) + scale * (scaled - normed * shared)
        r.grad_mid[at, :] = made
        r.grad_mid_low[at, :] = made.astype(BF16)

    loop(rows // size, ffn_back)


def mix_back_kernel(shape, r):
    seqs, positions, chans = shape
    tiles = chans // LANES
    steps = positions // SUB
    rows = seqs * positions
    width = 2 * chans
    small = row_block(rows, 336)
    r.sums_out[...] = jnp.zeros(r.sums_out.shape, F32)

    def mix_back(step):
        at = rows_at(step, small)
        back = dot(r.grad_mid_low[at, :], r.wout[...], 1, 1)
        squares = jnp.zeros((small, LANES), F32)
        for tile in range(2 * tiles):
            part = r.states[tile, at, :]
            squares = squares + part * part
        scale = lax.rsqrt(jnp.sum(squares, axis=-1, keepdims=True) / width + epsilon)
        shared = jnp.zeros((small, LANES), F32)
        for tile in range(2 * tiles):
            lanes = slice(tile * LANES, (tile + 1) * LANES)
            gated = r.gate[tile, at, :]
            sigma = sigmoid(gated)
            act = gated * sigma
            normed = r.states[tile, at, :] * scale
            part = back[:, lanes]
            gain = r.vec[1:2, lanes]
            r.grad_gate[at, lanes] = (part * normed * gain * (sigma + act * (1.0 - sigma))).astype(BF16)
            inner = part * act
            product = inner * normed
            r.sums_out[:, lanes] += fold_rows(product)
            shared = shared + product * gain
            r.seeds[tile, at, :] = inner * gain
        mean = jnp.sum(shared, axis=-1, keepdims=True) / width
        for tile in range(2 * tiles):
            normed = r.states[tile, at, :] * scale
            r.seeds[tile, at, :] = scale * (r.seeds[tile, at, :] - normed * mean)

    loop(rows // small, mix_back)

    def scan(seq):
        for tile in range(tiles):
            lanes = slice(tile * LANES, (tile + 1) * LANES)
            low_bound, cos_t, sin_t = r.vec[3:4, lanes], r.vec[4:5, lanes], sine_of(r, lanes)
            flow_r = jnp.zeros((SUB, LANES), F32)
            flow_i = jnp.zeros((SUB, LANES), F32)
            for step in reversed(range(steps)):
                at = pl.ds(seq * positions + step, SUB, stride=steps)
                _, _, _, retain = forget_gate(r.pre[2 * tiles + tile, at, :], low_bound)
                mul_r, mul_i = retain * cos_t, retain * sin_t
                adj_r = r.seeds[tile, at, :] + flow_r
                adj_i = r.seeds[tiles + tile, at, :] + flow_i
                flow_r = mul_r * adj_r + mul_i * adj_i
                flow_i = mul_r * adj_i - mul_i * adj_r
            at = pl.ds(pl.multiple_of(seq * SUB, SUB), SUB)
            r.chunks_back[tile, at, :] = flow_r
            r.chunks_back[tiles + tile, at, :] = flow_i

    r.chunks_back[...] = jnp.zeros(r.chunks_back.shape, F32)
    loop(seqs, scan)
    pad = r.ends_back.shape[2]
    for tile in range(tiles):
        product = jnp.ones((pad, LANES), F32)
        add_r, add_i = jnp.zeros((pad, LANES), F32), jnp.zeros((pad, LANES), F32)
        for chunk in reversed(range(SUB)):
            at = pl.ds(chunk, pad, stride=SUB)
            product = product * r.chunks[tile, at, :]
            _, _, add_r, add_i = chunk_step(r, tiles, tile, at, r.chunks_back, 0, add_r, add_i, True)
        r.ends_back[0, tile] = product
        r.ends_back[0, tiles + tile] = add_r
        r.ends_back[0, 2 * tiles + tile] = add_i


def append_kernel(r):
    count = r.have.shape[0]
    r.both[:count] = r.have[...]
    r.both[count:] = r.got[...]


def enter_kernel(bits, r):
    mine = lax.axis_index(N.seq)
    count = r.have.shape[0]
    tiles = r.have.shape[1] // 3
    r.both[:count] = r.have[...]
    r.both[count:] = r.got[...]
    for tile in range(tiles):
        lanes = slice(tile * LANES, (tile + 1) * LANES)
        chans = r.vec.shape[1] // 2
        turn_r = r.vec[6:7, lanes]
        turn_i = r.vec[6:7, chans + lanes.start : chans + lanes.stop]
        now_r = jnp.zeros(r.have.shape[2:], F32)
        now_i = jnp.zeros(r.have.shape[2:], F32)
        for other in reversed(range(1, 2 * count)):
            index = 0
            for place, bit in enumerate(bits):
                index = index + ((((mine ^ other) & bit) // bit) << place)
            product = r.both[index, tile]
            mul_r, mul_i = product * turn_r, product * turn_i
            next_r = mul_r * now_r + mul_i * now_i + r.both[index, tiles + tile]
            next_i = mul_r * now_i - mul_i * now_r + r.both[index, 2 * tiles + tile]
            now_r = jnp.where(other > mine, next_r, now_r)
            now_i = jnp.where(other > mine, next_i, now_i)
        r.start[tile] = now_r
        r.start[tiles + tile] = now_i


def scan_back_kernel(shape, r):
    seqs, positions, chans = shape
    tiles = chans // LANES
    steps = positions // SUB
    entered(r, tiles, r.chunks_back, 0, r.start, r.entries_back, True)
    r.sums_scan[...] = jnp.zeros(r.sums_scan.shape, F32)
    mine = lax.axis_index(N.batch) & 1
    half = r.turned.shape[1] // 2
    shift = 3 * chans - half
    keep_at = pl.ds(pl.multiple_of(mine * shift, LANES), half)
    send_at = pl.ds(pl.multiple_of((1 - mine) * shift, LANES), half)

    def scan(seq):
        for tile in range(tiles):
            lanes = slice(tile * LANES, (tile + 1) * LANES)
            low_bound, cos_t, sin_t = r.vec[3:4, lanes], r.vec[4:5, lanes], sine_of(r, lanes)
            chunk_at = pl.ds(pl.multiple_of(seq * SUB, SUB), SUB)
            flow_r, flow_i = r.entries_back[tile, chunk_at, :], r.entries_back[tiles + tile, chunk_at, :]
            sum_lower = jnp.zeros((SUB, LANES), F32)
            sum_fbias = jnp.zeros((SUB, LANES), F32)
            sum_phase = jnp.zeros((SUB, LANES), F32)
            for step in reversed(range(steps)):
                at = pl.ds(seq * positions + step, SUB, stride=steps)
                in_r, in_i = r.pre[tile, at, :], r.pre[tiles + tile, at, :]
                opened, shut, intake, retain = forget_gate(r.pre[2 * tiles + tile, at, :], low_bound)
                sig_r, sig_i = sigmoid(in_r), sigmoid(in_i)
                act_r, act_i = in_r * sig_r, in_i * sig_i
                adj_r = r.seeds[tile, at, :] + flow_r
                adj_i = r.seeds[tiles + tile, at, :] + flow_i
                mul_r, mul_i = retain * cos_t, retain * sin_t
                flow_r = mul_r * adj_r + mul_i * adj_i
                flow_i = mul_r * adj_i - mul_i * adj_r
                if step > 0:
                    before = pl.ds(seq * positions + step - 1, SUB, stride=steps)
                    past_r, past_i = r.states[tile, before, :], r.states[tiles + tile, before, :]
                else:
                    past_r, past_i = r.entries[tile, chunk_at, :], r.entries[tiles + tile, chunk_at, :]
                grad_r = adj_r * past_r + adj_i * past_i
                grad_i = adj_i * past_r - adj_r * past_i
                grad_retain = grad_r * cos_t + grad_i * sin_t - (adj_r * act_r + adj_i * act_i)
                sum_phase = sum_phase + retain * (grad_i * cos_t - grad_r * sin_t)
                sum_lower = sum_lower + grad_retain * shut
                grad_forget = grad_retain * intake * opened
                sum_fbias = sum_fbias + grad_forget
                at = pl.ds(step, SUB, stride=steps)
                r.made_pre[tile, at, :] = adj_r * intake * (sig_r + act_r * (1.0 - sig_r))
                r.made_pre[tiles + tile, at, :] = adj_i * intake * (sig_i + act_i * (1.0 - sig_i))
                r.made_pre[2 * tiles + tile, at, :] = grad_forget
            r.sums_scan[0:SUB, lanes] += sum_lower
            r.sums_scan[SUB : 2 * SUB, lanes] += sum_fbias
            r.sums_scan[2 * SUB : 3 * SUB, lanes] += sum_phase
        seq_rows = rows_at(seq, positions)
        for tile in range(3 * tiles):
            r.grad_pre[seq_rows, tile * LANES : (tile + 1) * LANES] = r.made_pre[tile].astype(BF16)
        r.turned[seq_rows, :half] = r.grad_pre[seq_rows, keep_at]
        r.turned[seq_rows, half:] = r.grad_pre[seq_rows, send_at]

    loop(seqs, scan)


def grad_scan_kernel(plan, chans, r):
    kept, sent = block_slots(plan)
    half = r.turned.shape[1] // 2
    size = r.low.shape[1] // plan.made
    tall = min(r.low.shape[1], 384)
    count = tall // size
    for part in range(r.low.shape[1] // tall):
        made = dot(r.low[:, part * tall : (part + 1) * tall], r.turned[...], 0, 0)
        there = slice(part * count, (part + 1) * count)
        store_blocks(r.keep_scan, kept[there], size, slice(0, half), made[:, :half], SUB)
        store_blocks(r.made, sent[there], size, slice(0, half), made[:, half:])
    zero = jnp.zeros((SUB, half), F32)
    r.keep_scan[0:SUB, :] = zero
    index = 0
    for source in (r.sums_in, r.sums_out, r.sums_ffn):
        for tile in range(source.shape[1] // LANES):
            total = jnp.sum(source[:, tile * LANES : (tile + 1) * LANES], axis=0, keepdims=True)
            put_sum(r.keep_scan, index, total)
            index += 1
    for part in range(3):
        for tile in range(chans // LANES):
            block = r.sums_scan[part * SUB : (part + 1) * SUB, tile * LANES : (tile + 1) * LANES]
            put_sum(r.keep_scan, index, jnp.sum(block, axis=0, keepdims=True))
            index += 1
    rows = r.made.shape[0] // PIECES
    r.send_scan0[0:SUB, :] = r.keep_scan[0:SUB, :]
    r.send_scan0[SUB:, :] = r.made[:rows, :]
    for piece in range(1, PIECES):
        getattr(r, "send_scan%d" % piece)[...] = r.made[piece * rows : (piece + 1) * rows, :]


def sum_place(wide, index):
    row, tile = divmod(index, wide // LANES)
    return slice(row, row + 1), slice(tile * LANES, (tile + 1) * LANES)


def put_sum(ref, index, total):
    rows, lanes = sum_place(ref.shape[1], index)
    ref[rows, lanes] = total


def input_back_kernel(r):
    rows, chans3 = r.grad_pre.shape
    size = row_block(rows, 336)
    r.sums_in[...] = jnp.zeros(r.sums_in.shape, F32)

    for step in range(rows // size):
        at = pl.ds(step * size, size)
        back = dot(r.grad_pre[at, :], r.wmix[:, :chans3], 1, 1)
        back = back + dot(r.grad_gate[at, :], r.wmix[:, chans3:], 1, 1)
        inputs = r.tok[at, :].astype(F32)
        scale = lax.rsqrt(jnp.mean(inputs * inputs, axis=-1, keepdims=True) + epsilon)
        normed = inputs * scale
        r.sums_in[...] += fold_rows(back * normed)
        scaled = back * r.vec[0:1, :]
        shared = jnp.mean(scaled * normed, axis=-1, keepdims=True)
        r.made[at, :] = r.grad_mid[at, :] + scale * (scaled - normed * shared)
        r.save(r.made.at[at, :], r.grad_tokens.at[at, :])


def output_kernel(count, r):
    rows, _ = r.output.shape
    r.mark[...] = jnp.zeros(r.mark.shape, F32)
    size = rows // count
    r.wait(N.wdown_in)
    for step in range(count):
        at = pl.ds(step * size, size)
        for name in (N.after_in, N.hidden_in):
            r.wait(name + str(step))
        made = dot(getattr(r, N.hidden_in + str(step))[...], r.wdown_in[...], 1, 0)
        r.made[at, :] = (getattr(r, N.after_in + str(step))[...] + made).astype(BF16)
        r.save(r.made.at[at, :], r.output.at[at, :])


def run(pool, kernel, name, new=(), args=None, fetch=None, load=None, out=(), drop=(), reuse=None, scratch=None, vmem=5, after=(), late=(), raw=None):
    args, fetch, load, reuse, scratch = args or {}, fetch or {}, load or {}, reuse or {}, scratch or {}
    whole = {key: value for key, value in load.items() if not isinstance(value, tuple)}
    scratch = {**scratch, **{key: pltpu.VMEM(value.shape, value.dtype) for key, value in whole.items()}}
    parts = {key: value for key, value in load.items() if isinstance(value, tuple)}
    load = {key: value for key, value in load.items() if key not in parts}
    incoming = {**fetch, **load}
    for key, (value, count) in parts.items():
        rows = value.shape[0] // count
        for part in range(count):
            scratch[key + str(part)] = pltpu.VMEM((rows,) + value.shape[1:], value.dtype)
    kept = [key for key in pool if key not in drop]
    dropped = [key for key in pool if key in drop]
    new_names = [item[0] for item in new]
    operands = [pool[key] for key in kept + dropped]
    operands += [pltpu.with_memory_space_constraint(value, pltpu.VMEM) for value in args.values()]
    operands += [pltpu.with_memory_space_constraint(value, pltpu.HBM) for value in incoming.values()]
    in_names = kept + dropped + list(args) + ["hbm " + key for key in incoming] + ["after%d" % index for index in range(len(after))]
    operands += list(after)
    in_names += ["hbm " + key for key in parts] + list(raw or {})
    operands += [pltpu.with_memory_space_constraint(value, pltpu.HBM) for value, _ in parts.values()]
    operands += [pltpu.with_memory_space_constraint(value, pltpu.HBM) for value in (raw or {}).values()]
    shapes = [pltpu.VMEM(pool[key].shape, pool[key].dtype) for key in kept]
    shapes += [pltpu.VMEM(shape, kind) for _, shape, kind in new]
    shapes += [pltpu.VMEM(value.shape, value.dtype) for value in fetch.values()]
    shapes += [pltpu.HBM(shape, kind) for _, shape, kind in out]
    out_names = ["out " + key for key in kept] + new_names + list(fetch) + [item[0] for item in out]
    aliases = {index: index for index in range(len(kept))}
    for key, old in reuse.items():
        aliases[in_names.index(old)] = out_names.index(key)
    copies = len(incoming) + sum(count for _, count in parts.values()) + len(out) + 8

    def body(*refs):
        r = types.SimpleNamespace(**dict(zip(in_names + out_names + list(scratch), refs)))
        sems = refs[-1]
        waiting = {}
        for index, key in enumerate(incoming):
            copy = pltpu.make_async_copy(getattr(r, "hbm " + key), getattr(r, key), sems.at[index])
            if key not in late:
                copy.start()
            waiting[key] = copy

        index = len(incoming)
        for part in range(max([count for _, count in parts.values()], default=0)):
            for key, (value, count) in parts.items():
                rows = value.shape[0] // count
                source = getattr(r, "hbm " + key).at[pl.ds(part * rows, rows), :]
                copy = pltpu.make_async_copy(source, getattr(r, key + str(part)), sems.at[index])
                copy.start()
                waiting[key + str(part)] = copy
                index += 1
        taken = index

        def save(source, target):
            index = taken + len([key for key in waiting if key.startswith("save ")])
            copy = pltpu.make_async_copy(source, target, sems.at[index])
            copy.start()
            waiting["save " + str(index)] = copy

        r.wait = lambda key: waiting.pop(key).wait()
        r.save = save
        r.start_late = lambda: [waiting[key].start() for key in late]
        kernel(r)
        for copy in waiting.values():
            copy.wait()

    made = pl.pallas_call(
        body,
        out_shape=shapes,
        in_specs=[pl.BlockSpec(memory_space=pltpu.VMEM)] * (len(kept) + len(dropped) + len(args))
        + [pl.BlockSpec(memory_space=pltpu.HBM)] * len(incoming)
        + [pl.BlockSpec(memory_space=pl.ANY)] * len(after)
        + [pl.BlockSpec(memory_space=pltpu.HBM)] * (len(parts) + len(raw or {})),
        out_specs=[pl.BlockSpec(memory_space=pl.ANY)] * len(kept)
        + [pl.BlockSpec(memory_space=pltpu.VMEM)] * (len(new) + len(fetch))
        + [pl.BlockSpec(memory_space=pltpu.HBM)] * len(out),
        scratch_shapes=list(scratch.values()) + [pltpu.SemaphoreType.DMA((copies,))],
        input_output_aliases=aliases,
        compiler_params=pltpu.CompilerParams(vmem_limit_bytes=vmem * MIB),
        cost_estimate=pl.CostEstimate(flops=int(SCALE * TIME.get(name, FOLD if name.startswith(N.fold) else 0.3) * 1.15e9), bytes_accessed=0, transcendentals=0),
        name=name,
    )(*operands)
    pool.clear()
    count = len(kept) + len(new) + len(fetch)
    pool.update(zip(kept + new_names + list(fetch), made[:count]))
    return made[count:]


def combine(earlier, later_part):
    mul_r, mul_i, add_r, add_i = earlier
    new_r, new_i, plus_r, plus_i = later_part
    out_mr = mul_r * new_r - mul_i * new_i
    out_mi = mul_r * new_i + mul_i * new_r
    out_ar = new_r * add_r - new_i * add_i + plus_r
    out_ai = new_r * add_i + new_i * add_r + plus_i
    return (out_mr, out_mi, out_ar, out_ai)


def across(value, axis, bit):
    size = lax.axis_size(axis)
    return lax.ppermute(value, axis, [(at, at ^ bit) for at in range(size)])


def across_by_core(value, dims):
    seq_size, batch_size = lax.axis_size(N.seq), lax.axis_size(N.batch)
    pairs = []
    for seq in range(seq_size):
        for batch in range(batch_size):
            axis, bit = dims[batch & 1]
            to = (seq ^ bit, batch) if axis == N.seq else (seq, batch ^ bit)
            pairs.append((seq * batch_size + batch, to[0] * batch_size + to[1]))
    return lax.ppermute(value, (N.seq, N.batch), pairs)


def make_plan(seq_size, batch_size, width, kind):
    along_seq = [(N.seq, 1 << bit) for bit in range(seq_size.bit_length() - 1)]
    along_batch = [(N.batch, 1 << bit) for bit in range(1, batch_size.bit_length() - 1)]
    near, next_bit, far = along_seq[:1], along_seq[1:2], along_seq[2:]
    rest = batch_size // 2
    places = {"y": near, "z": next_bit, "w": far, "x": along_batch}
    orders = tuple(sum((places[letter] for letter in order), []) for order in ORDERS[kind])
    blocks = seq_size * rest
    in_place = width % (blocks * SUB) == 0
    return types.SimpleNamespace(
        seq_size=seq_size, batch_size=batch_size, orders=orders, blocks=blocks, in_place=in_place, rest=rest,
        made=blocks if in_place else 2 * SUB, steps=list(zip(*orders)),
    )


class Chunk:
    def __init__(self, pool, plan, name, parts=None, head=0):
        self.pool, self.plan, self.name, self.head, self.done = pool, plan, name, head, 0
        self.parts, self.got = parts or (name,), {}

    def begin(self, part=None):
        part = part or self.name
        names = [key for key in self.pool if key.startswith(N.send_ + part)]
        sent = [self.pool.pop(key) for key in names]
        if not self.plan.in_place:
            sent = [self.arranged(jnp.concatenate(sent, axis=0), 1)]
            self.pool[N.keep_ + part] = self.arranged(self.pool[N.keep_ + part], 0)
        for piece, value in enumerate(sent):
            self.got["got_%s%d" % (part, piece)] = across(value, N.batch, 1)

    def arranged(self, values, side):
        seq, batch = lax.axis_index(N.seq), lax.axis_index(N.batch)
        rest = self.plan.rest
        block = np.arange(self.plan.blocks)
        found = []
        for order in self.plan.orders:
            slots = jnp.zeros(block.shape, jnp.int32)
            for place, (axis, bit) in enumerate(order):
                fixed = block // rest if axis == N.seq else (block % rest) * 2
                mine = seq if axis == N.seq else batch
                flag = (((jnp.asarray(fixed, jnp.int32) ^ mine) & bit) != 0).astype(jnp.int32)
                slots = slots + (flag << (len(order) - 1 - place))
            found.append(slots)
        odd = (batch & 1) == 1
        slots = jnp.where(odd, found[1 - side], found[side])
        body = values[self.head :]
        cut = body.reshape((self.plan.blocks, -1) + body.shape[1:])
        body = jnp.take(cut, jnp.argsort(slots), axis=0).reshape(body.shape)
        return jnp.concatenate([values[: self.head], body], axis=0) if self.head else body

    def apart(self):
        names = [N.keep_ + part for part in self.parts] if self.done == 0 else [N.keep_ + self.name]
        self.pool = {name: self.pool.pop(name) for name in names}

    def fold(self, after=()):
        keep, head = N.keep_ + self.name, self.head
        send, later = N.send_ + self.name, N.later_ + self.name
        names = [N.keep_ + part for part in self.parts] if self.done == 0 else [keep]
        rows, cols = self.pool[names[0]].shape[0], sum(self.pool[name].shape[1] for name in names)
        half = (rows - head) // 2
        if half % SUB == 0:
            if self.done == 0:
                pieces = len(self.got) // len(self.parts)
                kernel = functools.partial(fold_first_kernel, self.parts, head, pieces, (send, later))
            else:
                kernel = functools.partial(fold_kernel, (keep, send, later), head)
            run(
                self.pool, kernel, N.fold_ + self.name,
                new=[(send, (head + half, cols), F32), (later, (head + half, cols), F32)], args=self.got, drop=tuple(names),
                vmem=6 if self.plan.in_place else 24, after=after,
            )
            self.pool[keep] = self.pool.pop(later)
            self.sent = self.pool.pop(send)
        else:
            values = [self.pool.pop(name) + got for name, got in zip(names, self.got.values())]
            value = jnp.concatenate(values, axis=1)
            self.sent = jnp.concatenate([value[:head], value[head + half :]], axis=0)
            self.pool[keep] = value[: head + half]

    def send(self):
        self.got = {N.got: across_by_core(self.sent, self.plan.steps[self.done])}
        self.done += 1

    def step(self, after=()):
        self.fold(after)
        self.send()

    def whole(self, after=()):
        run(
            self.pool, functools.partial(sum_kernel, N.keep_ + self.name), N.sum_ + self.name,
            new=[(N.total, self.pool[N.keep_ + self.name].shape, F32)], args=self.got, drop=(N.keep_ + self.name,), after=after,
        )
        return self.pool.pop(N.total)


def carry(pool, total, between):
    size = lax.axis_size(N.seq)
    hops = size.bit_length() - 1
    sent = pool.pop(total)
    for hop in range(hops):
        first, last = hop == 0, hop == hops - 1
        got = across(sent, N.seq, 1 << hop)
        between(hop)
        shape = sent.shape
        if last:
            new = [(N.start, (shape[0] // 2,) + shape[1:], F32)]
        else:
            new = [(N.before_next, shape, F32), (N.total_next, shape, F32)]
        run(
            pool, functools.partial(carry_kernel, 1 << hop, first, last, False), N.carry,
            new=new, args={N.got: got, N.total: sent}, drop=(N.before,),
        )
        if not last:
            sent = pool.pop(N.total_next)
            pool[N.before] = pool.pop(N.before_next)


def carry_back(pool, name, between):
    size = lax.axis_size(N.seq)
    order = [HOPS[place] for place in range(3) if HOPS[place] < size.bit_length() - 1] + list(range(3, size.bit_length() - 1))
    bits = [1 << hop for hop in order]
    sent = pool.pop(name)
    for hop, bit in enumerate(bits):
        got = across(sent, N.seq, bit)
        between(hop)
        shape = sent.shape
        if hop < len(bits) - 1:
            run(pool, append_kernel, N.append, new=[(N.both, (2 * shape[0],) + shape[1:], F32)], args={N.have: sent, N.got: got})
            sent = pool.pop(N.both)
        else:
            run(
                pool, functools.partial(enter_kernel, bits), N.enter,
                new=[(N.start, (2 * shape[1] // 3,) + shape[2:], F32)], args={N.have: sent, N.got: got},
                scratch={N.both: pltpu.VMEM((2 * shape[0],) + shape[1:], F32)},
            )


def per_device(
    tokens, cotangent, gain_in, w_mix, lower, fbias, phase, gain_out, w_out, gain_ffn, w_gu, w_down
):
    seqs, positions, width = tokens.shape
    chans = lower.shape[0]
    units = w_down.shape[0]
    rows = seqs * positions
    tiles = chans // LANES
    shape = (seqs, positions, chans)
    pad = -(-seqs // SUB) * SUB
    seq_size, batch_size = lax.axis_size(N.seq), lax.axis_size(N.batch)
    tokens = tokens.reshape(rows, width)
    cotangent = cotangent.reshape(rows, width)
    wide_plan, down_plan, scan_plan = (
        make_plan(seq_size, batch_size, width, kind) for kind in (N.wide, N.down, N.scan)
    )
    pool = {}
    raw = {N.raw_in: gain_in, N.raw_lower: lower, N.raw_fbias: fbias, N.raw_phase: phase, N.raw_out: gain_out, N.raw_ffn: gain_ffn}
    run(
        pool, functools.partial(project_kernel, shape), N.project,
        new=[(N.vec, (SUB, width), F32), (N.wmix, w_mix.shape, BF16), (N.low, (rows, width), BF16), (N.pre, (3 * tiles, rows, LANES), F32), (N.decay, (tiles, rows, LANES), F32), (N.adds, (2 * tiles, rows, LANES), F32),
             (N.chunks, (3 * tiles, pad * SUB, LANES), F32), (N.ends, (4 * tiles, pad, LANES), F32)],
        fetch={N.tok: tokens, N.wdown: w_down, N.cot: cotangent}, load=raw, late=(N.wdown, N.cot), raw={N.mix: w_mix},
        scratch={N.own: pltpu.SemaphoreType.DMA((2,))},
    )

    def between(hop):
        if hop == 0:
            run(
                pool, functools.partial(gate_kernel, chans), N.gate, new=[(N.gate, (2 * tiles, rows, LANES), F32)],
                fetch={N.wout: w_out}, drop=(N.wmix,),
            )
        elif hop <= 2:
            run(
                pool, functools.partial(hidden_back_kernel, (hop - 1) * units // 2, "back%d" % (hop - 1)), N.hidden_back,
                new=[("back%d" % (hop - 1), (rows, units // 2), BF16)], drop=(N.wdown,) if hop == 2 else (),
            )

    carry(pool, N.ends, between)
    run(
        pool, functools.partial(mix_kernel, shape), N.mix,
        new=[(N.states, (2 * tiles, rows, LANES), F32), (N.entries, (2 * tiles, pad * SUB, LANES), F32),
             (N.mixed, (rows, width), BF16), (N.after, (rows, width), F32), (N.ffn_low, (rows, width), BF16)],
        fetch={N.wgu: w_gu}, drop=(N.start, N.wout, N.tok, N.decay, N.adds),
    )
    away = (N.after, N.mixed, N.low, N.pre, N.states, N.gate)
    kinds = [(key + N._out, pool[key].shape, pool[key].dtype) for key in away]
    stored = run(
        pool, ffn_kernel, N.ffn, new=[(N.hidden, (rows, units), BF16), (N.grad_gu, (rows, 2 * units), BF16)],
        out=kinds, drop=(N.back0, N.back1) + away[1:],
    )
    stored = dict(zip(away, stored))
    wide, down = Chunk(pool, wide_plan, N.wide), Chunk(pool, down_plan, N.down)
    for side, sending in ((N.send_wide, True), (N.keep_wide, False)):
        run(
            pool, functools.partial(grad_wide_kernel, wide_plan, N.ffn_low, N.grad_gu, side, sending, 512), N.grad_gu,
            new=[(side, (width, units), F32)], drop=() if sending else (N.ffn_low,),
        )
        if sending:
            sent = pool.pop(N.send_wide)
    pool[N.send_wide] = sent
    wide.begin()
    (hidden_out,) = run(
        pool, lambda r: (r.save(r.hidden, r.hidden_out),
                         grad_narrow_kernel(down_plan, N.hidden, N.cot, N.keep_down, N.send_down, r)), N.grad_down,
        new=[(N.send_down, (units, width // 2), F32), (N.keep_down, (units, width // 2), F32)],
        out=[(N.hidden_out, (rows, units), BF16)], drop=(N.hidden,),
        scratch={N.turned: pltpu.VMEM((rows, width), BF16)},
    )
    down.begin()
    wide.step()
    run(
        pool, ffn_back_kernel, N.ffn_back,
        new=[(N.grad_mid, (rows, width), F32), (N.grad_mid_low, (rows, width), BF16), (N.sums_ffn, (SUB, width), F32)],
        fetch={N.states: stored[N.states], N.gate: stored[N.gate], N.wout: w_out, N.pre: stored[N.pre]},
        drop=(N.grad_gu, N.wgu, N.after, N.cot), reuse={N.grad_mid: N.after},
    )
    down.step()
    run(
        pool, functools.partial(mix_back_kernel, shape), N.mix_back,
        new=[(N.grad_gate, (rows, width), BF16), (N.seeds, (2 * tiles, rows, LANES), F32),
             (N.chunks_back, (2 * tiles, pad * SUB, LANES), F32), (N.ends_back, (1, 3 * tiles, pad, LANES), F32),
             (N.sums_out, (SUB, width), F32)],
        fetch={N.low: stored[N.low], N.mixed: stored[N.mixed]}, drop=(N.gate, N.wout), reuse={N.seeds: N.gate},
    )
    half = width // 2
    turned = {N.turned: pltpu.VMEM((rows, width), BF16)}
    third = Chunk(pool, down_plan, N.third, (N.out, N.gates))
    hops = seq_size.bit_length() - 1

    def between(hop):
        if hop == 0:
            run(
                pool, functools.partial(grad_narrow_kernel, down_plan, N.mixed, N.grad_mid_low, N.keep_out, N.send_out),
                N.grad_out, new=[(N.keep_out, (width, half), F32), (N.send_out, (width, half), F32)],
                drop=(N.mixed, N.grad_mid_low), scratch=turned,
            )
            third.begin(N.out)
        elif hop == 1:
            run(
                pool, functools.partial(grad_narrow_kernel, down_plan, N.low, N.grad_gate, N.keep_gates, N.send_gates),
                N.grad_gate, new=[(N.keep_gates, (width, half), F32), (N.send_gates, (width, half), F32)], scratch=turned,
            )
            third.begin(N.gates)
            wide.fold()
        if hop == hops - 1:
            wide.send()

    carry_back(pool, N.ends_back, between)
    span = -(-3 * tiles // 2) * LANES
    run(
        pool, functools.partial(scan_back_kernel, shape), N.scan_back,
        new=[(N.grad_pre, (rows, 3 * chans), BF16), (N.sums_scan, (3 * SUB, chans), F32), (N.turned, (rows, 2 * span), BF16)],
        fetch={N.wmix: w_mix, N.tok: tokens}, drop=(N.start, N.seeds, N.chunks, N.chunks_back, N.pre, N.states, N.entries),
        scratch={N.entries_back: pltpu.VMEM((2 * tiles, pad * SUB, LANES), F32),
                 N.made_pre: pltpu.VMEM((3 * tiles, positions, LANES), F32)},
    )
    third.step()
    (grad_tokens,) = run(
        pool, input_back_kernel, N.input_back, new=[(N.sums_in, (SUB, width), F32)],
        out=[(N.grad_tokens, (rows, width), F32)], drop=(N.grad_pre, N.grad_gate, N.wmix, N.tok, N.grad_mid),
        scratch={N.made: pltpu.VMEM((rows, width), F32)}, vmem=9,
    )
    fourth = Chunk(pool, scan_plan, N.scan, head=SUB)
    run(
        pool, functools.partial(grad_scan_kernel, scan_plan, chans), N.grad_scan,
        new=[(N.keep_scan, (SUB + width, span), F32)]
        + [("send_scan%d" % piece, (width // PIECES + (0 if piece else SUB), span), F32) for piece in range(PIECES)],
        scratch={N.made: pltpu.VMEM((width, span), F32)},
        drop=(N.turned, N.low, N.sums_in, N.sums_out, N.sums_ffn, N.sums_scan),
    )
    fourth.begin()
    block = width // wide_plan.blocks
    pair = Chunk({}, down_plan, N.pair)
    sets = {"w": wide, "p": pair, "s": fourth}
    for chunk in (wide, down, third, fourth):
        chunk.apart()

    def begin_pair(before):
        pair.pool = {**down.pool, **third.pool}
        (shape,) = {pair.pool[N.keep_down].shape}
        half = (shape[0] // 2, 2 * shape[1])
        run(
            pair.pool, functools.partial(fold_pair_kernel, down_plan.blocks // 2), N.fold_pair,
            new=[(N.send_pair, half, F32), (N.later_pair, half, F32)],
            args={N.got_down: down.got[N.got], N.got_third: third.got[N.got]}, drop=(N.keep_down, N.keep_third), after=before,
            vmem=5 if down_plan.in_place else 24,
        )
        pair.pool[N.keep_pair] = pair.pool.pop(N.later_pair)
        pair.sent = pair.pool.pop(N.send_pair)
        pair.done = 1
        pair.send()

    found, trail = {}, {}

    def gather_wide(before=()):
        found[N.first] = wide.whole(before)
        found[N.first_got] = across(found[N.first], N.batch, 2)

    def gather_pair(before=()):
        run(
            pair.pool, pack_kernel, N.pack, new=[(N.packed, (block, units), F32)], args=pair.got, drop=(N.keep_pair,), after=before,
        )
        found[N.second] = pair.pool.pop(N.packed)
        found[N.second_got] = across(found[N.second], N.batch, 2)

    def gather_scan():
        found[N.mine] = fourth.whole()
        found[N.got] = across(found[N.mine], N.batch, 2)

    for letter in ROUNDS:
        chunk = sets.get(letter)
        token = letter + str(chunk.done) if chunk else letter
        before = [trail[name] for name in DEPS.get(token, "").split() if name in trail]
        if letter == "o":
            space = {}
            (output,) = run(
                space, functools.partial(output_kernel, 3), N.output, new=[(N.mark, (SUB, LANES), F32)], out=[(N.output, (rows, width), BF16)],
                load={N.wdown_in: w_down, N.after_in: (stored[N.after], 3), N.hidden_in: (hidden_out, 3)},
                scratch={N.made: pltpu.VMEM((rows, width), BF16)}, vmem=14, after=before,
            )
            trail[token] = space[N.mark]
        elif chunk is pair and chunk.done == 0:
            begin_pair(before)
            trail[token] = pair.pool[N.keep_pair]
        elif chunk.done < len(chunk.plan.steps):
            chunk.step(before)
            trail[token] = chunk.pool[N.keep_ + chunk.name]
        elif letter == "w":
            if N.first not in found:
                gather_wide(before)
                trail[token] = found[N.first]
        elif letter == "s":
            if N.mine not in found:
                gather_scan()
                trail[token] = found[N.mine]
        elif N.second not in found:
            gather_pair(before)
    while any(chunk.done < len(chunk.plan.steps) for chunk in sets.values()):
        for chunk in sets.values():
            if chunk.done < len(chunk.plan.steps):
                chunk.step()
    for key, gather in ((N.first, gather_wide), (N.second, gather_pair), (N.mine, gather_scan)):
        if key not in found:
            gather()
    total, total_got = found.pop(N.mine), found.pop(N.got)
    final_rows = 2 * block
    run(
        pool, functools.partial(stack_kernel, N.batch, 2), N.stack, new=[(N.both, (final_rows, 2 * units), F32)],
        args=found, after=(total,),
    )
    packed = pool.pop(N.both)
    packed_got = across(packed, N.batch, 1)
    grad_down, grad_wide, grad_out, gate_part = finish(
        functools.partial(unpack_kernel, batch_size // 2), N.unpack, {N.mine: packed, N.got: packed_got},
        [(N.grad_down, (units // seq_size, width)), (N.grad_wide, (final_rows, 2 * units)), (N.grad_out, (final_rows, width)),
         (N.gate_part, (final_rows, width))], local=(N.gate_part,),
    )
    run(
        pool, functools.partial(stack_head_kernel, N.batch, 2, SUB), N.stack_scan,
        new=[(N.both, (SUB + final_rows, span), F32)], args={N.mine: total, N.got: total_got}, after=(gate_part,),
    )
    total = pool.pop(N.both)
    total_got = across(total, N.batch, 1)
    grad_mix, *gains = finish(
        finish_kernel, N.finish, {N.mine: total, N.got: total_got, N.gate_part: gate_part},
        [(N.grad_mix, (final_rows, 3 * chans + width)), (N.vec_in, (width,)), (N.vec_out, (width,)), (N.vec_ffn, (width,)),
         (N.vec_lower, (chans,)), (N.vec_fbias, (chans,)), (N.vec_phase, (chans,))],
    )
    return (
        output.reshape(seqs, positions, width),
        grad_tokens.reshape(seqs, positions, width),
        grad_mix,
        grad_out,
        grad_wide,
        grad_down,
        *gains,
    )


def finish(kernel, name, args, outs, local=()):
    names = list(args) + [item[0] for item in outs]

    def body(*refs):
        kernel(types.SimpleNamespace(**dict(zip(names, refs))))

    return pl.pallas_call(
        body,
        out_shape=[
            pltpu.VMEM(shape, F32) if key in local else jax.ShapeDtypeStruct(shape, F32) for key, shape in outs
        ],
        in_specs=[pl.BlockSpec(memory_space=pltpu.VMEM)] * len(args),
        out_specs=[pl.BlockSpec(memory_space=pltpu.VMEM)] * len(outs),
        compiler_params=pltpu.CompilerParams(vmem_limit_bytes=8 * MIB),
        name=name,
    )(*args.values())


def solution(mesh):
    in_specs = (P(N.batch, N.seq, None), P(N.batch, N.seq, None)) + (P(),) * 10
    rows = P(N.seq, None)
    out_specs = (P(N.batch, N.seq, None), P(N.batch, N.seq, None), rows, rows, rows, rows) + (P(),) * 6
    return jax.shard_map(
        per_device, mesh=mesh, in_specs=in_specs, out_specs=out_specs, check_vma=False
    )
```
